32 devices in a mesh: clouds: 8 (over z, y), pts: 4 (over x, core).
Axes of the slice: x: 2, y: 2, z: 4, core: 2. Of those that a mesh axis runs over, the one named last changes fastest.
Arguments:
- features: float32 [32, 1024, 64], P('clouds', 'pts')
- neighbours_one: int32 [32, 20, 1024], P('clouds', None, 'pts'), may hold values from 0 to 1023
- neighbours_two: int32 [32, 20, 1024], P('clouds', None, 'pts'), may hold values from 0 to 1023
- weight_one: float32 [128, 128], replicated, may hold values from -0.5 to 0.5
- gain_one: float32 [128], replicated, may hold values from 0.25 to 1.75
- shift_one: float32 [128], replicated, may hold values from -3 to 3
- weight_two: float32 [256, 256], replicated, may hold values from -0.375 to 0.375
- gain_two: float32 [256], replicated, may hold values from 0.25 to 1.75
- shift_two: float32 [256], replicated, may hold values from -3 to 3
- grad_act: float32 [32, 1024, 256], P('clouds', 'pts'), may hold values from -6 to 6
- grad_max: float32 [32, 256], P('clouds'), may hold values from -48 to 48
- grad_mean: float32 [32, 256], P('clouds'), may hold values from -48 to 48
Outputs:
- activations: float32 [32, 1024, 256], P('clouds', 'pts')
- pool_max: float32 [32, 256], P('clouds')
- pool_mean: float32 [32, 256], P('clouds')
- grad_features: float32 [32, 1024, 64], P('clouds', 'pts')
- grad_weight_one: float32 [128, 128], replicated
- grad_gain_one: float32 [128], replicated
- grad_shift_one: float32 [128], replicated
- grad_weight_two: float32 [256, 256], replicated
- grad_gain_two: float32 [256], replicated
- grad_shift_two: float32 [256], replicated
The draws below stay inside these ranges and needn't reach their ends.
All inputs are finite; a program needn't handle non-finite values.
Results may differ from the reference program's by a relative error of at most 0.0003.
Values sent between devices are 32-bit elements; how exact they have to be, the bound alone decides.
No kernel may reach another device: no remote copies, remote signals or barrier semaphores. Data moves between devices by JAX's collectives and lax.ppermute only.
A program may use at most 256 MiB of HBM per device.

```python
import jax
import jax.numpy as jnp
from jax import lax

C0 = 64
C1 = 128
C2 = 256
K = 20
NPTS = 1024
CLOUDS = 32


def draw_features(key, part):
    key = jax.random.fold_in(key, 7)
    key_base = jax.random.fold_in(key, 0)
    cloud_scale = 0.6 + 1.2 * jnp.arange(CLOUDS, dtype=jnp.float32) / max(CLOUDS - 1, 1)
    values = jax.random.normal(key_base, (CLOUDS, NPTS, C0), jnp.float32)
    return values * cloud_scale[:, None, None]


def touch_ends(result, rng, smallest, largest):
    shape = result.shape
    place = [jax.random.randint(jax.random.fold_in(rng, axis), (), 0, shape[axis]) for axis in range(len(shape))]
    result = result.at[tuple(place)].set(smallest)
    longest = shape.index(max(shape))
    place[longest] = (place[longest] + 1) % shape[longest]
    return result.at[tuple(place)].set(largest)


def levels(stream_key, shape, cuts, smallest, largest):
    gain, own = 1.0, jax.random.fold_in(stream_key, 6)
    for position, parts in cuts:
        draws = jnp.exp(jax.random.uniform(jax.random.fold_in(own, position), (parts,), jnp.float32, smallest / len(cuts), largest / len(cuts)))
        gain = gain * jnp.repeat(draws, shape[position] // parts).reshape([-1 if axis == position else 1 for axis in range(len(shape))])
    return gain


def scatter_about(rng, dims, scale, limit, shards=(), kind=jnp.bfloat16):
    result = scale * jax.random.normal(rng, dims, jnp.float32)
    if shards:
        result = result * levels(rng, dims, shards, -0.22, 0.18)
    return jnp.clip(result, -limit, limit).astype(kind)


def setup_inputs(seed: int = 0) -> dict:
    key_list = jax.random.split(jax.random.key(seed), 13)
    return {
        "features": draw_features(jax.random.fold_in(key_list[12], 71), 0),
        "neighbours_one": touch_ends(jax.random.randint(key_list[1], (CLOUDS, K, NPTS), 0, NPTS), jax.random.fold_in(key_list[1], 1), 0, NPTS - 1).astype(jnp.int32),
        "neighbours_two": touch_ends(jax.random.randint(key_list[2], (CLOUDS, K, NPTS), 0, NPTS), jax.random.fold_in(key_list[2], 1), 0, NPTS - 1).astype(jnp.int32),
        "weight_one": scatter_about(key_list[3], (2 * C0, C1), (2 * C0) ** -0.5, 0.5, (), jnp.float32),
        "gain_one": jnp.clip(1.0 + 0.15 * jax.random.normal(key_list[4], (C1,), jnp.float32), 0.25, 1.75),
        "shift_one": scatter_about(key_list[5], (C1,), 0.5, 3.0, (), jnp.float32),
        "weight_two": scatter_about(key_list[6], (2 * C1, C2), (2 * C1) ** -0.5, 0.375, (), jnp.float32),
        "gain_two": jnp.clip(1.0 + 0.15 * jax.random.normal(key_list[7], (C2,), jnp.float32), 0.25, 1.75),
        "shift_two": scatter_about(key_list[8], (C2,), 0.5, 3.0, (), jnp.float32),
        "grad_act": scatter_about(key_list[9], (CLOUDS, NPTS, C2), 1.0, 6.0, ((0, 8), (1, 4)), jnp.float32),
        "grad_max": scatter_about(key_list[10], (CLOUDS, C2), 8.0, 48.0, ((0, 8),), jnp.float32),
        "grad_mean": scatter_about(key_list[11], (CLOUDS, C2), 8.0, 48.0, ((0, 8),), jnp.float32),
    }


highest_mode = lax.Precision.HIGHEST
norm_eps = 1e-05

@jax.custom_vjp
def low(v):
    return lax.optimization_barrier(v.astype(jnp.bfloat16)).astype(jnp.float32)

@jax.custom_vjp
def low_back(v):
    return v

def low_keep(v):
    return (low(v), None)

def low_pass(kept, grad):
    return (grad,)

def back_keep(v):
    return (v, None)

def back_low(kept, grad):
    return (low(grad),)
low.defvjp(low_keep, low_pass)
low_back.defvjp(back_keep, back_low)

def smooth_leaky(inputs):
    return 0.2 * inputs + 0.8 * jax.nn.softplus(inputs)

def edge_block(cloud_rows, places, weight):
    neighbour_rows = cloud_rows[places.T]
    centre = jnp.broadcast_to(cloud_rows[:, None, :], neighbour_rows.shape)
    edge_feats = jnp.concatenate([centre, neighbour_rows - centre], axis=-1)
    return jnp.einsum('pkf,fo->pko', edge_feats, weight, precision=highest_mode)

def edge_layer(inputs, places, weight, gain_vec, bias_vec):
    edge_count = inputs.shape[0] * inputs.shape[1] * places.shape[1]

    def block_sum(operands):
        return lax.optimization_barrier(jnp.sum(edge_block(operands[0], operands[1], weight), axis=(0, 1)))
    mean_val = lax.optimization_barrier(jnp.sum(lax.map(jax.checkpoint(block_sum), (inputs, places)), axis=0)) / edge_count

    def block_square(operands):
        deviation = edge_block(operands[0], operands[1], weight) - mean_val
        return lax.optimization_barrier(jnp.sum(deviation * deviation, axis=(0, 1)))
    spread = lax.optimization_barrier(jnp.sum(lax.map(jax.checkpoint(block_square), (inputs, places)), axis=0)) / edge_count
    inv_std = lax.rsqrt(spread + norm_eps)

    def finish(operands):
        normed = (edge_block(operands[0], operands[1], weight) - mean_val) * inv_std
        return jax.nn.logsumexp(smooth_leaky(gain_vec * normed + bias_vec), axis=1)
    return lax.map(jax.checkpoint(finish), (inputs, places))

def reference(features, neighbours_one, neighbours_two, weight_one, gain_one, shift_one, weight_two, gain_two, shift_two, grad_act, grad_max, grad_mean):

    def forward(feat_in, first_weight, first_gain, first_shift, second_weight, second_gain, second_shift):
        hidden = edge_layer(feat_in, neighbours_one, first_weight, first_gain, first_shift)
        output = edge_layer(hidden, neighbours_two, second_weight, second_gain, second_shift)
        return (output, jax.nn.logsumexp(output, axis=1), lax.optimization_barrier(jnp.mean(output, axis=1)))
    results, pullback = jax.vjp(forward, features, weight_one, gain_one, shift_one, weight_two, gain_two, shift_two)
    grads = pullback((grad_act, grad_max, grad_mean))
    return (results[0], results[1], results[2], grads[0], grads[1], grads[2], grads[3], grads[4], grads[5], grads[6])
```

```python
import functools

import jax
import jax.numpy as jnp
from jax import lax
from jax.experimental import pallas as pl
from jax.experimental.pallas import tpu as pltpu
from jax.sharding import PartitionSpec as P

norm_eps = 1e-05
LOG2E = 1.4426950408889634
HIGHEST = lax.Precision.HIGHEST
BOTH = ("clouds", "pts")
MIB = 2**20


def f32(*shape):
    return jax.ShapeDtypeStruct(shape, jnp.float32)


def params(mib):
    return pltpu.CompilerParams(vmem_limit_bytes=mib * MIB)


def whole(shape):
    return pl.BlockSpec(shape, lambda *step: (0,) * len(shape))


SMEM = pl.BlockSpec(memory_space=pltpu.SMEM)


def exchange(x, axes, mask):
    size = lax.axis_size(axes)
    return lax.ppermute(x, axes, [(i, i ^ mask) for i in range(size)])


def bit_groups(size):
    bits = [1 << i for i in range(size.bit_length() - 1)]
    groups = [bits[:1]]
    rest = bits[1:]
    while rest:
        groups.append(rest[:2])
        rest = rest[2:]
    return groups


def group_values(x, bits):
    masks = [0]
    for bit in bits:
        masks = masks + [mask | bit for mask in masks]
    return [x] + [exchange(x, BOTH, mask) for mask in masks[1:]]


def pair_sum(values):
    while len(values) > 1:
        values = [values[i] + values[i + 1] for i in range(0, len(values), 2)]
    return values[0]


def sum_all(x):
    for bits in bit_groups(lax.axis_size(BOTH)):
        x = pair_sum(group_values(x, bits))
    return x


def join_stats(stat, count):
    for bits in bit_groups(lax.axis_size(BOTH)):
        parts = group_values(stat, bits)
        mean = pair_sum([part[0:1] for part in parts]) / len(parts)
        away = pair_sum([(part[0:1] - mean) ** 2 for part in parts])
        stat = jnp.concatenate([mean, pair_sum([part[1:2] for part in parts]) + count * away], axis=0)
        count = count * len(parts)
    return stat


def pack_kernel(slots, me_ref, feat_ref, one_ref, two_ref, *outs):
    me = me_ref[0]
    rows, width = feat_ref.shape[1], feat_ref.shape[2]
    for mask, out in enumerate(outs):
        cloud = me ^ mask
        ids = jnp.concatenate([one_ref[cloud], two_ref[cloud]], axis=0) ^ (cloud * rows)
        fill = jnp.zeros((128 - width - 2 * slots, rows), jnp.float32)
        ids = jnp.concatenate([ids.astype(jnp.float32), fill], axis=0)
        out[...] = jnp.concatenate([feat_ref[cloud], ids.T], axis=1)


def pack(me, features, neighbours_one, neighbours_two):
    clouds, rows, _ = features.shape
    slots = neighbours_one.shape[1]
    return pl.pallas_call(
        functools.partial(pack_kernel, slots),
        in_specs=[SMEM] + [pl.BlockSpec(memory_space=pltpu.VMEM)] * 3,
        out_shape=[f32(rows, 128)] * clouds,
        compiler_params=params(16),
        name="pack",
    )(me, features, neighbours_one, neighbours_two)


def split_kernel(me_ref, x_ref, *outs):
    me = me_ref[0]
    for mask, out in enumerate(outs):
        out[...] = x_ref[me ^ mask]


def split(me, x):
    clouds, rows, width = x.shape
    return pl.pallas_call(
        split_kernel,
        in_specs=[SMEM, pl.BlockSpec(memory_space=pltpu.VMEM)],
        out_shape=[f32(rows, width)] * clouds,
        compiler_params=params(16),
        name="split",
    )(me, x)


def unpack_output_kernel(rows, me_ref, *refs):
    parts, (act_ref, max_ref, mean_ref) = refs[:-3], refs[-3:]
    me = me_ref[0]
    for mask, part in enumerate(parts):
        cloud = me ^ mask
        act_ref[cloud] = part[0:rows]
        max_ref[pl.ds(cloud, 1), :] = part[rows : rows + 1]
        mean_ref[pl.ds(cloud, 1), :] = part[rows + 1 : rows + 2]


def unpack_output(me, parts):
    clouds, width = len(parts), parts[0].shape[1]
    rows = parts[0].shape[0] - 8
    return pl.pallas_call(
        functools.partial(unpack_output_kernel, rows),
        in_specs=[SMEM] + [pl.BlockSpec(memory_space=pltpu.VMEM)] * clouds,
        out_shape=[f32(clouds, rows, width), f32(clouds, width), f32(clouds, width)],
        compiler_params=params(16),
        name="unpack_output",
    )(me, *parts)


def unpack_grad_kernel(me_ref, *refs):
    me = me_ref[0]
    for mask, part in enumerate(refs[:-1]):
        refs[-1][me ^ mask] = part[...]


def unpack_grad(me, parts):
    return pl.pallas_call(
        unpack_grad_kernel,
        in_specs=[SMEM] + [pl.BlockSpec(memory_space=pltpu.VMEM)] * len(parts),
        out_shape=f32(len(parts), *parts[0].shape),
        compiler_params=params(16),
        name="unpack_grad",
    )(me, *parts)


def two_terms(x):
    high = x.astype(jnp.bfloat16)
    low = (x - high.astype(jnp.float32)).astype(jnp.bfloat16)
    return jnp.concatenate([high, low], axis=1)


def halves_sum(x):
    half = x.shape[1] // 2
    return x[:, :half] + x[:, half:]


def column_sum(x):
    return jnp.sum(x, axis=0, keepdims=True)


def count_links(ids_ref, first, slots, wide, links):
    points = links.shape[0]
    block = 256
    lane_ids = lax.broadcasted_iota(jnp.int32, (16, points), 0).astype(jnp.bfloat16)
    one = jnp.ones((16, points), jnp.bfloat16)
    zero = jnp.zeros((16, points), jnp.bfloat16)
    for start in range(0, points, block):
        for k in range(slots):
            local = ids_ref[first + k : first + k + 1, :] - float(start)
            local = jnp.where((local >= 0) & (local < block), local, -1.0)
            wide[k] = jnp.broadcast_to(local, (16, points)).astype(jnp.bfloat16)

        def sixteen(step, carry):
            here = lane_ids + (step * 16).astype(jnp.float32).astype(jnp.bfloat16)
            total = zero
            for k in range(slots):
                total = total + jnp.where(wide[k] == here, one, zero)
            links[pl.ds(pl.multiple_of(start + step * 16, 16), 16), :] = total
            return carry

        lax.fori_loop(0, block // 16, sixteen, 0)


def table_stats(x, weight, links, slots, a_ref, b_ref, in_ref, deg_ref, stat_ref):
    points, width = x.shape
    outs = weight.shape[1]
    upper, lower = weight[:width], weight[width:]
    both = jnp.dot(x, jnp.concatenate([upper - lower, lower], axis=1), precision=HIGHEST)
    a, b = both[:, :outs], both[:, outs:]
    mean_a = column_sum(a) / points
    a_off = a - mean_a
    seen = halves_sum(jnp.dot(links, two_terms(a_off), preferred_element_type=jnp.float32))
    degree = jnp.sum(links.astype(jnp.float32), axis=1, keepdims=True)
    mean_b = column_sum(degree * b) / (points * slots)
    b_off = b - mean_b
    inward = seen + degree * b_off
    a_ref[...] = a
    b_ref[...] = b
    in_ref[...] = inward
    deg_ref[...] = jnp.broadcast_to(degree, deg_ref.shape)
    stat_ref[0:1, :] = mean_a + mean_b
    stat_ref[1:2, :] = slots * column_sum(a_off * a_off) + column_sum((seen + inward) * b_off)


def first_kernel(slots, width, *refs):
    parts, (weight_ref, x_ref, ids_ref, a_ref, b_ref, in_ref, deg_ref, stat_ref, links, wide) = (
        refs[:-10],
        refs[-10:],
    )
    rows = parts[0].shape[0]
    for m, part in enumerate(parts):
        x_ref[m * rows : (m + 1) * rows, :] = part[...]
    ids_ref[...] = x_ref[...].T[width:, :]
    count_links(ids_ref, 0, slots, wide, links)
    table_stats(
        x_ref[:, :width], weight_ref[...], links[...], slots, a_ref, b_ref, in_ref, deg_ref, stat_ref
    )


def first_tables(parts, weight, slots):
    points = len(parts) * parts[0].shape[0]
    width, outs = weight.shape[0] // 2, weight.shape[1]
    return pl.pallas_call(
        functools.partial(first_kernel, slots, width),
        out_shape=[
            f32(points, 128),
            f32(128 - width, points),
            f32(points, outs),
            f32(points, outs),
            f32(points, outs),
            f32(points, 128),
            f32(2, outs),
        ],
        scratch_shapes=[
            pltpu.VMEM((points, points), jnp.bfloat16),
            pltpu.VMEM((slots, 16, points), jnp.bfloat16),
        ],
        compiler_params=params(40),
        name="first_tables",
    )(*parts, weight)


def links_kernel(first, slots, ids_ref, links, wide):
    count_links(ids_ref, first, slots, wide, links)


def count_second_links(ids, first, slots):
    points = ids.shape[1]
    return pl.pallas_call(
        functools.partial(links_kernel, first, slots),
        out_shape=jax.ShapeDtypeStruct((points, points), jnp.bfloat16),
        scratch_shapes=[pltpu.VMEM((slots, 16, points), jnp.bfloat16)],
        compiler_params=params(24),
        cost_estimate=pl.CostEstimate(flops=10**9, bytes_accessed=16 * MIB, transcendentals=0),
        name="links_two",
    )(ids)


def second_kernel(slots, x_ref, weight_ref, links, a_ref, b_ref, in_ref, deg_ref, stat_ref):
    table_stats(
        x_ref[...], weight_ref[...], links[...], slots, a_ref, b_ref, in_ref, deg_ref, stat_ref
    )


def second_tables(x, weight, links, slots):
    points, outs = x.shape[0], weight.shape[1]
    return pl.pallas_call(
        functools.partial(second_kernel, slots),
        out_shape=[
            f32(points, outs),
            f32(points, outs),
            f32(points, outs),
            f32(points, 128),
            f32(2, outs),
        ],
        compiler_params=params(40),
        name="second_tables",
    )(x, weight, links)


def edge_kernel(
    edges, slots, first, group, tile, x_ref, a_ref, b_ref, stat_ref, gain_ref, shift_ref,
    out_ref, weight_ref, inv_ref, slope_ref, moment_ref, ysum_ref, held, table, centre,
):
    points, width = a_ref.shape
    tiles = points // tile
    step = pl.program_id(0)
    block = 8

    @pl.when(step == 0)
    def _():
        scale = gain_ref[...] * lax.rsqrt(stat_ref[1:2, :] / edges + norm_eps) * LOG2E
        middle = column_sum(b_ref[...]) / points
        table[...] = two_terms((b_ref[...] - middle) * scale)
        centre[...] = (a_ref[...] + (middle - stat_ref[0:1, :])) * scale + shift_ref[...] * LOG2E

    def gather(k):
        rows = pl.ds(pl.multiple_of(step * tile, tile), tile)
        columns = lax.broadcasted_iota(jnp.int32, (tile, points), 1).astype(jnp.float32)
        picks = [
            jnp.where(x_ref[rows, first + k + g : first + k + g + 1] == columns, 1.0, 0.0).astype(
                jnp.bfloat16
            )
            for g in range(group)
        ]
        found = jnp.dot(jnp.concatenate(picks, axis=0), table[...], preferred_element_type=jnp.float32)
        for g in range(group):
            held[step % 2, k + g] = centre[rows, :] + halves_sum(found[g * tile : (g + 1) * tile])

    def rise(y):
        grown = 1.0 + jnp.exp2(jnp.minimum(y, 64.0))
        return 0.2 * y + jnp.maximum(0.8 * y, (0.8 * LOG2E) * jnp.log(grown)), grown

    def activate(b):
        mine = (step + 1) % 2
        rows = pl.ds(b * block, block)
        top = held[mine, 0, rows, :]
        for k in range(1, slots):
            top = jnp.maximum(top, held[mine, k, rows, :])
        peak, _ = rise(top)
        mass = slope = moment = total = jnp.zeros((block, width), jnp.float32)
        for k in range(slots):
            y = held[mine, k, rows, :]
            level, grown = rise(y)
            share = jnp.exp2(level - peak)
            part = share * (1.0 - 0.8 * pltpu.reciprocal(grown))
            weight_ref[k, rows, :] = part
            mass = mass + share
            slope = slope + part
            moment = moment + part * y
            total = total + y
        out_ref[rows, :] = peak * (1.0 / LOG2E) + jnp.log(mass)
        inv = 1.0 / mass
        inv_ref[rows, :] = inv
        slope_ref[rows, :] = slope * inv
        moment_ref[rows, :] = moment * inv * (1.0 / LOG2E)
        ysum_ref[rows, :] = total * (1.0 / LOG2E)

    blocks = tile // block

    @pl.when(step == 0)
    def _():
        for k in range(0, slots, group):
            gather(k)

    @pl.when((step > 0) & (step < tiles))
    def _():
        done = 0
        for k in range(0, slots, group):
            goal = (k + group) * blocks // slots
            while done < goal:
                activate(done)
                done += 1
            gather(k)

    @pl.when(step == tiles)
    def _():
        for b in range(blocks):
            activate(b)


def edge_forward(edges, slots, first, group, tile, x, a, b, stat, gain, shift):
    points, width = a.shape
    before = pl.BlockSpec((tile, width), lambda step: (jnp.maximum(step - 1, 0), 0))
    return pl.pallas_call(
        functools.partial(edge_kernel, edges, slots, first, group, tile),
        grid=(points // tile + 1,),
        in_specs=[whole(v.shape) for v in (x, a, b, stat, gain, shift)],
        out_specs=[
            before,
            pl.BlockSpec((slots, tile, width), lambda step: (0, jnp.maximum(step - 1, 0), 0)),
        ]
        + [before] * 4,
        out_shape=[f32(points, width), f32(slots, points, width)] + [f32(points, width)] * 4,
        scratch_shapes=[
            pltpu.VMEM((2, slots, tile, width), jnp.float32),
            pltpu.VMEM((points, 2 * width), jnp.bfloat16),
            pltpu.VMEM((points, width), jnp.float32),
        ],
        compiler_params=params(40),
        name="edges",
    )(x, a, b, stat, gain, shift)


def pool_kernel(me_ref, out_ref, inv_ref, slope_ref, moment_ref, gmax_ref, gmean_ref, *refs):
    count = (len(refs) - 3) // 2
    acts, parts = refs[:count], refs[count : 2 * count]
    scaled_ref, own_ref, sums_ref = refs[2 * count :]
    me = me_ref[0]
    points, width = out_ref.shape
    rows = points // count
    out = out_ref[...]
    top = jnp.max(out, axis=0, keepdims=True)
    pool = top + jnp.log(column_sum(jnp.exp(out - top)))
    mean = column_sum(out) / points
    to_max = gmax_ref[pl.ds(me, 1), :]
    to_mean = gmean_ref[pl.ds(me, 1), :] / points
    own_sum = moment_sum = jnp.zeros((1, width), jnp.float32)
    for m in range(count):
        here = slice(m * rows, (m + 1) * rows)
        part = out[here]
        parts[m][0:rows, :] = part
        parts[m][rows : rows + 1, :] = pool
        parts[m][rows + 1 : rows + 2, :] = mean
        parts[m][rows + 2 : rows + 8, :] = jnp.zeros((6, width), jnp.float32)
        grad = acts[m][...] + to_max * jnp.exp(part - pool) + to_mean
        own = grad * slope_ref[here, :]
        scaled_ref[here, :] = grad * inv_ref[here, :]
        own_ref[here, :] = own
        own_sum = own_sum + column_sum(own)
        moment_sum = moment_sum + column_sum(grad * moment_ref[here, :])
    sums_ref[0:1, :] = own_sum
    sums_ref[1:2, :] = moment_sum


def pools(me, out, inv, slope, moment, grad_max, grad_mean, acts):
    points, width = out.shape
    count = len(acts)
    rows = points // count
    results = pl.pallas_call(
        pool_kernel,
        in_specs=[SMEM] + [pl.BlockSpec(memory_space=pltpu.VMEM)] * (6 + count),
        out_shape=[f32(rows + 8, width)] * count + [f32(points, width)] * 2 + [f32(2, width)],
        compiler_params=params(40),
        name="pools",
    )(me, out, inv, slope, moment, grad_max, grad_mean, *acts)
    return results[:count], results[count], results[count + 1], results[count + 2]


def scatter_kernel(first, group, ids_ref, grad_ref, weight_ref, sum_ref):
    step = pl.program_id(0)
    points = grad_ref.shape[0]
    rows = lax.broadcasted_iota(jnp.int32, (points, points), 0).astype(jnp.float32)
    picks, terms = [], []
    for g in range(group):
        ids = ids_ref[pl.ds(first + step * group + g, 1), :]
        picks.append(jnp.where(ids == rows, 1.0, 0.0).astype(jnp.bfloat16))
        terms.append(two_terms(grad_ref[...] * weight_ref[g]))
    found = halves_sum(
        jnp.dot(
            jnp.concatenate(picks, axis=1),
            jnp.concatenate(terms, axis=0),
            preferred_element_type=jnp.float32,
        )
    )

    @pl.when(step == 0)
    def _():
        sum_ref[...] = found

    @pl.when(step > 0)
    def _():
        sum_ref[...] += found


def scatter(ids, first, grad, weight, start, stop, group):
    points, width = grad.shape
    edges = (stop - start) * points
    return pl.pallas_call(
        functools.partial(scatter_kernel, first + start, group),
        grid=((stop - start) // group,),
        in_specs=[
            whole(ids.shape),
            whole(grad.shape),
            pl.BlockSpec((group, points, width), lambda step: (start // group + step, 0, 0)),
        ],
        out_specs=whole((points, width)),
        out_shape=f32(points, width),
        compiler_params=params(48),
        cost_estimate=pl.CostEstimate(
            flops=4 * edges * points * width, bytes_accessed=4 * edges * width, transcendentals=0
        ),
        name="scatter",
    )(ids, grad, weight)


def point_grads(edges, slots, own, inward_grads, ysum, inward, degree, local, stat, sums, gain, shift):
    spread = lax.rsqrt(stat[1:2, :] / edges + norm_eps)
    scale = gain * spread
    own_all = sums[0:1, :]
    gain_all = (sums[1:2, :] - shift * own_all) / gain
    shift_part = own_all / edges
    gain_part = gain_all / edges
    leave = scale * (own - slots * shift_part - gain_part * ((ysum - slots * shift) / gain))
    normed = spread * (inward + degree * (local[0:1, :] - stat[0:1, :]))
    reach = scale * (inward_grads - degree * shift_part - gain_part * normed)
    return leave, reach, gain_all


def to_inputs(leave, reach, weight, width):
    turned = jnp.concatenate([weight[:width] - weight[width:], weight[width:]], axis=1)
    return lax.dot_general(
        jnp.concatenate([leave, reach], axis=1),
        turned,
        (((1,), (1,)), ((), ())),
        precision=HIGHEST,
        preferred_element_type=jnp.float32,
    )


def to_weight(x, leave, reach, grad_ref):
    width, outs = x.shape[1], leave.shape[1]
    both = lax.dot_general(
        x,
        jnp.concatenate([leave, reach - leave], axis=1),
        (((0,), (0,)), ((), ())),
        precision=HIGHEST,
        preferred_element_type=jnp.float32,
    )
    grad_ref[0:width, :] = both[:, :outs]
    grad_ref[width:, :] = both[:, outs:]


def middle_kernel(
    edges, slots, own_ref, ysum_ref, in_ref, deg_ref, local_ref, stat_ref, sums_ref, gain_ref,
    shift_ref, x_ref, weight_ref, inv_ref, slope_ref, moment_ref, *refs,
):
    reached, (wgrad_ref, scaled_ref, next_ref, next_sums_ref, gain_out_ref) = refs[:-5], refs[-5:]
    inward_grads = reached[0][...]
    for more in reached[1:]:
        inward_grads = inward_grads + more[...]
    leave, reach, gain_all = point_grads(
        edges, slots, own_ref[...], inward_grads, ysum_ref[...], in_ref[...], deg_ref[:, 0:1],
        local_ref[...], stat_ref[...], sums_ref[...], gain_ref[...], shift_ref[...],
    )
    x = x_ref[...]
    to_weight(x, leave, reach, wgrad_ref)
    gain_out_ref[...] = gain_all
    grad = to_inputs(leave, reach, weight_ref[...], x.shape[1])
    own = grad * slope_ref[...]
    scaled_ref[...] = grad * inv_ref[...]
    next_ref[...] = own
    next_sums_ref[0:1, :] = column_sum(own)
    next_sums_ref[1:2, :] = column_sum(grad * moment_ref[...])


def middle(edges, slots, own, ysum, inward, degree, local, stat, sums, gain, shift, x, weight, inv, slope, moment, reached):
    points, width = x.shape
    outs = weight.shape[1]
    return pl.pallas_call(
        functools.partial(middle_kernel, edges, slots),
        out_shape=[
            f32(2 * width, outs),
            f32(points, width),
            f32(points, width),
            f32(2, width),
            f32(1, outs),
        ],
        compiler_params=params(48),
        name="middle",
    )(own, ysum, inward, degree, local, stat, sums, gain, shift, x, weight, inv, slope, moment, *reached)


def last_kernel(
    edges, slots, count, own_ref, ysum_ref, in_ref, deg_ref, local_ref, stat_ref, sums_ref,
    gain_ref, shift_ref, x_ref, weight_ref, *refs,
):
    reached, (wgrad_ref, gain_out_ref), parts = (
        refs[: -2 - count],
        refs[-2 - count : -count],
        refs[-count:],
    )
    inward_grads = reached[0][...]
    for more in reached[1:]:
        inward_grads = inward_grads + more[...]
    leave, reach, gain_all = point_grads(
        edges, slots, own_ref[...], inward_grads, ysum_ref[...], in_ref[...], deg_ref[:, 0:1],
        local_ref[...], stat_ref[...], sums_ref[...], gain_ref[...], shift_ref[...],
    )
    width = weight_ref.shape[0] // 2
    to_weight(x_ref[:, :width], leave, reach, wgrad_ref)
    gain_out_ref[...] = gain_all
    grad = to_inputs(leave, reach, weight_ref[...], width)
    rows = grad.shape[0] // count
    for m in range(count):
        parts[m][...] = grad[m * rows : (m + 1) * rows]


def last(edges, slots, count, own, ysum, inward, degree, local, stat, sums, gain, shift, x, weight, reached):
    points = x.shape[0]
    width, outs = weight.shape[0] // 2, weight.shape[1]
    results = pl.pallas_call(
        functools.partial(last_kernel, edges, slots, count),
        out_shape=[f32(2 * width, outs), f32(1, outs)] + [f32(points // count, width)] * count,
        compiler_params=params(48),
        name="last",
    )(own, ysum, inward, degree, local, stat, sums, gain, shift, x, weight, *reached)
    return results[0], results[1], results[2:]


def body(
    features,
    neighbours_one,
    neighbours_two,
    weight_one,
    gain_one,
    shift_one,
    weight_two,
    gain_two,
    shift_two,
    grad_act,
    grad_max,
    grad_mean,
):
    clouds, rows, width = features.shape
    slots = neighbours_one.shape[1]
    count = lax.axis_size("pts")
    assert clouds == count
    points = rows * count
    local_edges = points * slots
    edges = float(local_edges * lax.axis_size(BOTH))
    me = lax.axis_index("pts").astype(jnp.int32).reshape(1)
    gain_one, shift_one, gain_two, shift_two = (
        v.reshape(1, -1) for v in (gain_one, shift_one, gain_two, shift_two)
    )

    def to_owner(parts):
        return [parts[0]] + [exchange(part, "pts", m) for m, part in enumerate(parts) if m]

    with jax.named_scope("bring_clouds"):
        parts = to_owner(pack(me, features, neighbours_one, neighbours_two))
    with jax.named_scope("bring_cotangents"):
        acts = to_owner(split(me, grad_act))

    with jax.named_scope("layer_one"):
        x, ids, a_one, b_one, in_one, deg_one, local_one = first_tables(parts, weight_one, slots)
        links = count_second_links(ids, slots, slots)
        stat_one = join_stats(local_one, local_edges)
        hidden, share_one, inv_one, slope_one, moment_one, ysum_one = edge_forward(
            edges, slots, width, 2, 128, x, a_one, b_one, stat_one, gain_one, shift_one
        )
    with jax.named_scope("layer_two"):
        a_two, b_two, in_two, deg_two, local_two = second_tables(hidden, weight_two, links, slots)
        stat_two = join_stats(local_two, local_edges)
        out, share_two, inv_two, slope_two, moment_two, ysum_two = edge_forward(
            edges, slots, width + slots, 4, 64, x, a_two, b_two, stat_two, gain_two, shift_two
        )
    with jax.named_scope("pools"):
        out_parts, scaled_two, own_two, sums_two = pools(
            me, out, inv_two, slope_two, moment_two, grad_max, grad_mean, acts
        )
        output, pool_max, pool_mean = unpack_output(me, to_owner(out_parts))

    cuts = ((0, 8), (8, 16), (16, 20))
    with jax.named_scope("layer_two_back"):
        sums_two = sum_all(sums_two)
        reached = [scatter(ids, slots, scaled_two, share_two, lo, hi, 4) for lo, hi in cuts]
        wgrad_two, scaled_one, own_one, sums_one, gain_grad_two = middle(
            edges, slots, own_two, ysum_two, in_two, deg_two, local_two, stat_two, sums_two,
            gain_two, shift_two, hidden, weight_two, inv_one, slope_one, moment_one, reached,
        )
        wgrad_two = sum_all(wgrad_two)
    with jax.named_scope("layer_one_back"):
        sums_one = sum_all(sums_one)
        reached = [scatter(ids, 0, scaled_one, share_one, lo, hi, 4) for lo, hi in cuts]
        wgrad_one, gain_grad_one, grad_parts = last(
            edges, slots, count, own_one, ysum_one, in_one, deg_one, local_one, stat_one, sums_one,
            gain_one, shift_one, x, weight_one, reached,
        )
        wgrad_one = sum_all(wgrad_one)
        grad_features = unpack_grad(me, to_owner(grad_parts))
    return (
        output,
        pool_max,
        pool_mean,
        grad_features,
        wgrad_one,
        gain_grad_one.reshape(-1),
        sums_one[0],
        wgrad_two,
        gain_grad_two.reshape(-1),
        sums_two[0],
    )


def solution(mesh):
    placed = (
        P("clouds", "pts", None),
        P("clouds", None, "pts"),
        P("clouds", None, "pts"),
        P(),
        P(),
        P(),
        P(),
        P(),
        P(),
        P("clouds", "pts", None),
        P("clouds", None),
        P("clouds", None),
    )
    return jax.shard_map(
        body,
        mesh=mesh,
        in_specs=placed,
        out_specs=(
            P("clouds", "pts", None),
            P("clouds", None),
            P("clouds", None),
            P("clouds", "pts", None),
            P(),
            P(),
            P(),
            P(),
            P(),
            P(),
        ),
        check_vma=False,
    )
```

```python
import functools

import jax
import jax.numpy as jnp
from jax import lax
from jax.experimental import pallas as pl
from jax.experimental.pallas import tpu as pltpu
from jax.sharding import PartitionSpec as P

norm_eps = 1e-05
LOG2E = 1.4426950408889634
HIGHEST = lax.Precision.HIGHEST
BOTH = ("clouds", "pts")
MIB = 2**20


def f32(*shape):
    return jax.ShapeDtypeStruct(shape, jnp.float32)


def params(mib):
    return pltpu.CompilerParams(vmem_limit_bytes=mib * MIB)


def whole(shape):
    return pl.BlockSpec(shape, lambda *step: (0,) * len(shape))


SMEM = pl.BlockSpec(memory_space=pltpu.SMEM)


def exchange(x, axes, mask):
    size = lax.axis_size(axes)
    return lax.ppermute(x, axes, [(i, i ^ mask) for i in range(size)])


def bit_groups(size):
    bits = [1 << i for i in range(size.bit_length() - 1)]
    groups = [bits[:1]] if bits else []
    rest = bits[1:]
    while rest:
        groups.append(rest[:2])
        rest = rest[2:]
    return groups


def stages():
    yield "pts", list(range(1, lax.axis_size("pts")))
    for bits in bit_groups(lax.axis_size("clouds")):
        masks = [0]
        for bit in bits:
            masks = masks + [mask | bit for mask in masks]
        yield "clouds", masks[1:]


def swap(x, axes, masks):
    return [x] + [exchange(x, axes, mask) for mask in masks]


def pair_sum(values):
    while len(values) > 1:
        values = [values[i] + values[i + 1] for i in range(0, len(values), 2)]
    return values[0]


def sum_over_clouds(x):
    for axis, masks in list(stages())[1:]:
        x = pair_sum(swap(x, axis, masks))
    return x


def join_stats(stat, count):
    for axis, masks in stages():
        parts = swap(stat, axis, masks)
        mean = pair_sum([part[0:1] for part in parts]) / len(parts)
        away = pair_sum([(part[0:1] - mean) ** 2 for part in parts])
        stat = jnp.concatenate([mean, pair_sum([part[1:2] for part in parts]) + count * away], axis=0)
        count = count * len(parts)
    return stat


def pack_kernel(slots, me_ref, feat_ref, one_ref, two_ref, *outs):
    me = me_ref[0]
    width, rows = feat_ref.shape[1], feat_ref.shape[2]
    for mask, out in enumerate(outs):
        cloud = me ^ mask
        out[0:width, :] = feat_ref[cloud]
        for k in range(slots):
            for at, ids in ((width, one_ref), (width + slots, two_ref)):
                row = ids[k, pl.ds(cloud, 1), :] ^ (cloud * rows)
                out[at + k : at + k + 1, :] = row.astype(jnp.float32)


def pack(me, features, neighbours_one, neighbours_two):
    clouds, rows, width = features.shape
    slots = neighbours_one.shape[1]
    return pl.pallas_call(
        functools.partial(pack_kernel, slots),
        in_specs=[SMEM] + [pl.BlockSpec(memory_space=pltpu.VMEM)] * 3,
        out_shape=[f32(width + 2 * slots, rows)] * clouds,
        compiler_params=params(16),
        name="pack",
    )(
        me,
        jnp.swapaxes(features, 1, 2),
        jnp.swapaxes(neighbours_one, 0, 1),
        jnp.swapaxes(neighbours_two, 0, 1),
    )


def split_kernel(me_ref, x_ref, *outs):
    me = me_ref[0]
    for mask, out in enumerate(outs):
        out[...] = x_ref[me ^ mask]


def split(me, x):
    clouds, rows, width = x.shape
    return pl.pallas_call(
        split_kernel,
        in_specs=[SMEM, pl.BlockSpec(memory_space=pltpu.VMEM)],
        out_shape=[f32(rows, width)] * clouds,
        compiler_params=params(16),
        name="split",
    )(me, x)


def unpack_output_kernel(rows, me_ref, *refs):
    parts, (act_ref, max_ref, mean_ref) = refs[:-3], refs[-3:]
    me = me_ref[0]
    for mask, part in enumerate(parts):
        cloud = me ^ mask
        act_ref[cloud] = part[0:rows]
        max_ref[pl.ds(cloud, 1), :] = part[rows : rows + 1]
        mean_ref[pl.ds(cloud, 1), :] = part[rows + 1 : rows + 2]


def unpack_output(me, parts):
    clouds, width = len(parts), parts[0].shape[1]
    rows = parts[0].shape[0] - 8
    return pl.pallas_call(
        functools.partial(unpack_output_kernel, rows),
        in_specs=[SMEM] + [pl.BlockSpec(memory_space=pltpu.VMEM)] * clouds,
        out_shape=[f32(clouds, rows, width), f32(clouds, width), f32(clouds, width)],
        compiler_params=params(16),
        name="unpack_output",
    )(me, *parts)


def unpack_grad_kernel(me_ref, *refs):
    parts, (grad_ref, wgrad_ref) = refs[:-2], refs[-2:]
    me = me_ref[0]
    width = grad_ref.shape[1]
    piece = wgrad_ref.shape[0] // len(parts)
    for mask, part in enumerate(parts):
        other = me ^ mask
        grad_ref[other] = part[0:width]
        wgrad_ref[pl.ds(pl.multiple_of(other * piece, piece), piece), :] = part[2 * width :]


def unpack_grad(me, parts, width):
    rows, lanes = parts[0].shape
    count = len(parts)
    return pl.pallas_call(
        unpack_grad_kernel,
        in_specs=[SMEM] + [pl.BlockSpec(memory_space=pltpu.VMEM)] * count,
        out_shape=[f32(count, width, lanes), f32(count * (rows - 2 * width), lanes)],
        compiler_params=params(16),
        name="unpack_grad",
    )(me, *parts)


def two_terms(x):
    high = x.astype(jnp.bfloat16)
    low = (x - high.astype(jnp.float32)).astype(jnp.bfloat16)
    return jnp.concatenate([high, low], axis=1)


def halves_sum(x):
    half = x.shape[1] // 2
    return x[:, :half] + x[:, half:]


def column_sum(x):
    return jnp.sum(x, axis=0, keepdims=True)


def count_links(ids_ref, first, slots, wide, links):
    points = links.shape[0]
    block = 256
    lane_ids = lax.broadcasted_iota(jnp.int32, (16, points), 0).astype(jnp.bfloat16)
    one = jnp.ones((16, points), jnp.bfloat16)
    zero = jnp.zeros((16, points), jnp.bfloat16)
    for start in range(0, points, block):
        for k in range(slots):
            local = ids_ref[first + k : first + k + 1, :] - float(start)
            local = jnp.where((local >= 0) & (local < block), local, -1.0)
            wide[k] = jnp.broadcast_to(local, (16, points)).astype(jnp.bfloat16)

        def sixteen(step, carry):
            here = lane_ids + (step * 16).astype(jnp.float32).astype(jnp.bfloat16)
            total = zero
            for k in range(slots):
                total = total + jnp.where(wide[k] == here, one, zero)
            links[pl.ds(pl.multiple_of(start + step * 16, 16), 16), :] = total
            return carry

        lax.fori_loop(0, block // 16, sixteen, 0)


def table_stats(x, weight, links, slots, a_ref, b_ref, in_ref, deg_ref, stat_ref):
    points, width = x.shape
    outs = weight.shape[1]
    upper, lower = weight[:width], weight[width:]
    both = jnp.dot(x, jnp.concatenate([upper - lower, lower], axis=1), precision=HIGHEST)
    a, b = both[:, :outs], both[:, outs:]
    mean_a = column_sum(a) / points
    a_off = a - mean_a
    seen = halves_sum(jnp.dot(links, two_terms(a_off), preferred_element_type=jnp.float32))
    degree = jnp.sum(links.astype(jnp.float32), axis=1, keepdims=True)
    mean_b = column_sum(degree * b) / (points * slots)
    b_off = b - mean_b
    inward = seen + degree * b_off
    a_ref[...] = a
    b_ref[...] = b
    in_ref[...] = inward
    deg_ref[...] = jnp.broadcast_to(degree, deg_ref.shape)
    stat_ref[0:1, :] = mean_a + mean_b
    stat_ref[1:2, :] = slots * column_sum(a_off * a_off) + column_sum((seen + inward) * b_off)


def first_kernel(slots, width, *refs):
    parts, (weight_ref, x_ref, ids_ref, a_ref, b_ref, in_ref, deg_ref, stat_ref, links, wide) = (
        refs[:-10],
        refs[-10:],
    )
    rows = parts[0].shape[1]
    fill = jnp.zeros((128 - parts[0].shape[0], rows), jnp.float32)
    for m, part in enumerate(parts):
        ids_ref[:, m * rows : (m + 1) * rows] = part[width:, :]
        x_ref[m * rows : (m + 1) * rows, :] = jnp.concatenate([part[...], fill], axis=0).T
    count_links(ids_ref, 0, slots, wide, links)
    table_stats(
        x_ref[:, :width], weight_ref[...], links[...], slots, a_ref, b_ref, in_ref, deg_ref, stat_ref
    )


def first_tables(parts, weight, slots):
    points = len(parts) * parts[0].shape[1]
    width, outs = weight.shape[0] // 2, weight.shape[1]
    return pl.pallas_call(
        functools.partial(first_kernel, slots, width),
        out_shape=[
            f32(points, 128),
            f32(2 * slots, points),
            f32(points, outs),
            f32(points, outs),
            f32(points, outs),
            f32(points, 128),
            f32(2, outs),
        ],
        scratch_shapes=[
            pltpu.VMEM((points, points), jnp.bfloat16),
            pltpu.VMEM((slots, 16, points), jnp.bfloat16),
        ],
        compiler_params=params(40),
        name="first_tables",
    )(*parts, weight)


def links_kernel(first, slots, ids_ref, links, wide):
    count_links(ids_ref, first, slots, wide, links)


def count_second_links(ids, first, slots):
    points = ids.shape[1]
    return pl.pallas_call(
        functools.partial(links_kernel, first, slots),
        out_shape=jax.ShapeDtypeStruct((points, points), jnp.bfloat16),
        scratch_shapes=[pltpu.VMEM((slots, 16, points), jnp.bfloat16)],
        compiler_params=params(24),
        cost_estimate=pl.CostEstimate(flops=10**9, bytes_accessed=16 * MIB, transcendentals=0),
        name="links_two",
    )(ids)


def second_kernel(slots, x_ref, weight_ref, links, a_ref, b_ref, in_ref, deg_ref, stat_ref):
    table_stats(
        x_ref[...], weight_ref[...], links[...], slots, a_ref, b_ref, in_ref, deg_ref, stat_ref
    )


def second_tables(x, weight, links, slots):
    points, outs = x.shape[0], weight.shape[1]
    return pl.pallas_call(
        functools.partial(second_kernel, slots),
        out_shape=[
            f32(points, outs),
            f32(points, outs),
            f32(points, outs),
            f32(points, 128),
            f32(2, outs),
        ],
        compiler_params=params(40),
        name="second_tables",
    )(x, weight, links)


def edge_kernel(
    edges, slots, first, group, tile, x_ref, a_ref, b_ref, stat_ref, gain_ref, shift_ref,
    out_ref, weight_ref, inv_ref, slope_ref, moment_ref, ysum_ref, held, table, centre,
):
    points, width = a_ref.shape
    tiles = points // tile
    step = pl.program_id(0)
    block = 8

    @pl.when(step == 0)
    def _():
        scale = gain_ref[...] * lax.rsqrt(stat_ref[1:2, :] / edges + norm_eps) * LOG2E
        middle = column_sum(b_ref[...]) / points
        table[...] = two_terms((b_ref[...] - middle) * scale)
        centre[...] = (a_ref[...] + (middle - stat_ref[0:1, :])) * scale + shift_ref[...] * LOG2E

    def gather(k):
        rows = pl.ds(pl.multiple_of(step * tile, tile), tile)
        columns = lax.broadcasted_iota(jnp.int32, (tile, points), 1).astype(jnp.float32)
        picks = [
            jnp.where(x_ref[rows, first + k + g : first + k + g + 1] == columns, 1.0, 0.0).astype(
                jnp.bfloat16
            )
            for g in range(group)
        ]
        found = jnp.dot(jnp.concatenate(picks, axis=0), table[...], preferred_element_type=jnp.float32)
        for g in range(group):
            held[step % 2, k + g] = centre[rows, :] + halves_sum(found[g * tile : (g + 1) * tile])

    def rise(y):
        grown = 1.0 + jnp.exp2(jnp.minimum(y, 64.0))
        return 0.2 * y + jnp.maximum(0.8 * y, (0.8 * LOG2E) * jnp.log(grown)), grown

    def activate(b):
        mine = (step + 1) % 2
        rows = pl.ds(b * block, block)
        top = held[mine, 0, rows, :]
        for k in range(1, slots):
            top = jnp.maximum(top, held[mine, k, rows, :])
        peak, _ = rise(top)
        mass = slope = moment = total = jnp.zeros((block, width), jnp.float32)
        for k in range(slots):
            y = held[mine, k, rows, :]
            level, grown = rise(y)
            share = jnp.exp2(level - peak)
            part = share * (1.0 - 0.8 * pltpu.reciprocal(grown))
            weight_ref[k, rows, :] = part
            mass = mass + share
            slope = slope + part
            moment = moment + part * y
            total = total + y
        out_ref[rows, :] = peak * (1.0 / LOG2E) + jnp.log(mass)
        inv = 1.0 / mass
        inv_ref[rows, :] = inv
        slope_ref[rows, :] = slope * inv
        moment_ref[rows, :] = moment * inv * (1.0 / LOG2E)
        ysum_ref[rows, :] = total * (1.0 / LOG2E)

    blocks = tile // block

    @pl.when(step == 0)
    def _():
        for k in range(0, slots, group):
            gather(k)

    @pl.when((step > 0) & (step < tiles))
    def _():
        done = 0
        for k in range(0, slots, group):
            goal = (k + group) * blocks // slots
            while done < goal:
                activate(done)
                done += 1
            gather(k)

    @pl.when(step == tiles)
    def _():
        for b in range(blocks):
            activate(b)


def edge_forward(edges, slots, first, group, tile, x, a, b, stat, gain, shift):
    points, width = a.shape
    before = pl.BlockSpec((tile, width), lambda step: (jnp.maximum(step - 1, 0), 0))
    return pl.pallas_call(
        functools.partial(edge_kernel, edges, slots, first, group, tile),
        grid=(points // tile + 1,),
        in_specs=[whole(v.shape) for v in (x, a, b, stat, gain, shift)],
        out_specs=[
            before,
            pl.BlockSpec((slots, tile, width), lambda step: (0, jnp.maximum(step - 1, 0), 0)),
        ]
        + [before] * 4,
        out_shape=[f32(points, width), f32(slots, points, width)] + [f32(points, width)] * 4,
        scratch_shapes=[
            pltpu.VMEM((2, slots, tile, width), jnp.float32),
            pltpu.VMEM((points, 2 * width), jnp.bfloat16),
            pltpu.VMEM((points, width), jnp.float32),
        ],
        compiler_params=params(40),
        name="edges",
    )(x, a, b, stat, gain, shift)


def pool_kernel(me_ref, out_ref, inv_ref, slope_ref, moment_ref, gmax_ref, gmean_ref, *refs):
    count = (len(refs) - 2) // 2
    acts, parts = refs[:count], refs[count : 2 * count]
    scaled_ref, own_ref = refs[2 * count :]
    me = me_ref[0]
    points, width = out_ref.shape
    rows = points // count
    out = out_ref[...]
    top = jnp.max(out, axis=0, keepdims=True)
    pool = top + jnp.log(column_sum(jnp.exp(out - top)))
    mean = column_sum(out) / points
    to_max = gmax_ref[pl.ds(me, 1), :]
    to_mean = gmean_ref[pl.ds(me, 1), :] / points
    own_sum = moment_sum = jnp.zeros((1, width), jnp.float32)
    for m in range(count):
        here = slice(m * rows, (m + 1) * rows)
        part = out[here]
        parts[m][0:rows, :] = part
        parts[m][rows : rows + 1, :] = pool
        parts[m][rows + 1 : rows + 2, :] = mean
        parts[m][rows + 4 : rows + 8, :] = jnp.zeros((4, width), jnp.float32)
        grad = acts[m][...] + to_max * jnp.exp(part - pool) + to_mean
        own = grad * slope_ref[here, :]
        scaled_ref[here, :] = grad * inv_ref[here, :]
        own_ref[here, :] = own
        own_sum = own_sum + column_sum(own)
        moment_sum = moment_sum + column_sum(grad * moment_ref[here, :])
    for m in range(count):
        parts[m][rows + 2 : rows + 3, :] = own_sum
        parts[m][rows + 3 : rows + 4, :] = moment_sum


def pools(me, out, inv, slope, moment, grad_max, grad_mean, acts):
    points, width = out.shape
    count = len(acts)
    rows = points // count
    results = pl.pallas_call(
        pool_kernel,
        in_specs=[SMEM] + [pl.BlockSpec(memory_space=pltpu.VMEM)] * (6 + count),
        out_shape=[f32(rows + 8, width)] * count + [f32(points, width)] * 2,
        compiler_params=params(40),
        name="pools",
    )(me, out, inv, slope, moment, grad_max, grad_mean, *acts)
    return results[:count], results[count], results[count + 1]


def scatter_kernel(first, group, ids_ref, grad_ref, weight_ref, sum_ref):
    step = pl.program_id(0)
    points = grad_ref.shape[0]
    rows = lax.broadcasted_iota(jnp.int32, (points, points), 0).astype(jnp.float32)
    picks, terms = [], []
    for g in range(group):
        ids = ids_ref[pl.ds(first + step * group + g, 1), :]
        picks.append(jnp.where(ids == rows, 1.0, 0.0).astype(jnp.bfloat16))
        terms.append(two_terms(grad_ref[...] * weight_ref[g]))
    found = halves_sum(
        jnp.dot(
            jnp.concatenate(picks, axis=1),
            jnp.concatenate(terms, axis=0),
            preferred_element_type=jnp.float32,
        )
    )

    @pl.when(step == 0)
    def _():
        sum_ref[...] = found

    @pl.when(step > 0)
    def _():
        sum_ref[...] += found


def scatter(ids, first, grad, weight, start, stop, group):
    points, width = grad.shape
    edges = (stop - start) * points
    return pl.pallas_call(
        functools.partial(scatter_kernel, first + start, group),
        grid=((stop - start) // group,),
        in_specs=[
            whole(ids.shape),
            whole(grad.shape),
            pl.BlockSpec((group, points, width), lambda step: (start // group + step, 0, 0)),
        ],
        out_specs=whole((points, width)),
        out_shape=f32(points, width),
        compiler_params=params(48),
        cost_estimate=pl.CostEstimate(
            flops=4 * edges * points * width, bytes_accessed=4 * edges * width, transcendentals=0
        ),
        name="scatter",
    )(ids, grad, weight)


def point_grads(edges, slots, own, inward_grads, ysum, inward, degree, local, stat, sums, gain, shift):
    spread = lax.rsqrt(stat[1:2, :] / edges + norm_eps)
    scale = gain * spread
    own_all = sums[0:1, :]
    gain_all = (sums[1:2, :] - shift * own_all) / gain
    shift_part = own_all / edges
    gain_part = gain_all / edges
    leave = scale * (own - slots * shift_part - gain_part * ((ysum - slots * shift) / gain))
    normed = spread * (inward + degree * (local[0:1, :] - stat[0:1, :]))
    reach = scale * (inward_grads - degree * shift_part - gain_part * normed)
    return leave, reach, gain_all


def turned(weight):
    width = weight.shape[0] // 2
    return jnp.concatenate([weight[:width] - weight[width:], weight[width:]], axis=1)


def lanes_product(x, y):
    return lax.dot_general(
        x, y, (((1,), (1,)), ((), ())), precision=HIGHEST, preferred_element_type=jnp.float32
    )


def rows_product(x, y):
    return lax.dot_general(
        x, y, (((0,), (0,)), ((), ())), precision=HIGHEST, preferred_element_type=jnp.float32
    )


def total_of(refs):
    total = refs[0][...]
    for ref in refs[1:]:
        total = total + ref[...]
    return total


def middle_kernel(
    edges, slots, count, me_ref, own_ref, ysum_ref, in_ref, deg_ref, local_ref, stat_ref, sums_ref,
    gain_ref, shift_ref, x_ref, weight_ref, inv_ref, slope_ref, moment_ref, *refs,
):
    wgrad = refs[-1]
    scaled_ref, next_ref, gain_out_ref = refs[-4:-1]
    reached, parts = refs[: -4 - count], refs[-4 - count : -4]
    leave, reach, gain_all = point_grads(
        edges, slots, own_ref[...], total_of(reached), ysum_ref[...], in_ref[...], deg_ref[:, 0:1],
        local_ref[...], stat_ref[...], sums_ref[...], gain_ref[...], shift_ref[...],
    )
    gain_out_ref[...] = gain_all
    width, outs = x_ref.shape[1], leave.shape[1]
    both = rows_product(x_ref[...], jnp.concatenate([leave, reach - leave], axis=1))
    wgrad[0:width, :] = both[:, :outs]
    wgrad[width:, :] = both[:, outs:]
    grad = lanes_product(jnp.concatenate([leave, reach], axis=1), turned(weight_ref[...]))
    own = grad * slope_ref[...]
    scaled_ref[...] = grad * inv_ref[...]
    next_ref[...] = own
    own_sum = column_sum(own)
    moment_sum = column_sum(grad * moment_ref[...])
    me = me_ref[0]
    piece = 2 * width // count
    for mask, part in enumerate(parts):
        start = pl.multiple_of((me ^ mask) * piece, piece)
        part[0:piece, :] = wgrad[pl.ds(start, piece), :]
        part[piece:, :] = jnp.zeros((8, outs), jnp.float32)
        part[piece : piece + 1, 0:width] = own_sum
        part[piece + 1 : piece + 2, 0:width] = moment_sum


def middle(
    edges, slots, count, me, own, ysum, inward, degree, local, stat, sums, gain, shift, x, weight,
    inv, slope, moment, reached,
):
    points, width = x.shape
    outs = weight.shape[1]
    operands = (own, ysum, inward, degree, local, stat, sums, gain, shift, x, weight, inv, slope, moment)
    results = pl.pallas_call(
        functools.partial(middle_kernel, edges, slots, count),
        in_specs=[SMEM] + [pl.BlockSpec(memory_space=pltpu.VMEM)] * (len(operands) + len(reached)),
        out_shape=[f32(2 * width // count + 8, outs)] * count
        + [f32(points, width), f32(points, width), f32(1, outs)],
        scratch_shapes=[pltpu.VMEM((2 * width, outs), jnp.float32)],
        compiler_params=params(48),
        name="middle",
    )(me, *operands, *reached)
    return results[:count], *results[count:]


def last_kernel(
    edges, slots, count, own_ref, ysum_ref, in_ref, deg_ref, local_ref, stat_ref, joined_ref,
    gain_ref, shift_ref, x_ref, weight_ref, *refs,
):
    reached, gain_out_ref, parts = refs[: -1 - count], refs[-1 - count], refs[-count:]
    width, outs = weight_ref.shape[0] // 2, weight_ref.shape[1]
    piece = joined_ref.shape[0] - 8
    leave, reach, gain_all = point_grads(
        edges, slots, own_ref[...], total_of(reached), ysum_ref[...], in_ref[...], deg_ref[:, 0:1],
        local_ref[...], stat_ref[...], joined_ref[piece : piece + 2, 0:outs], gain_ref[...],
        shift_ref[...],
    )
    gain_out_ref[...] = gain_all
    wgrad = rows_product(x_ref[:, 0:width], jnp.concatenate([leave, reach - leave], axis=1))
    grad = lanes_product(turned(weight_ref[...]), jnp.concatenate([leave, reach], axis=1))
    rows = grad.shape[1] // count
    for m, part in enumerate(parts):
        part[0:width, :] = grad[:, m * rows : (m + 1) * rows]
        part[width : 2 * width, :] = wgrad
        part[2 * width :, :] = joined_ref[0:piece, :]


def last(
    edges, slots, count, own, ysum, inward, degree, local, stat, joined, gain, shift, x, weight, reached
):
    points = x.shape[0]
    width, outs = weight.shape[0] // 2, weight.shape[1]
    lanes = points // count
    assert lanes == 2 * outs == joined.shape[1]
    results = pl.pallas_call(
        functools.partial(last_kernel, edges, slots, count),
        out_shape=[f32(1, outs)] + [f32(2 * width + joined.shape[0] - 8, lanes)] * count,
        compiler_params=params(48),
        name="last",
    )(own, ysum, inward, degree, local, stat, joined, gain, shift, x, weight, *reached)
    return results[0], results[1:]


def body(
    features,
    neighbours_one,
    neighbours_two,
    weight_one,
    gain_one,
    shift_one,
    weight_two,
    gain_two,
    shift_two,
    grad_act,
    grad_max,
    grad_mean,
):
    clouds, rows, width = features.shape
    slots = neighbours_one.shape[1]
    count = lax.axis_size("pts")
    assert clouds == count
    points = rows * count
    local_edges = points * slots
    edges = float(local_edges * lax.axis_size(BOTH))
    me = lax.axis_index("pts").astype(jnp.int32).reshape(1)
    gain_one, shift_one, gain_two, shift_two = (
        v.reshape(1, -1) for v in (gain_one, shift_one, gain_two, shift_two)
    )

    def to_owner(parts):
        return [parts[0]] + [exchange(part, "pts", m) for m, part in enumerate(parts) if m]

    with jax.named_scope("bring_clouds"):
        parts = to_owner(pack(me, features, neighbours_one, neighbours_two))
    with jax.named_scope("bring_cotangents"):
        acts = to_owner(split(me, grad_act))

    with jax.named_scope("layer_one"):
        x, ids, a_one, b_one, in_one, deg_one, local_one = first_tables(parts, weight_one, slots)
        links = count_second_links(ids, slots, slots)
        stat_one = join_stats(local_one, local_edges)
        hidden, share_one, inv_one, slope_one, moment_one, ysum_one = edge_forward(
            edges, slots, width, 2, 128, x, a_one, b_one, stat_one, gain_one, shift_one
        )
    with jax.named_scope("layer_two"):
        a_two, b_two, in_two, deg_two, local_two = second_tables(hidden, weight_two, links, slots)
        stat_two = join_stats(local_two, local_edges)
        out, share_two, inv_two, slope_two, moment_two, ysum_two = edge_forward(
            edges, slots, width + slots, 4, 64, x, a_two, b_two, stat_two, gain_two, shift_two
        )
    with jax.named_scope("pools"):
        out_parts, scaled_two, own_two = pools(
            me, out, inv_two, slope_two, moment_two, grad_max, grad_mean, acts
        )
        out_parts = to_owner(out_parts)
        output, pool_max, pool_mean = unpack_output(me, out_parts)

    cuts = ((0, 8), (8, 16), (16, 20))
    with jax.named_scope("layer_two_back"):
        sums_two = sum_over_clouds(pair_sum([part[rows + 2 : rows + 4] for part in out_parts]))
        reached = [scatter(ids, slots, scaled_two, share_two, lo, hi, 4) for lo, hi in cuts]
        wgrad_parts, scaled_one, own_one, gain_grad_two = middle(
            edges, slots, count, me, own_two, ysum_two, in_two, deg_two, local_two, stat_two, sums_two,
            gain_two, shift_two, hidden, weight_two, inv_one, slope_one, moment_one, reached,
        )
    with jax.named_scope("layer_one_back"):
        joined = sum_over_clouds(pair_sum(to_owner(wgrad_parts)))
        reached = [scatter(ids, 0, scaled_one, share_one, lo, hi, 4) for lo, hi in cuts]
        gain_grad_one, grad_parts = last(
            edges, slots, count, own_one, ysum_one, in_one, deg_one, local_one, stat_one, joined,
            gain_one, shift_one, x, weight_one, reached,
        )
        grad_parts = to_owner(grad_parts)
        wgrad_one = sum_over_clouds(pair_sum([part[width : 2 * width] for part in grad_parts]))
        wgrad_one = jnp.concatenate(jnp.split(wgrad_one, 2, axis=1), axis=0)
        grad_features, wgrad_two = unpack_grad(me, grad_parts, width)
    return (
        output,
        pool_max,
        pool_mean,
        jnp.swapaxes(grad_features, 1, 2),
        wgrad_one,
        gain_grad_one.reshape(-1),
        joined[-8, : weight_one.shape[1]],
        wgrad_two,
        gain_grad_two.reshape(-1),
        sums_two[0],
    )


def solution(mesh):
    placed = (
        P("clouds", "pts", None),
        P("clouds", None, "pts"),
        P("clouds", None, "pts"),
        P(),
        P(),
        P(),
        P(),
        P(),
        P(),
        P("clouds", "pts", None),
        P("clouds", None),
        P("clouds", None),
    )
    return jax.shard_map(
        body,
        mesh=mesh,
        in_specs=placed,
        out_specs=(
            P("clouds", "pts", None),
            P("clouds", None),
            P("clouds", None),
            P("clouds", "pts", None),
            P(),
            P(),
            P(),
            P(),
            P(),
            P(),
        ),
        check_vma=False,
    )
```

```python
import functools

import jax
import jax.numpy as jnp
from jax import lax
from jax.experimental import pallas as pl
from jax.experimental.pallas import tpu as pltpu
from jax.sharding import PartitionSpec as P

norm_eps = 1e-05
LOG2E = 1.4426950408889634
HIGHEST = lax.Precision.HIGHEST
BOTH = ("clouds", "pts")
MIB = 2**20


def f32(*shape):
    return jax.ShapeDtypeStruct(shape, jnp.float32)


def in_hbm(*shape):
    return pltpu.HBM(shape, jnp.float32)


def from_hbm(x):
    return pltpu.with_memory_space_constraint(x, pltpu.HBM)


def params(mib):
    return pltpu.CompilerParams(vmem_limit_bytes=mib * MIB)


def whole(shape):
    return pl.BlockSpec(shape, lambda *step: (0,) * len(shape))


SMEM = pl.BlockSpec(memory_space=pltpu.SMEM)


def exchange(x, axes, mask):
    size = lax.axis_size(axes)
    return lax.ppermute(x, axes, [(i, i ^ mask) for i in range(size)])


def bit_groups(size):
    bits = [1 << i for i in range(size.bit_length() - 1)]
    groups = [bits[:1]] if bits else []
    rest = bits[1:]
    while rest:
        groups.append(rest[:2])
        rest = rest[2:]
    return groups


def stages():
    yield "pts", list(range(1, lax.axis_size("pts")))
    for bits in bit_groups(lax.axis_size("clouds")):
        masks = [0]
        for bit in bits:
            masks = masks + [mask | bit for mask in masks]
        yield "clouds", masks[1:]


def swap(x, axes, masks):
    return [x] + [exchange(x, axes, mask) for mask in masks]


def pair_sum(values):
    while len(values) > 1:
        values = [values[i] + values[i + 1] for i in range(0, len(values), 2)]
    return values[0]


def sum_over_clouds(x):
    for axis, masks in list(stages())[1:]:
        x = pair_sum(swap(x, axis, masks))
    return x


def join_stats(stat, count):
    for axis, masks in stages():
        parts = swap(stat, axis, masks)
        mean = pair_sum([part[0:1] for part in parts]) / len(parts)
        away = pair_sum([(part[0:1] - mean) ** 2 for part in parts])
        stat = jnp.concatenate([mean, pair_sum([part[1:2] for part in parts]) + count * away], axis=0)
        count = count * len(parts)
    return stat


def pack_kernel(slots, me_ref, *refs):
    sources, outs, fetched, sems = refs[:9], refs[9:-10], refs[-10:-1], refs[-1]
    parts, small_ref, weights = outs[:-3], outs[-3], outs[-2:]
    copies = [
        pltpu.make_async_copy(source, target, sems.at[i])
        for i, (source, target) in enumerate(zip(sources, fetched))
    ]
    for copy in copies:
        copy.start()
    for copy in copies:
        copy.wait()
    feat_ref, one_ref, two_ref = fetched[:3]
    me = me_ref[0]
    width, rows = feat_ref.shape[1], feat_ref.shape[2]
    for mask, out in enumerate(parts):
        cloud = me ^ mask
        out[0:width, :] = feat_ref[cloud]
        for k in range(slots):
            for at, ids in ((width, one_ref), (width + slots, two_ref)):
                row = ids[k, pl.ds(cloud, 1), :] ^ (cloud * rows)
                out[at + k : at + k + 1, :] = row.astype(jnp.float32)
    small_ref[...] = jnp.zeros_like(small_ref)
    for i, vector in enumerate(fetched[3:7]):
        small_ref[i : i + 1, 0 : vector.shape[1]] = vector[...]
    for kept, weight in zip(weights, fetched[7:9]):
        kept[...] = weight[...]


def pack(me, features, neighbours_one, neighbours_two, vectors, weights):
    clouds, rows, width = features.shape
    slots = neighbours_one.shape[1]
    operands = (
        jnp.swapaxes(features, 1, 2),
        jnp.swapaxes(neighbours_one, 0, 1),
        jnp.swapaxes(neighbours_two, 0, 1),
        *(v.reshape(1, -1) for v in vectors),
        *weights,
    )
    results = pl.pallas_call(
        functools.partial(pack_kernel, slots),
        in_specs=[SMEM] + [pl.BlockSpec(memory_space=pltpu.HBM)] * len(operands),
        out_shape=[f32(width + 2 * slots, rows)] * clouds
        + [f32(8, max(v.shape[0] for v in vectors))]
        + [f32(*w.shape) for w in weights],
        scratch_shapes=[pltpu.VMEM(v.shape, v.dtype) for v in operands]
        + [pltpu.SemaphoreType.DMA((len(operands),))],
        compiler_params=params(8),
        name="pack",
    )(me, *(from_hbm(v) for v in operands))
    return results[:clouds], results[clouds], results[clouds + 1 :]


def split_kernel(me_ref, x_ref, *outs):
    me = me_ref[0]
    for mask, out in enumerate(outs):
        out[...] = x_ref[me ^ mask]


def split(me, x):
    clouds, rows, width = x.shape
    return pl.pallas_call(
        split_kernel,
        in_specs=[SMEM, pl.BlockSpec(memory_space=pltpu.VMEM)],
        out_shape=[f32(rows, width)] * clouds,
        compiler_params=params(16),
        name="split",
    )(me, from_hbm(x))


def unpack_output_kernel(rows, me_ref, *refs):
    parts, (act_ref, max_ref, mean_ref) = refs[:-3], refs[-3:]
    me = me_ref[0]
    for mask, part in enumerate(parts):
        cloud = me ^ mask
        act_ref[cloud] = part[0:rows]
        max_ref[pl.ds(cloud, 1), :] = part[rows : rows + 1]
        mean_ref[pl.ds(cloud, 1), :] = part[rows + 1 : rows + 2]


def unpack_output(me, parts):
    clouds, width = len(parts), parts[0].shape[1]
    rows = parts[0].shape[0] - 8
    return pl.pallas_call(
        functools.partial(unpack_output_kernel, rows),
        in_specs=[SMEM] + [pl.BlockSpec(memory_space=pltpu.VMEM)] * clouds,
        out_shape=[f32(clouds, rows, width), f32(clouds, width), f32(clouds, width)],
        compiler_params=params(16),
        name="unpack_output",
    )(me, *parts)


def unpack_grad_kernel(me_ref, *refs):
    parts, (grad_ref, wgrad_ref) = refs[:-2], refs[-2:]
    me = me_ref[0]
    width = grad_ref.shape[1]
    piece = wgrad_ref.shape[0] // len(parts)
    for mask, part in enumerate(parts):
        other = me ^ mask
        grad_ref[other] = part[0:width]
        wgrad_ref[pl.ds(pl.multiple_of(other * piece, piece), piece), :] = part[width:]


def unpack_grad(me, parts, width):
    rows, lanes = parts[0].shape
    count = len(parts)
    return pl.pallas_call(
        unpack_grad_kernel,
        in_specs=[SMEM] + [pl.BlockSpec(memory_space=pltpu.VMEM)] * count,
        out_shape=[f32(count, width, lanes), f32(count * (rows - width), lanes)],
        compiler_params=params(16),
        name="unpack_grad",
    )(me, *parts)


def two_terms(x):
    high = x.astype(jnp.bfloat16)
    low = (x - high.astype(jnp.float32)).astype(jnp.bfloat16)
    return jnp.concatenate([high, low], axis=1)


def halves_sum(x):
    half = x.shape[1] // 2
    return x[:, :half] + x[:, half:]


def column_sum(x):
    return jnp.sum(x, axis=0, keepdims=True)


def count_links(ids_ref, first, slots, wide, links):
    points = links.shape[0]
    block = 256
    lane_ids = lax.broadcasted_iota(jnp.int32, (16, points), 0).astype(jnp.bfloat16)
    one = jnp.ones((16, points), jnp.bfloat16)
    zero = jnp.zeros((16, points), jnp.bfloat16)
    for start in range(0, points, block):
        for k in range(slots):
            local = ids_ref[first + k : first + k + 1, :] - float(start)
            local = jnp.where((local >= 0) & (local < block), local, -1.0)
            wide[k] = jnp.broadcast_to(local, (16, points)).astype(jnp.bfloat16)

        def sixteen(step, carry):
            here = lane_ids + (step * 16).astype(jnp.float32).astype(jnp.bfloat16)
            total = zero
            for k in range(slots):
                total = total + jnp.where(wide[k] == here, one, zero)
            links[pl.ds(pl.multiple_of(start + step * 16, 16), 16), :] = total
            return carry

        lax.fori_loop(0, block // 16, sixteen, 0)


def table_stats(x, weight, links, slots, a_ref, b_ref, in_ref, deg_ref, stat_ref):
    points, width = x.shape
    outs = weight.shape[1]
    upper, lower = weight[:width], weight[width:]
    both = jnp.dot(x, jnp.concatenate([upper - lower, lower], axis=1), precision=HIGHEST)
    a, b = both[:, :outs], both[:, outs:]
    mean_a = column_sum(a) / points
    a_off = a - mean_a
    seen = halves_sum(jnp.dot(links, two_terms(a_off), preferred_element_type=jnp.float32))
    degree = jnp.sum(links.astype(jnp.float32), axis=1, keepdims=True)
    mean_b = column_sum(degree * b) / (points * slots)
    b_off = b - mean_b
    inward = seen + degree * b_off
    a_ref[...] = a
    b_ref[...] = b
    in_ref[...] = inward
    deg_ref[...] = jnp.broadcast_to(degree, deg_ref.shape)
    stat_ref[0:1, :] = mean_a + mean_b
    stat_ref[1:2, :] = slots * column_sum(a_off * a_off) + column_sum((seen + inward) * b_off)


def first_kernel(slots, width, *refs):
    parts, (weight_ref, x_ref, ids_ref, a_ref, b_ref, in_ref, deg_ref, stat_ref, links, wide) = (
        refs[:-10],
        refs[-10:],
    )
    rows = parts[0].shape[1]
    fill = jnp.zeros((128 - parts[0].shape[0], rows), jnp.float32)
    for m, part in enumerate(parts):
        ids_ref[:, m * rows : (m + 1) * rows] = part[width:, :]
        x_ref[m * rows : (m + 1) * rows, :] = jnp.concatenate([part[...], fill], axis=0).T
    count_links(ids_ref, 0, slots, wide, links)
    table_stats(
        x_ref[:, :width], weight_ref[...], links[...], slots, a_ref, b_ref, in_ref, deg_ref, stat_ref
    )


def first_tables(parts, weight, slots):
    points = len(parts) * parts[0].shape[1]
    width, outs = weight.shape[0] // 2, weight.shape[1]
    return pl.pallas_call(
        functools.partial(first_kernel, slots, width),
        out_shape=[
            f32(points, 128),
            f32(2 * slots, points),
            f32(points, outs),
            f32(points, outs),
            f32(points, outs),
            f32(points, 128),
            f32(2, outs),
        ],
        scratch_shapes=[
            pltpu.VMEM((points, points), jnp.bfloat16),
            pltpu.VMEM((slots, 16, points), jnp.bfloat16),
        ],
        compiler_params=params(24),
        name="first_tables",
    )(*parts, weight)


def links_kernel(first, slots, ids_ref, links, wide):
    count_links(ids_ref, first, slots, wide, links)


def count_second_links(ids, first, slots):
    points = ids.shape[1]
    return pl.pallas_call(
        functools.partial(links_kernel, first, slots),
        out_shape=jax.ShapeDtypeStruct((points, points), jnp.bfloat16),
        scratch_shapes=[pltpu.VMEM((slots, 16, points), jnp.bfloat16)],
        compiler_params=params(12),
        cost_estimate=pl.CostEstimate(flops=10**9, bytes_accessed=16 * MIB, transcendentals=0),
        name="links_two",
    )(ids)


def second_kernel(slots, x_ref, weight_ref, links, a_ref, b_ref, in_ref, deg_ref, stat_ref):
    table_stats(
        x_ref[...], weight_ref[...], links[...], slots, a_ref, b_ref, in_ref, deg_ref, stat_ref
    )


def second_tables(x, weight, links, slots):
    points, outs = x.shape[0], weight.shape[1]
    return pl.pallas_call(
        functools.partial(second_kernel, slots),
        out_shape=[
            f32(points, outs),
            f32(points, outs),
            f32(points, outs),
            f32(points, 128),
            f32(2, outs),
        ],
        compiler_params=params(24),
        name="second_tables",
    )(x, weight, links)


def edge_kernel(
    edges, layer, slots, first, tile, x_ref, a_ref, b_ref, stat_ref, small_ref,
    out_ref, weight_ref, inv_ref, slope_ref, moment_ref, ysum_ref, table, centre, sums, held, bounded,
):
    points, width = a_ref.shape
    step = pl.program_id(0)
    block = 8

    @pl.when(step == 0)
    def _():
        gain = small_ref[2 * layer : 2 * layer + 1, 0:width]
        shift = small_ref[2 * layer + 1 : 2 * layer + 2, 0:width]
        scale = gain * lax.rsqrt(stat_ref[1:2, :] / edges + norm_eps) * -LOG2E
        middle = column_sum(b_ref[...]) / points
        there = (b_ref[...] - middle) * scale
        here = (a_ref[...] + (middle - stat_ref[0:1, :])) * scale - shift * LOG2E
        table[...] = two_terms(there)
        centre[...] = here
        reach = jnp.max(jnp.abs(here), axis=0, keepdims=True) + jnp.max(
            jnp.abs(there), axis=0, keepdims=True
        )
        bounded[0] = (jnp.max(reach) < 60.0).astype(jnp.int32)

    rows = pl.ds(pl.multiple_of(step * tile, tile), tile)
    columns = lax.broadcasted_iota(jnp.int32, (tile, points), 1).astype(jnp.float32)

    def gather(ids):
        pick = jnp.where(ids == columns, 1.0, 0.0).astype(jnp.bfloat16)
        return jnp.dot(pick, table[...], preferred_element_type=jnp.float32)

    def finish(at, top, totals):
        mass, slope, moment, total = totals
        out_ref[at, :] = top + jnp.log(mass)
        inv = 0.8 / mass
        inv_ref[at, :] = inv
        slope_ref[at, :] = slope * inv
        moment_ref[at, :] = moment * inv * (-1.0 / LOG2E)
        ysum_ref[at, :] = total * (-1.0 / LOG2E)

    @pl.when(bounded[0] == 1)
    def _():
        for k in range(slots):
            found = gather(x_ref[rows, first + k : first + k + 1])
            for start in range(0, tile, block):
                at = slice(start, start + block)
                here = pl.ds(pl.multiple_of(step * tile + start, block), block)
                t = centre[here, :] + halves_sum(found[at])
                grown = 1.0 + jnp.exp2(t)
                fall = jnp.exp2((-0.2 * LOG2E) * jnp.log(grown) - t)
                share = grown * fall
                part = fall + 0.25 * share
                weight_ref[k, at, :] = part
                terms = (share, part, part * t, t)
                if k:
                    terms = [sums[i, at, :] + term for i, term in enumerate(terms)]
                if k < slots - 1:
                    for i, term in enumerate(terms):
                        sums[i, at, :] = term
                else:
                    finish(at, 0.0, terms)

    @pl.when(bounded[0] == 0)
    def _():
        lanes = lax.broadcasted_iota(jnp.int32, (tile, x_ref.shape[1]), 1)

        def collect(k, carry):
            ids = jnp.sum(jnp.where(lanes == first + k, x_ref[rows, :], 0.0), axis=1, keepdims=True)
            held[k] = centre[rows, :] + halves_sum(gather(ids))
            return carry

        lax.fori_loop(0, slots, collect, 0)

        def rise(t):
            grown = 1.0 + jnp.exp2(jnp.minimum(t, 64.0))
            return jnp.maximum((0.8 * LOG2E) * jnp.log(grown), 0.8 * t) - t, grown

        def some(b, carry):
            at = pl.ds(pl.multiple_of(b * block, block), block)
            low = held[0, at, :]
            for k in range(1, slots):
                low = jnp.minimum(low, held[k, at, :])
            peak, _ = rise(low)
            totals = [jnp.zeros((block, width), jnp.float32)] * 4
            for k in range(slots):
                t = held[k, at, :]
                level, grown = rise(t)
                share = jnp.exp2(level - peak)
                part = share * (1.0 / grown + 0.25)
                weight_ref[k, at, :] = part
                totals = [total + term for total, term in zip(totals, (share, part, part * t, t))]
            finish(at, peak * (1.0 / LOG2E), totals)
            return carry

        lax.fori_loop(0, tile // block, some, 0)


def edge_forward(edges, layer, slots, first, tile, x, a, b, stat, small):
    points, width = a.shape
    some = pl.BlockSpec((tile, width), lambda step: (step, 0))
    return pl.pallas_call(
        functools.partial(edge_kernel, edges, layer, slots, first, tile),
        grid=(points // tile,),
        in_specs=[whole(v.shape) for v in (x, a, b, stat, small)],
        out_specs=[some, pl.BlockSpec((slots, tile, width), lambda step: (0, step, 0))] + [some] * 4,
        out_shape=[f32(points, width), in_hbm(slots, points, width)] + [f32(points, width)] * 4,
        scratch_shapes=[
            pltpu.VMEM((points, 2 * width), jnp.bfloat16),
            pltpu.VMEM((points, width), jnp.float32),
            pltpu.VMEM((4, tile, width), jnp.float32),
            pltpu.VMEM((slots, tile, width), jnp.float32),
            pltpu.SMEM((1,), jnp.int32),
        ],
        compiler_params=params(24),
        name="edges",
    )(x, a, b, stat, small)


def pool_kernel(me_ref, out_ref, inv_ref, slope_ref, moment_ref, gmax_ref, gmean_ref, *refs):
    count = (len(refs) - 2) // 2
    acts, parts = refs[:count], refs[count : 2 * count]
    scaled_ref, own_ref = refs[2 * count :]
    me = me_ref[0]
    points, width = out_ref.shape
    rows = points // count
    out = out_ref[...]
    top = jnp.max(out, axis=0, keepdims=True)
    pool = top + jnp.log(column_sum(jnp.exp(out - top)))
    mean = column_sum(out) / points
    to_max = gmax_ref[pl.ds(me, 1), :]
    to_mean = gmean_ref[pl.ds(me, 1), :] / points
    own_sum = moment_sum = jnp.zeros((1, width), jnp.float32)
    for m in range(count):
        here = slice(m * rows, (m + 1) * rows)
        part = out[here]
        parts[m][0:rows, :] = part
        parts[m][rows : rows + 1, :] = pool
        parts[m][rows + 1 : rows + 2, :] = mean
        parts[m][rows + 4 : rows + 8, :] = jnp.zeros((4, width), jnp.float32)
        grad = acts[m][...] + to_max * jnp.exp(part - pool) + to_mean
        own = grad * slope_ref[here, :]
        scaled_ref[here, :] = grad * inv_ref[here, :]
        own_ref[here, :] = own
        own_sum = own_sum + column_sum(own)
        moment_sum = moment_sum + column_sum(grad * moment_ref[here, :])
    for m in range(count):
        parts[m][rows + 2 : rows + 3, :] = own_sum
        parts[m][rows + 3 : rows + 4, :] = moment_sum


def pools(me, out, inv, slope, moment, grad_max, grad_mean, acts):
    points, width = out.shape
    count = len(acts)
    rows = points // count
    results = pl.pallas_call(
        pool_kernel,
        in_specs=[SMEM] + [pl.BlockSpec(memory_space=pltpu.VMEM)] * (6 + count),
        out_shape=[f32(rows + 8, width)] * count + [f32(points, width)] * 2,
        compiler_params=params(16),
        name="pools",
    )(me, out, inv, slope, moment, grad_max, grad_mean, *acts)
    return results[:count], results[count], results[count + 1]


def scatter_kernel(first, group, ids_ref, grad_ref, weight_ref, sum_ref):
    step = pl.program_id(0)
    points = grad_ref.shape[0]
    rows = lax.broadcasted_iota(jnp.int32, (points, points), 0).astype(jnp.float32)
    picks, terms = [], []
    for g in range(group):
        ids = ids_ref[pl.ds(first + step * group + g, 1), :]
        picks.append(jnp.where(ids == rows, 1.0, 0.0).astype(jnp.bfloat16))
        terms.append(two_terms(grad_ref[...] * weight_ref[g]))
    found = halves_sum(
        jnp.dot(
            jnp.concatenate(picks, axis=1),
            jnp.concatenate(terms, axis=0),
            preferred_element_type=jnp.float32,
        )
    )

    @pl.when(step == 0)
    def _():
        sum_ref[...] = found

    @pl.when(step > 0)
    def _():
        sum_ref[...] += found


def scatter(ids, first, grad, weight, start, stop, group):
    points, width = grad.shape
    edges = (stop - start) * points
    return pl.pallas_call(
        functools.partial(scatter_kernel, first + start, group),
        grid=((stop - start) // group,),
        in_specs=[
            whole(ids.shape),
            whole(grad.shape),
            pl.BlockSpec((group, points, width), lambda step: (start // group + step, 0, 0)),
        ],
        out_specs=whole((points, width)),
        out_shape=f32(points, width),
        compiler_params=params(28),
        cost_estimate=pl.CostEstimate(
            flops=4 * edges * points * width, bytes_accessed=4 * edges * width, transcendentals=0
        ),
        name="scatter",
    )(ids, grad, from_hbm(weight))


def point_grads(edges, slots, own, inward_grads, ysum, inward, degree, local, stat, sums, gain, shift):
    spread = lax.rsqrt(stat[1:2, :] / edges + norm_eps)
    scale = gain * spread
    own_all = sums[0:1, :]
    gain_all = (sums[1:2, :] - shift * own_all) / gain
    shift_part = own_all / edges
    gain_part = gain_all / edges
    leave = scale * (own - slots * shift_part - gain_part * ((ysum - slots * shift) / gain))
    normed = spread * (inward + degree * (local[0:1, :] - stat[0:1, :]))
    reach = scale * (inward_grads - degree * shift_part - gain_part * normed)
    return leave, reach, gain_all


def turned(weight):
    width = weight.shape[0] // 2
    return jnp.concatenate([weight[:width] - weight[width:], weight[width:]], axis=1)


def lanes_product(x, y):
    return lax.dot_general(
        x, y, (((1,), (1,)), ((), ())), precision=HIGHEST, preferred_element_type=jnp.float32
    )


def rows_product(x, y):
    return lax.dot_general(
        x, y, (((0,), (0,)), ((), ())), precision=HIGHEST, preferred_element_type=jnp.float32
    )


def total_of(refs):
    total = refs[0][...]
    for ref in refs[1:]:
        total = total + ref[...]
    return total


def middle_kernel(
    edges, slots, count, me_ref, own_ref, ysum_ref, in_ref, deg_ref, local_ref, stat_ref, sums_ref,
    small_ref, x_ref, weight_ref, inv_ref, slope_ref, moment_ref, *refs,
):
    wgrad = refs[-1]
    scaled_ref, next_ref, gain_out_ref = refs[-4:-1]
    reached, parts = refs[: -4 - count], refs[-4 - count : -4]
    leave, reach, gain_all = point_grads(
        edges, slots, own_ref[...], total_of(reached), ysum_ref[...], in_ref[...], deg_ref[:, 0:1],
        local_ref[...], stat_ref[...], sums_ref[...], small_ref[2:3, :], small_ref[3:4, :],
    )
    gain_out_ref[...] = gain_all
    width, outs = x_ref.shape[1], leave.shape[1]
    both = rows_product(x_ref[...], jnp.concatenate([leave, reach - leave], axis=1))
    wgrad[0:width, :] = both[:, :outs]
    wgrad[width:, :] = both[:, outs:]
    grad = lanes_product(jnp.concatenate([leave, reach], axis=1), turned(weight_ref[...]))
    own = grad * slope_ref[...]
    scaled_ref[...] = grad * inv_ref[...]
    next_ref[...] = own
    own_sum = column_sum(own)
    moment_sum = column_sum(grad * moment_ref[...])
    me = me_ref[0]
    piece = 2 * width // count
    for mask, part in enumerate(parts):
        start = pl.multiple_of((me ^ mask) * piece, piece)
        part[0:piece, :] = wgrad[pl.ds(start, piece), :]
        part[piece:, :] = jnp.zeros((8, outs), jnp.float32)
        part[piece : piece + 1, 0:width] = own_sum
        part[piece + 1 : piece + 2, 0:width] = moment_sum


def middle(
    edges, slots, count, me, own, ysum, inward, degree, local, stat, sums, small, x, weight,
    inv, slope, moment, reached,
):
    points, width = x.shape
    outs = weight.shape[1]
    operands = (own, ysum, inward, degree, local, stat, sums, small, x, weight, inv, slope, moment)
    results = pl.pallas_call(
        functools.partial(middle_kernel, edges, slots, count),
        in_specs=[SMEM] + [pl.BlockSpec(memory_space=pltpu.VMEM)] * (len(operands) + len(reached)),
        out_shape=[f32(2 * width // count + 8, outs)] * count
        + [f32(points, width), f32(points, width), f32(1, outs)],
        scratch_shapes=[pltpu.VMEM((2 * width, outs), jnp.float32)],
        compiler_params=params(32),
        name="middle",
    )(me, *operands, *reached)
    return results[:count], *results[count:]


def last_kernel(
    edges, slots, count, own_ref, ysum_ref, in_ref, deg_ref, local_ref, stat_ref, joined_ref,
    small_ref, x_ref, weight_ref, *refs,
):
    reached, (gain_out_ref, wgrad_ref), parts = (
        refs[: -2 - count],
        refs[-2 - count : -count],
        refs[-count:],
    )
    width, outs = weight_ref.shape[0] // 2, weight_ref.shape[1]
    piece = joined_ref.shape[0] - 8
    leave, reach, gain_all = point_grads(
        edges, slots, own_ref[...], total_of(reached), ysum_ref[...], in_ref[...], deg_ref[:, 0:1],
        local_ref[...], stat_ref[...], joined_ref[piece : piece + 2, 0:outs],
        small_ref[0:1, 0:outs], small_ref[1:2, 0:outs],
    )
    gain_out_ref[...] = gain_all
    wgrad_ref[...] = rows_product(x_ref[:, 0:width], jnp.concatenate([leave, reach - leave], axis=1))
    grad = lanes_product(turned(weight_ref[...]), jnp.concatenate([leave, reach], axis=1))
    rows = grad.shape[1] // count
    for m, part in enumerate(parts):
        part[0:width, :] = grad[:, m * rows : (m + 1) * rows]
        part[width:, :] = joined_ref[0:piece, :]


def last(
    edges, slots, count, own, ysum, inward, degree, local, stat, joined, small, x, weight, reached
):
    points = x.shape[0]
    width, outs = weight.shape[0] // 2, weight.shape[1]
    lanes = points // count
    assert lanes == 2 * outs == joined.shape[1]
    results = pl.pallas_call(
        functools.partial(last_kernel, edges, slots, count),
        out_shape=[f32(1, outs), f32(width, 2 * outs)] + [f32(width + joined.shape[0] - 8, lanes)] * count,
        compiler_params=params(32),
        name="last",
    )(own, ysum, inward, degree, local, stat, joined, small, x, weight, *reached)
    return results[0], results[1], results[2:]


def body(
    features,
    neighbours_one,
    neighbours_two,
    weight_one,
    gain_one,
    shift_one,
    weight_two,
    gain_two,
    shift_two,
    grad_act,
    grad_max,
    grad_mean,
):
    clouds, rows, width = features.shape
    slots = neighbours_one.shape[1]
    count = lax.axis_size("pts")
    assert clouds == count
    points = rows * count
    local_edges = points * slots
    edges = float(local_edges * lax.axis_size(BOTH))
    me = lax.axis_index("pts").astype(jnp.int32).reshape(1)
    def to_owner(parts):
        return [parts[0]] + [exchange(part, "pts", m) for m, part in enumerate(parts) if m]

    with jax.named_scope("bring_clouds"):
        parts, small, (weight_one, weight_two) = pack(
            me, features, neighbours_one, neighbours_two,
            (gain_one, shift_one, gain_two, shift_two), (weight_one, weight_two),
        )
        parts = to_owner(parts)
    with jax.named_scope("bring_cotangents"):
        acts = to_owner(split(me, grad_act))

    with jax.named_scope("layer_one"):
        x, ids, a_one, b_one, in_one, deg_one, local_one = first_tables(parts, weight_one, slots)
        links = count_second_links(ids, slots, slots)
        stat_one = join_stats(local_one, local_edges)
        hidden, share_one, inv_one, slope_one, moment_one, ysum_one = edge_forward(
            edges, 0, slots, width, 128, x, a_one, b_one, stat_one, small
        )
    with jax.named_scope("layer_two"):
        a_two, b_two, in_two, deg_two, local_two = second_tables(hidden, weight_two, links, slots)
        stat_two = join_stats(local_two, local_edges)
        out, share_two, inv_two, slope_two, moment_two, ysum_two = edge_forward(
            edges, 1, slots, width + slots, 128, x, a_two, b_two, stat_two, small
        )
    with jax.named_scope("pools"):
        out_parts, scaled_two, own_two = pools(
            me, out, inv_two, slope_two, moment_two, grad_max, grad_mean, acts
        )
        out_parts = to_owner(out_parts)
        output, pool_max, pool_mean = unpack_output(me, out_parts)

    cuts = ((0, 8), (8, 16), (16, 20))
    with jax.named_scope("layer_two_back"):
        sums_two = sum_over_clouds(pair_sum([part[rows + 2 : rows + 4] for part in out_parts]))
        reached = [scatter(ids, slots, scaled_two, share_two, lo, hi, 4) for lo, hi in cuts]
        wgrad_parts, scaled_one, own_one, gain_grad_two = middle(
            edges, slots, count, me, own_two, ysum_two, in_two, deg_two, local_two, stat_two, sums_two,
            small, hidden, weight_two, inv_one, slope_one, moment_one, reached,
        )
    with jax.named_scope("layer_one_back"):
        joined = sum_over_clouds(pair_sum(to_owner(wgrad_parts)))
        reached = [scatter(ids, 0, scaled_one, share_one, lo, hi, 4) for lo, hi in cuts]
        gain_grad_one, wgrad_one, grad_parts = last(
            edges, slots, count, own_one, ysum_one, in_one, deg_one, local_one, stat_one, joined,
            small, x, weight_one, reached,
        )
        wgrad_one = pair_sum(to_owner([wgrad_one] * count))
        wgrad_one, *grad_parts = lax.optimization_barrier((wgrad_one, *grad_parts))
        grad_parts = to_owner(grad_parts)
        wgrad_one = sum_over_clouds(wgrad_one)
        wgrad_one = jnp.concatenate(jnp.split(wgrad_one, 2, axis=1), axis=0)
        grad_features, wgrad_two = unpack_grad(me, grad_parts, width)
    return (
        output,
        pool_max,
        pool_mean,
        jnp.swapaxes(grad_features, 1, 2),
        wgrad_one,
        gain_grad_one.reshape(-1),
        joined[-8, : weight_one.shape[1]],
        wgrad_two,
        gain_grad_two.reshape(-1),
        sums_two[0],
    )


def solution(mesh):
    placed = (
        P("clouds", "pts", None),
        P("clouds", None, "pts"),
        P("clouds", None, "pts"),
        P(),
        P(),
        P(),
        P(),
        P(),
        P(),
        P("clouds", "pts", None),
        P("clouds", None),
        P("clouds", None),
    )
    return jax.shard_map(
        body,
        mesh=mesh,
        in_specs=placed,
        out_specs=(
            P("clouds", "pts", None),
            P("clouds", None),
            P("clouds", None),
            P("clouds", "pts", None),
            P(),
            P(),
            P(),
            P(),
            P(),
            P(),
        ),
        check_vma=False,
    )
```

```python
import functools

import jax
import jax.numpy as jnp
from jax import lax
from jax.experimental import pallas as pl
from jax.experimental.pallas import tpu as pltpu
from jax.sharding import PartitionSpec as P

norm_eps = 1e-05
LOG2E = 1.4426950408889634
BOTH = ("clouds", "pts")
MIB = 2**20


def f32(*shape):
    return jax.ShapeDtypeStruct(shape, jnp.float32)


def in_hbm(*shape):
    return pltpu.HBM(shape, jnp.float32)


def from_hbm(x):
    return pltpu.with_memory_space_constraint(x, pltpu.HBM)


def params(mib):
    return pltpu.CompilerParams(vmem_limit_bytes=mib * MIB)


def whole(shape):
    return pl.BlockSpec(shape, lambda *step: (0,) * len(shape))


SMEM = pl.BlockSpec(memory_space=pltpu.SMEM)


def exchange(x, axes, mask):
    size = lax.axis_size(axes)
    return lax.ppermute(x, axes, [(i, i ^ mask) for i in range(size)])


def bit_groups(size):
    bits = [1 << i for i in range(size.bit_length() - 1)]
    groups = [bits[:1]] if bits else []
    rest = bits[1:]
    while rest:
        groups.append(rest[:2])
        rest = rest[2:]
    return groups


def stages():
    yield "pts", list(range(1, lax.axis_size("pts")))
    for bits in bit_groups(lax.axis_size("clouds")):
        masks = [0]
        for bit in bits:
            masks = masks + [mask | bit for mask in masks]
        yield "clouds", masks[1:]


def swap(x, axes, masks):
    return [x] + [exchange(x, axes, mask) for mask in masks]


def pair_sum(values):
    while len(values) > 1:
        values = [values[i] + values[i + 1] for i in range(0, len(values), 2)]
    return values[0]


def sum_stages(x, cloud_stages):
    for axis, masks in cloud_stages:
        x = pair_sum(swap(x, axis, masks))
    return x


def after(value, *others):
    return lax.optimization_barrier((value, *others))[0]


def sum_beside(message, received, work):
    (axis, masks), *rest = list(stages())[:0:-1]
    first = work[0](None)
    total = message(lax.optimization_barrier((*received, first))[:-1])
    moving = swap(total, axis, masks)
    second = work[1](total)
    total = pair_sum(list(lax.optimization_barrier((*moving, second))[:-1]))
    return sum_stages(total, rest), [first, second]


def join_stats(stat, count):
    for axis, masks in stages():
        parts = swap(stat, axis, masks)
        mean = pair_sum([part[0:1] for part in parts]) / len(parts)
        away = pair_sum([(part[0:1] - mean) ** 2 for part in parts])
        stat = jnp.concatenate([mean, pair_sum([part[1:2] for part in parts]) + count * away], axis=0)
        count = count * len(parts)
    return stat


def pack_kernel(slots, me_ref, *refs):
    sources, outs, fetched, sems = refs[:9], refs[9:-10], refs[-10:-1], refs[-1]
    parts, small_ref, weights = outs[:-3], outs[-3], outs[-2:]
    copies = [
        pltpu.make_async_copy(source, target, sems.at[i])
        for i, (source, target) in enumerate(zip(sources, fetched))
    ]
    for copy in copies:
        copy.start()
    for copy in copies:
        copy.wait()
    feat_ref, one_ref, two_ref = fetched[:3]
    me = me_ref[0]
    width, rows = feat_ref.shape[1], feat_ref.shape[2]
    for mask, out in enumerate(parts):
        cloud = me ^ mask
        out[0:width, :] = feat_ref[cloud]
        for k in range(slots):
            for at, ids in ((width, one_ref), (width + slots, two_ref)):
                row = ids[k, pl.ds(cloud, 1), :] ^ (cloud * rows)
                out[at + k : at + k + 1, :] = row.astype(jnp.float32)
    small_ref[...] = jnp.zeros_like(small_ref)
    for i, vector in enumerate(fetched[3:7]):
        small_ref[i : i + 1, 0 : vector.shape[1]] = vector[...]
    for kept, weight in zip(weights, fetched[7:9]):
        kept[...] = weight[...]


def pack(me, features, neighbours_one, neighbours_two, vectors, weights):
    clouds, rows, width = features.shape
    slots = neighbours_one.shape[1]
    operands = (
        jnp.swapaxes(features, 1, 2),
        jnp.swapaxes(neighbours_one, 0, 1),
        jnp.swapaxes(neighbours_two, 0, 1),
        *(v.reshape(1, -1) for v in vectors),
        *weights,
    )
    results = pl.pallas_call(
        functools.partial(pack_kernel, slots),
        in_specs=[SMEM] + [pl.BlockSpec(memory_space=pltpu.HBM)] * len(operands),
        out_shape=[f32(width + 2 * slots, rows)] * clouds
        + [f32(8, max(v.shape[0] for v in vectors))]
        + [f32(*w.shape) for w in weights],
        scratch_shapes=[pltpu.VMEM(v.shape, v.dtype) for v in operands]
        + [pltpu.SemaphoreType.DMA((len(operands),))],
        compiler_params=params(8),
        name="pack",
    )(me, *(from_hbm(v) for v in operands))
    return results[:clouds], results[clouds], results[clouds + 1 :]


def split_kernel(me_ref, x_ref, *outs):
    me = me_ref[0]
    for mask, out in enumerate(outs):
        out[...] = x_ref[me ^ mask]


def split(me, x):
    clouds, rows, width = x.shape
    return pl.pallas_call(
        split_kernel,
        in_specs=[SMEM, pl.BlockSpec(memory_space=pltpu.VMEM)],
        out_shape=[f32(rows, width)] * clouds,
        compiler_params=params(16),
        name="split",
    )(me, from_hbm(x))


def unpack_output_kernel(rows, me_ref, *refs):
    parts, (act_ref, max_ref, mean_ref) = refs[:-3], refs[-3:]
    me = me_ref[0]
    for mask, part in enumerate(parts):
        cloud = me ^ mask
        act_ref[cloud] = part[0:rows]
        max_ref[pl.ds(cloud, 1), :] = part[rows : rows + 1]
        mean_ref[pl.ds(cloud, 1), :] = part[rows + 1 : rows + 2]


def unpack_output(me, parts):
    clouds, width = len(parts), parts[0].shape[1]
    rows = parts[0].shape[0] - 8
    return pl.pallas_call(
        functools.partial(unpack_output_kernel, rows),
        in_specs=[SMEM] + [pl.BlockSpec(memory_space=pltpu.VMEM)] * clouds,
        out_shape=[f32(clouds, rows, width), f32(clouds, width), f32(clouds, width)],
        compiler_params=params(16),
        name="unpack_output",
    )(me, *parts)


def unpack_grad_kernel(me_ref, *refs):
    parts, (grad_ref, wgrad_ref) = refs[:-2], refs[-2:]
    me = me_ref[0]
    width = grad_ref.shape[1]
    piece = wgrad_ref.shape[0] // len(parts)
    for mask, part in enumerate(parts):
        other = me ^ mask
        grad_ref[other] = part[0:width]
        wgrad_ref[pl.ds(pl.multiple_of(other * piece, piece), piece), :] = part[width:]


def unpack_grad(me, parts, width):
    rows, lanes = parts[0].shape
    count = len(parts)
    return pl.pallas_call(
        unpack_grad_kernel,
        in_specs=[SMEM] + [pl.BlockSpec(memory_space=pltpu.VMEM)] * count,
        out_shape=[f32(count, width, lanes), f32(count * (rows - width), lanes)],
        compiler_params=params(16),
        name="unpack_grad",
    )(me, *parts)


def two_terms(x):
    high = x.astype(jnp.bfloat16)
    low = (x - high.astype(jnp.float32)).astype(jnp.bfloat16)
    return jnp.concatenate([high, low], axis=1)


def halves_sum(x):
    half = x.shape[1] // 2
    return x[:, :half] + x[:, half:]


def product(x, y, on_x, on_y):
    x_high, y_high = x.astype(jnp.bfloat16), y.astype(jnp.bfloat16)
    x_low = (x - x_high.astype(jnp.float32)).astype(jnp.bfloat16)
    y_low = (y - y_high.astype(jnp.float32)).astype(jnp.bfloat16)
    return lax.dot_general(
        jnp.concatenate([x_high, x_low, x_high], axis=on_x),
        jnp.concatenate([y_high, y_high, y_low], axis=on_y),
        (((on_x,), (on_y,)), ((), ())),
        preferred_element_type=jnp.float32,
    )


def column_sum(x):
    return jnp.sum(x, axis=0, keepdims=True)


def count_links(ids_ref, first, slots, wide, links):
    points, columns = links.shape
    block = 256
    here = lax.broadcasted_iota(jnp.int32, (16, columns), 0).astype(jnp.bfloat16)
    one = jnp.ones((16, columns), jnp.bfloat16)
    zero = jnp.zeros((16, columns), jnp.bfloat16)
    for start in range(0, points, block):
        for k in range(slots):
            local = ids_ref[first + k : first + k + 1, :] - float(start)
            local = jnp.where((local >= 0) & (local < block), local, -1.0)
            wide[k] = jnp.broadcast_to(local, (16, columns)).astype(jnp.bfloat16)

        def sixteen(step, carry):
            row = here + (step * 16).astype(jnp.float32).astype(jnp.bfloat16)
            total = zero
            for k in range(slots):
                total = total + jnp.where(wide[k] == row, one, zero)
            links[pl.ds(pl.multiple_of(start + step * 16, 16), 16), :] = total
            return carry

        lax.fori_loop(0, block // 16, sixteen, 0)


def links_kernel(firsts, slots, ids_ref, *refs):
    wide = refs[-1]
    for first, links in zip(firsts, refs[:-1]):
        count_links(ids_ref, first, slots, wide, links)


def part_links(part, firsts, slots, points):
    columns = part.shape[1]
    edges = len(firsts) * slots * points * columns
    return pl.pallas_call(
        functools.partial(links_kernel, firsts, slots),
        out_shape=[jax.ShapeDtypeStruct((points, columns), jnp.bfloat16)] * len(firsts),
        scratch_shapes=[pltpu.VMEM((slots, 16, columns), jnp.bfloat16)],
        compiler_params=params(8),
        cost_estimate=pl.CostEstimate(
            flops=100 * edges, bytes_accessed=2 * points * columns, transcendentals=0
        ),
        name="part_links",
    )(part)


def table_stats(x, weight, links, slots, a_ref, b_ref, in_ref, deg_ref, stat_ref):
    points, width = x.shape
    outs = weight.shape[1]
    upper, lower = weight[:width], weight[width:]
    joined = jnp.concatenate([upper - lower, lower], axis=1)
    middle = column_sum(x) / points
    level = jnp.dot(
        jnp.broadcast_to(middle, (8, width)), joined, precision=lax.Precision.HIGHEST
    )
    both = product(x - middle, joined, 1, 0) + level[0:1]
    a, b = both[:, :outs], both[:, outs:]
    mean_a = column_sum(a) / points
    a_off = a - mean_a
    terms = two_terms(a_off)
    seen = degree = 0.0
    for m, part in enumerate(links):
        columns = part.shape[1]
        some = terms[m * columns : (m + 1) * columns]
        seen = seen + jnp.dot(part[...], some, preferred_element_type=jnp.float32)
        degree = degree + jnp.sum(part[...].astype(jnp.float32), axis=1, keepdims=True)
    seen = halves_sum(seen)
    mean_b = column_sum(degree * b) / (points * slots)
    b_off = b - mean_b
    inward = seen + degree * b_off
    a_ref[...] = a
    b_ref[...] = b
    in_ref[...] = inward
    deg_ref[...] = jnp.broadcast_to(degree, deg_ref.shape)
    stat_ref[0:1, :] = mean_a + mean_b
    stat_ref[1:2, :] = slots * column_sum(a_off * a_off) + column_sum((seen + inward) * b_off)


def first_kernel(slots, width, count, *refs):
    parts, early, (weight_ref, x_ref, ids_ref, a_ref, b_ref, in_ref, deg_ref, stat_ref, *late, wide) = (
        refs[:count],
        refs[count : count + count // 2],
        refs[count + count // 2 :],
    )
    rows = parts[0].shape[1]
    fill = jnp.zeros((128 - parts[0].shape[0], rows), jnp.float32)
    for m, part in enumerate(parts):
        ids_ref[:, m * rows : (m + 1) * rows] = part[width:, :]
        x_ref[m * rows : (m + 1) * rows, :] = jnp.concatenate([part[...], fill], axis=0).T
    for part, links in zip(parts[len(early) :], late):
        count_links(part, width, slots, wide, links)
    table_stats(
        x_ref[:, :width], weight_ref[...], (*early, *late), slots, a_ref, b_ref, in_ref, deg_ref, stat_ref
    )


def first_tables(parts, early, weight, slots):
    count, columns = len(parts), parts[0].shape[1]
    points = count * columns
    width, outs = weight.shape[0] // 2, weight.shape[1]
    return pl.pallas_call(
        functools.partial(first_kernel, slots, width, count),
        out_shape=[
            f32(points, 128),
            f32(2 * slots, points),
            f32(points, outs),
            f32(points, outs),
            f32(points, outs),
            f32(points, 128),
            f32(2, outs),
        ],
        scratch_shapes=[pltpu.VMEM((points, columns), jnp.bfloat16)] * (count - len(early))
        + [pltpu.VMEM((slots, 16, columns), jnp.bfloat16)],
        compiler_params=params(24),
        name="first_tables",
    )(*parts, *early, weight)


def second_kernel(slots, x_ref, weight_ref, *refs):
    links, outs = refs[:-5], refs[-5:]
    table_stats(x_ref[...], weight_ref[...], links, slots, *outs)


def second_tables(x, weight, links, slots):
    points, outs = x.shape[0], weight.shape[1]
    return pl.pallas_call(
        functools.partial(second_kernel, slots),
        out_shape=[
            f32(points, outs),
            f32(points, outs),
            f32(points, outs),
            f32(points, 128),
            f32(2, outs),
        ],
        compiler_params=params(24),
        name="second_tables",
    )(x, weight, *links)


def edge_kernel(
    edges, layer, slots, first, tile, x_ref, a_ref, b_ref, stat_ref, small_ref,
    out_ref, weight_ref, inv_ref, slope_ref, moment_ref, ysum_ref, table, centre, held, bounded,
):
    points, width = a_ref.shape
    step = pl.program_id(0)
    block = 8

    @pl.when(step == 0)
    def _():
        gain = small_ref[2 * layer : 2 * layer + 1, 0:width]
        shift = small_ref[2 * layer + 1 : 2 * layer + 2, 0:width]
        scale = gain * lax.rsqrt(stat_ref[1:2, :] / edges + norm_eps) * -LOG2E
        middle = column_sum(b_ref[...]) / points
        there = (b_ref[...] - middle) * scale
        here = (a_ref[...] + (middle - stat_ref[0:1, :])) * scale - shift * LOG2E
        table[...] = two_terms(there)
        centre[...] = here
        reach = jnp.max(jnp.abs(here), axis=0, keepdims=True) + jnp.max(
            jnp.abs(there), axis=0, keepdims=True
        )
        bounded[0] = (jnp.max(reach) < 60.0).astype(jnp.int32)

    rows = pl.ds(pl.multiple_of(step * tile, tile), tile)
    columns = lax.broadcasted_iota(jnp.int32, (tile, points), 1).astype(jnp.float32)

    def gather(ids):
        pick = jnp.where(ids == columns, 1.0, 0.0).astype(jnp.bfloat16)
        return jnp.dot(pick, table[...], preferred_element_type=jnp.float32)

    def finish(at, top, totals):
        mass, slope, moment, total = totals
        out_ref[at, :] = top + jnp.log(mass)
        inv = 0.8 / mass
        inv_ref[at, :] = inv
        slope_ref[at, :] = slope * inv
        moment_ref[at, :] = moment * inv * (-1.0 / LOG2E)
        ysum_ref[at, :] = total * (-1.0 / LOG2E)

    @pl.when(bounded[0] == 1)
    def _():
        found = [gather(x_ref[rows, first + k : first + k + 1]) for k in range(slots)]
        for start in range(0, tile, block):
            at = slice(start, start + block)
            here = centre[pl.ds(pl.multiple_of(step * tile + start, block), block), :]
            totals = [jnp.zeros((block, width), jnp.float32)] * 4
            for k in range(slots):
                t = here + halves_sum(found[k][at])
                grown = 1.0 + jnp.exp2(t)
                fall = jnp.exp2((-0.2 * LOG2E) * jnp.log(grown) - t)
                share = grown * fall
                part = fall + 0.25 * share
                weight_ref[k, at, :] = part
                totals = [total + term for total, term in zip(totals, (share, part, part * t, t))]
            finish(at, 0.0, totals)

    @pl.when(bounded[0] == 0)
    def _():
        lanes = lax.broadcasted_iota(jnp.int32, (tile, x_ref.shape[1]), 1)

        def collect(k, carry):
            ids = jnp.sum(jnp.where(lanes == first + k, x_ref[rows, :], 0.0), axis=1, keepdims=True)
            held[k] = centre[rows, :] + halves_sum(gather(ids))
            return carry

        lax.fori_loop(0, slots, collect, 0)

        def rise(t):
            grown = 1.0 + jnp.exp2(jnp.minimum(t, 64.0))
            return jnp.maximum((0.8 * LOG2E) * jnp.log(grown), 0.8 * t) - t, grown

        def some(b, carry):
            at = pl.ds(pl.multiple_of(b * block, block), block)
            low = held[0, at, :]
            for k in range(1, slots):
                low = jnp.minimum(low, held[k, at, :])
            peak, _ = rise(low)
            totals = [jnp.zeros((block, width), jnp.float32)] * 4
            for k in range(slots):
                t = held[k, at, :]
                level, grown = rise(t)
                share = jnp.exp2(level - peak)
                part = share * (1.0 / grown + 0.25)
                weight_ref[k, at, :] = part
                totals = [total + term for total, term in zip(totals, (share, part, part * t, t))]
            finish(at, peak * (1.0 / LOG2E), totals)
            return carry

        lax.fori_loop(0, tile // block, some, 0)


def edge_forward(edges, layer, slots, first, tile, x, a, b, stat, small):
    points, width = a.shape
    some = pl.BlockSpec((tile, width), lambda step: (step, 0))
    return pl.pallas_call(
        functools.partial(edge_kernel, edges, layer, slots, first, tile),
        grid=(points // tile,),
        in_specs=[whole(v.shape) for v in (x, a, b, stat, small)],
        out_specs=[some, pl.BlockSpec((slots, tile, width), lambda step: (0, step, 0))] + [some] * 4,
        out_shape=[f32(points, width), in_hbm(slots, points, width)] + [f32(points, width)] * 4,
        scratch_shapes=[
            pltpu.VMEM((points, 2 * width), jnp.bfloat16),
            pltpu.VMEM((points, width), jnp.float32),
            pltpu.VMEM((slots, tile, width), jnp.float32),
            pltpu.SMEM((1,), jnp.int32),
        ],
        compiler_params=params(24),
        name="edges",
    )(x, a, b, stat, small)


def pool_kernel(me_ref, out_ref, inv_ref, slope_ref, moment_ref, gmax_ref, gmean_ref, *refs):
    count = (len(refs) - 2) // 2
    acts, parts = refs[:count], refs[count : 2 * count]
    scaled_ref, own_ref = refs[2 * count :]
    me = me_ref[0]
    points, width = out_ref.shape
    rows = points // count
    out = out_ref[...]
    top = jnp.max(out, axis=0, keepdims=True)
    pool = top + jnp.log(column_sum(jnp.exp(out - top)))
    mean = column_sum(out) / points
    to_max = gmax_ref[pl.ds(me, 1), :]
    to_mean = gmean_ref[pl.ds(me, 1), :] / points
    own_sum = moment_sum = jnp.zeros((1, width), jnp.float32)
    for m in range(count):
        here = slice(m * rows, (m + 1) * rows)
        part = out[here]
        parts[m][0:rows, :] = part
        parts[m][rows : rows + 1, :] = pool
        parts[m][rows + 1 : rows + 2, :] = mean
        parts[m][rows + 4 : rows + 8, :] = jnp.zeros((4, width), jnp.float32)
        grad = acts[m][...] + to_max * jnp.exp(part - pool) + to_mean
        own = grad * slope_ref[here, :]
        scaled_ref[here, :] = grad * inv_ref[here, :]
        own_ref[here, :] = own
        own_sum = own_sum + column_sum(own)
        moment_sum = moment_sum + column_sum(grad * moment_ref[here, :])
    for m in range(count):
        parts[m][rows + 2 : rows + 3, :] = own_sum
        parts[m][rows + 3 : rows + 4, :] = moment_sum


def pools(me, out, inv, slope, moment, grad_max, grad_mean, acts):
    points, width = out.shape
    count = len(acts)
    rows = points // count
    results = pl.pallas_call(
        pool_kernel,
        in_specs=[SMEM] + [pl.BlockSpec(memory_space=pltpu.VMEM)] * (6 + count),
        out_shape=[f32(rows + 8, width)] * count + [f32(points, width)] * 2,
        compiler_params=params(16),
        name="pools",
    )(me, out, inv, slope, moment, grad_max, grad_mean, *acts)
    return results[:count], results[count], results[count + 1]


def scatter_kernel(first, group, ids_ref, grad_ref, weight_ref, sum_ref):
    step = pl.program_id(0)
    points = grad_ref.shape[0]
    rows = lax.broadcasted_iota(jnp.int32, (points, points), 0).astype(jnp.float32)
    picks, terms = [], []
    for g in range(group):
        ids = ids_ref[pl.ds(first + step * group + g, 1), :]
        picks.append(jnp.where(ids == rows, 1.0, 0.0).astype(jnp.bfloat16))
        terms.append(two_terms(grad_ref[...] * weight_ref[g]))
    found = halves_sum(
        jnp.dot(
            jnp.concatenate(picks, axis=1),
            jnp.concatenate(terms, axis=0),
            preferred_element_type=jnp.float32,
        )
    )

    @pl.when(step == 0)
    def _():
        sum_ref[...] = found

    @pl.when(step > 0)
    def _():
        sum_ref[...] += found


def scatter(ids, first, grad, weight, start, stop, group):
    points, width = grad.shape
    edges = (stop - start) * points
    return pl.pallas_call(
        functools.partial(scatter_kernel, first + start, group),
        grid=((stop - start) // group,),
        in_specs=[
            whole(ids.shape),
            whole(grad.shape),
            pl.BlockSpec((group, points, width), lambda step: (start // group + step, 0, 0)),
        ],
        out_specs=whole((points, width)),
        out_shape=f32(points, width),
        compiler_params=params(28),
        cost_estimate=pl.CostEstimate(
            flops=4 * edges * points * width, bytes_accessed=4 * edges * width, transcendentals=0
        ),
        name="scatter",
    )(ids, grad, from_hbm(weight))


def point_grads(edges, slots, own, inward_grads, ysum, inward, degree, local, stat, sums, gain, shift):
    spread = lax.rsqrt(stat[1:2, :] / edges + norm_eps)
    scale = gain * spread
    own_all = sums[0:1, :]
    gain_all = (sums[1:2, :] - shift * own_all) / gain
    shift_part = own_all / edges
    gain_part = gain_all / edges
    leave = scale * (own - slots * shift_part - gain_part * ((ysum - slots * shift) / gain))
    normed = spread * (inward + degree * (local[0:1, :] - stat[0:1, :]))
    reach = scale * (inward_grads - degree * shift_part - gain_part * normed)
    return leave, reach, gain_all


def turned(weight):
    width = weight.shape[0] // 2
    return jnp.concatenate([weight[:width] - weight[width:], weight[width:]], axis=1)


def weight_grad(x, leave, reach):
    grads = jnp.concatenate([leave, reach - leave], axis=1)
    middle = column_sum(x) / x.shape[0]
    level = lax.dot_general(
        jnp.broadcast_to(middle, (8, x.shape[1])) * 0.125,
        jnp.broadcast_to(column_sum(grads), (8, grads.shape[1])),
        (((0,), (0,)), ((), ())),
        precision=lax.Precision.HIGHEST,
        preferred_element_type=jnp.float32,
    )
    return product(x - middle, grads, 0, 0) + level


def total_of(refs):
    total = refs[0][...]
    for ref in refs[1:]:
        total = total + ref[...]
    return total


def middle_kernel(
    edges, slots, count, me_ref, own_ref, ysum_ref, in_ref, deg_ref, local_ref, stat_ref, sums_ref,
    small_ref, x_ref, weight_ref, inv_ref, slope_ref, moment_ref, *refs,
):
    wgrad = refs[-1]
    scaled_ref, next_ref, gain_out_ref = refs[-4:-1]
    reached, parts = refs[: -4 - count], refs[-4 - count : -4]
    leave, reach, gain_all = point_grads(
        edges, slots, own_ref[...], total_of(reached), ysum_ref[...], in_ref[...], deg_ref[:, 0:1],
        local_ref[...], stat_ref[...], sums_ref[...], small_ref[2:3, :], small_ref[3:4, :],
    )
    gain_out_ref[...] = gain_all
    width, outs = x_ref.shape[1], leave.shape[1]
    both = weight_grad(x_ref[...], leave, reach)
    wgrad[0:width, :] = both[:, :outs]
    wgrad[width:, :] = both[:, outs:]
    grad = product(jnp.concatenate([leave, reach], axis=1), turned(weight_ref[...]), 1, 1)
    own = grad * slope_ref[...]
    scaled_ref[...] = grad * inv_ref[...]
    next_ref[...] = own
    own_sum = column_sum(own)
    moment_sum = column_sum(grad * moment_ref[...])
    me = me_ref[0]
    piece = 2 * width // count
    for mask, part in enumerate(parts):
        start = pl.multiple_of((me ^ mask) * piece, piece)
        part[0:piece, :] = wgrad[pl.ds(start, piece), :]
        part[piece:, :] = jnp.zeros((8, outs), jnp.float32)
        part[piece : piece + 1, 0:width] = own_sum
        part[piece + 1 : piece + 2, 0:width] = moment_sum


def middle(
    edges, slots, count, me, own, ysum, inward, degree, local, stat, sums, small, x, weight,
    inv, slope, moment, reached,
):
    points, width = x.shape
    outs = weight.shape[1]
    operands = (own, ysum, inward, degree, local, stat, sums, small, x, weight, inv, slope, moment)
    results = pl.pallas_call(
        functools.partial(middle_kernel, edges, slots, count),
        in_specs=[SMEM] + [pl.BlockSpec(memory_space=pltpu.VMEM)] * (len(operands) + len(reached)),
        out_shape=[f32(2 * width // count + 8, outs)] * count
        + [f32(points, width), f32(points, width), f32(1, outs)],
        scratch_shapes=[pltpu.VMEM((2 * width, outs), jnp.float32)],
        compiler_params=params(32),
        name="middle",
    )(me, *operands, *reached)
    return results[:count], *results[count:]


def last_kernel(
    edges, slots, count, own_ref, ysum_ref, in_ref, deg_ref, local_ref, stat_ref, joined_ref,
    small_ref, x_ref, weight_ref, *refs,
):
    reached, (gain_out_ref, wgrad_ref), parts = (
        refs[: -2 - count],
        refs[-2 - count : -count],
        refs[-count:],
    )
    width, outs = weight_ref.shape[0] // 2, weight_ref.shape[1]
    piece = joined_ref.shape[0] - 8
    leave, reach, gain_all = point_grads(
        edges, slots, own_ref[...], total_of(reached), ysum_ref[...], in_ref[...], deg_ref[:, 0:1],
        local_ref[...], stat_ref[...], joined_ref[piece : piece + 2, 0:outs],
        small_ref[0:1, 0:outs], small_ref[1:2, 0:outs],
    )
    gain_out_ref[...] = gain_all
    wgrad_ref[...] = weight_grad(x_ref[:, 0:width], leave, reach)
    grad = product(turned(weight_ref[...]), jnp.concatenate([leave, reach], axis=1), 1, 1)
    rows = grad.shape[1] // count
    for m, part in enumerate(parts):
        part[0:width, :] = grad[:, m * rows : (m + 1) * rows]
        part[width:, :] = joined_ref[0:piece, :]


def last(
    edges, slots, count, own, ysum, inward, degree, local, stat, joined, small, x, weight, reached
):
    points = x.shape[0]
    width, outs = weight.shape[0] // 2, weight.shape[1]
    lanes = points // count
    assert lanes == 2 * outs == joined.shape[1]
    results = pl.pallas_call(
        functools.partial(last_kernel, edges, slots, count),
        out_shape=[f32(1, outs), f32(width, 2 * outs)] + [f32(width + joined.shape[0] - 8, lanes)] * count,
        compiler_params=params(32),
        name="last",
    )(own, ysum, inward, degree, local, stat, joined, small, x, weight, *reached)
    return results[0], results[1], results[2:]


def body(
    features,
    neighbours_one,
    neighbours_two,
    weight_one,
    gain_one,
    shift_one,
    weight_two,
    gain_two,
    shift_two,
    grad_act,
    grad_max,
    grad_mean,
):
    clouds, rows, width = features.shape
    slots = neighbours_one.shape[1]
    count = lax.axis_size("pts")
    assert clouds == count
    points = rows * count
    local_edges = points * slots
    edges = float(local_edges * lax.axis_size(BOTH))
    me = lax.axis_index("pts").astype(jnp.int32).reshape(1)
    def to_owner(parts):
        return [parts[0]] + [exchange(part, "pts", m) for m, part in enumerate(parts) if m]

    with jax.named_scope("bring_clouds"):
        parts, small, (weight_one, weight_two) = pack(
            me, features, neighbours_one, neighbours_two,
            (gain_one, shift_one, gain_two, shift_two), (weight_one, weight_two),
        )
        parts = to_owner(parts)
        firsts = (width, width + slots)
        early = [part_links(part, firsts, slots, points) for part in parts[: count // 2]]
    with jax.named_scope("bring_cotangents"):
        acts = to_owner(split(me, grad_act))

    with jax.named_scope("layer_one"):
        x, ids, a_one, b_one, in_one, deg_one, local_one = first_tables(
            parts, [links[0] for links in early], weight_one, slots
        )
        late = [part_links(part, firsts[1:], slots, points) for part in parts[count // 2 :]]
        links = [links[-1] for links in early + late]
        stat_one = join_stats(local_one, local_edges)
        hidden, share_one, inv_one, slope_one, moment_one, ysum_one = edge_forward(
            edges, 0, slots, width, 128, x, a_one, b_one, stat_one, small
        )
    with jax.named_scope("layer_two"):
        a_two, b_two, in_two, deg_two, local_two = second_tables(hidden, weight_two, links, slots)
        stat_two = join_stats(local_two, local_edges)
        out, share_two, inv_two, slope_two, moment_two, ysum_two = edge_forward(
            edges, 1, slots, width + slots, 128, x, a_two, b_two, stat_two, small
        )
    with jax.named_scope("pools"):
        out_parts, scaled_two, own_two = pools(
            me, out, inv_two, slope_two, moment_two, grad_max, grad_mean, acts
        )
        out_parts = to_owner(out_parts)
        output, pool_max, pool_mean = unpack_output(me, out_parts)

    cut = 4 * (3 * slots // 20)
    with jax.named_scope("layer_two_back"):
        sums_two, reached = sum_beside(
            lambda received: pair_sum([part[rows + 2 : rows + 4] for part in received]),
            out_parts,
            [
                lambda ready: scatter(ids, slots, scaled_two, share_two, 0, cut, 4),
                lambda ready: scatter(ids, slots, after(scaled_two, ready), share_two, cut, slots, 4),
            ],
        )
        wgrad_parts, scaled_one, own_one, gain_grad_two = middle(
            edges, slots, count, me, own_two, ysum_two, in_two, deg_two, local_two, stat_two, sums_two,
            small, hidden, weight_two, inv_one, slope_one, moment_one, reached,
        )
    with jax.named_scope("layer_one_back"):
        joined, reached = sum_beside(
            lambda received: pair_sum(list(received)),
            to_owner(wgrad_parts),
            [
                lambda ready: scatter(ids, 0, scaled_one, share_one, 0, cut, 4),
                lambda ready: scatter(ids, 0, after(scaled_one, ready), share_one, cut, slots, 4),
            ],
        )
        gain_grad_one, wgrad_one, grad_parts = last(
            edges, slots, count, own_one, ysum_one, in_one, deg_one, local_one, stat_one, joined,
            small, x, weight_one, reached,
        )
        wgrad_one = pair_sum(to_owner([wgrad_one] * count))
        wgrad_one, *grad_parts = lax.optimization_barrier((wgrad_one, *grad_parts))
        grad_parts = to_owner(grad_parts)
        wgrad_one = sum_stages(wgrad_one, list(stages())[1:])
        wgrad_one = jnp.concatenate(jnp.split(wgrad_one, 2, axis=1), axis=0)
        grad_features, wgrad_two = unpack_grad(me, grad_parts, width)
    return (
        output,
        pool_max,
        pool_mean,
        jnp.swapaxes(grad_features, 1, 2),
        wgrad_one,
        gain_grad_one.reshape(-1),
        joined[-8, : weight_one.shape[1]],
        wgrad_two,
        gain_grad_two.reshape(-1),
        sums_two[0],
    )


def solution(mesh):
    placed = (
        P("clouds", "pts", None),
        P("clouds", None, "pts"),
        P("clouds", None, "pts"),
        P(),
        P(),
        P(),
        P(),
        P(),
        P(),
        P("clouds", "pts", None),
        P("clouds", None),
        P("clouds", None),
    )
    return jax.shard_map(
        body,
        mesh=mesh,
        in_specs=placed,
        out_specs=(
            P("clouds", "pts", None),
            P("clouds", None),
            P("clouds", None),
            P("clouds", "pts", None),
            P(),
            P(),
            P(),
            P(),
            P(),
            P(),
        ),
        check_vma=False,
    )
```

```python
import functools

import jax
import jax.numpy as jnp
from jax import lax
from jax.experimental import pallas as pl
from jax.experimental.pallas import tpu as pltpu
from jax.sharding import PartitionSpec as P

norm_eps = 1e-05
LOG2E = 1.4426950408889634
BOTH = ("clouds", "pts")
MIB = 2**20


def f32(*shape):
    return jax.ShapeDtypeStruct(shape, jnp.float32)


def in_hbm(*shape):
    return pltpu.HBM(shape, jnp.float32)


def from_hbm(x):
    return pltpu.with_memory_space_constraint(x, pltpu.HBM)


def params(mib):
    return pltpu.CompilerParams(vmem_limit_bytes=mib * MIB)


def whole(shape):
    return pl.BlockSpec(shape, lambda *step: (0,) * len(shape))


SMEM = pl.BlockSpec(memory_space=pltpu.SMEM)


def exchange(x, axes, mask):
    size = lax.axis_size(axes)
    return lax.ppermute(x, axes, [(i, i ^ mask) for i in range(size)])


def bit_groups(size):
    bits = [1 << i for i in range(size.bit_length() - 1)]
    groups = [bits[:1]] if bits else []
    rest = bits[1:]
    while rest:
        groups.append(rest[:2])
        rest = rest[2:]
    return groups


def stages():
    yield "pts", list(range(1, lax.axis_size("pts")))
    for bits in bit_groups(lax.axis_size("clouds")):
        masks = [0]
        for bit in bits:
            masks = masks + [mask | bit for mask in masks]
        yield "clouds", masks[1:]


def swap(x, axes, masks):
    return [x] + [exchange(x, axes, mask) for mask in masks]


def pair_sum(values):
    while len(values) > 1:
        values = [values[i] + values[i + 1] for i in range(0, len(values), 2)]
    return values[0]


def sum_stages(x, cloud_stages):
    for axis, masks in cloud_stages:
        x = pair_sum(swap(x, axis, masks))
    return x


def after(value, *others):
    return lax.optimization_barrier((value, *others))[0]


def sum_beside(message, received, work):
    (axis, masks), *rest = list(stages())[:0:-1]
    first = work[0](None)
    total = message(lax.optimization_barrier((*received, first))[:-1])
    moving = swap(total, axis, masks)
    second = work[1](total)
    total = pair_sum(list(lax.optimization_barrier((*moving, second))[:-1]))
    return sum_stages(total, rest), [first, second]


def join_stats(stat, count):
    for axis, masks in stages():
        parts = swap(stat, axis, masks)
        mean = pair_sum([part[0:1] for part in parts]) / len(parts)
        away = pair_sum([(part[0:1] - mean) ** 2 for part in parts])
        stat = jnp.concatenate([mean, pair_sum([part[1:2] for part in parts]) + count * away], axis=0)
        count = count * len(parts)
    return stat


def pack_kernel(slots, me_ref, *refs):
    sources, outs, fetched, sems = refs[:9], refs[9:-10], refs[-10:-1], refs[-1]
    parts, small_ref, weights = outs[:-3], outs[-3], outs[-2:]
    copies = [
        pltpu.make_async_copy(source, target, sems.at[i])
        for i, (source, target) in enumerate(zip(sources, fetched))
    ]
    for copy in copies:
        copy.start()
    for copy in copies:
        copy.wait()
    feat_ref, one_ref, two_ref = fetched[:3]
    me = me_ref[0]
    width, rows = feat_ref.shape[1], feat_ref.shape[2]
    for mask, out in enumerate(parts):
        cloud = me ^ mask
        out[0:width, :] = feat_ref[cloud]
        for k in range(slots):
            for at, ids in ((width, one_ref), (width + slots, two_ref)):
                row = ids[k, pl.ds(cloud, 1), :] ^ (cloud * rows)
                out[at + k : at + k + 1, :] = row.astype(jnp.float32)
    small_ref[...] = jnp.zeros_like(small_ref)
    for i, vector in enumerate(fetched[3:7]):
        small_ref[i : i + 1, 0 : vector.shape[1]] = vector[...]
    for kept, weight in zip(weights, fetched[7:9]):
        kept[...] = weight[...]


def pack(me, features, neighbours_one, neighbours_two, vectors, weights):
    clouds, rows, width = features.shape
    slots = neighbours_one.shape[1]
    operands = (
        jnp.swapaxes(features, 1, 2),
        jnp.swapaxes(neighbours_one, 0, 1),
        jnp.swapaxes(neighbours_two, 0, 1),
        *(v.reshape(1, -1) for v in vectors),
        *weights,
    )
    results = pl.pallas_call(
        functools.partial(pack_kernel, slots),
        in_specs=[SMEM] + [pl.BlockSpec(memory_space=pltpu.HBM)] * len(operands),
        out_shape=[f32(width + 2 * slots, rows)] * clouds
        + [f32(8, max(v.shape[0] for v in vectors))]
        + [f32(*w.shape) for w in weights],
        scratch_shapes=[pltpu.VMEM(v.shape, v.dtype) for v in operands]
        + [pltpu.SemaphoreType.DMA((len(operands),))],
        compiler_params=params(8),
        name="pack",
    )(me, *(from_hbm(v) for v in operands))
    return results[:clouds], results[clouds], results[clouds + 1 :]


def split_kernel(me_ref, x_ref, *outs):
    me = me_ref[0]
    for mask, out in enumerate(outs):
        out[...] = x_ref[me ^ mask]


def split(me, x):
    clouds, rows, width = x.shape
    return pl.pallas_call(
        split_kernel,
        in_specs=[SMEM, pl.BlockSpec(memory_space=pltpu.VMEM)],
        out_shape=[f32(rows, width)] * clouds,
        compiler_params=params(16),
        name="split",
    )(me, from_hbm(x))


def unpack_output_kernel(rows, me_ref, *refs):
    parts, (act_ref, max_ref, mean_ref) = refs[:-3], refs[-3:]
    me = me_ref[0]
    for mask, part in enumerate(parts):
        cloud = me ^ mask
        act_ref[cloud] = part[0:rows]
        max_ref[pl.ds(cloud, 1), :] = part[rows : rows + 1]
        mean_ref[pl.ds(cloud, 1), :] = part[rows + 1 : rows + 2]


def unpack_output(me, parts):
    clouds, width = len(parts), parts[0].shape[1]
    rows = parts[0].shape[0] - 8
    return pl.pallas_call(
        functools.partial(unpack_output_kernel, rows),
        in_specs=[SMEM] + [pl.BlockSpec(memory_space=pltpu.VMEM)] * clouds,
        out_shape=[f32(clouds, rows, width), f32(clouds, width), f32(clouds, width)],
        compiler_params=params(16),
        name="unpack_output",
    )(me, *parts)


def unpack_grad_kernel(me_ref, *refs):
    parts, (grad_ref, wgrad_ref) = refs[:-2], refs[-2:]
    me = me_ref[0]
    width = grad_ref.shape[1]
    piece = wgrad_ref.shape[0] // len(parts)
    for mask, part in enumerate(parts):
        other = me ^ mask
        grad_ref[other] = part[0:width]
        wgrad_ref[pl.ds(pl.multiple_of(other * piece, piece), piece), :] = part[width:]


def unpack_grad(me, parts, width):
    rows, lanes = parts[0].shape
    count = len(parts)
    return pl.pallas_call(
        unpack_grad_kernel,
        in_specs=[SMEM] + [pl.BlockSpec(memory_space=pltpu.VMEM)] * count,
        out_shape=[f32(count, width, lanes), f32(count * (rows - width), lanes)],
        compiler_params=params(16),
        name="unpack_grad",
    )(me, *parts)


def two_terms(x):
    high = x.astype(jnp.bfloat16)
    low = (x - high.astype(jnp.float32)).astype(jnp.bfloat16)
    return jnp.concatenate([high, low], axis=1)


def halves_sum(x):
    half = x.shape[1] // 2
    return x[:, :half] + x[:, half:]


def product(x, y, on_x, on_y):
    x_high, y_high = x.astype(jnp.bfloat16), y.astype(jnp.bfloat16)
    x_low = (x - x_high.astype(jnp.float32)).astype(jnp.bfloat16)
    y_low = (y - y_high.astype(jnp.float32)).astype(jnp.bfloat16)
    return lax.dot_general(
        jnp.concatenate([x_high, x_low, x_high], axis=on_x),
        jnp.concatenate([y_high, y_high, y_low], axis=on_y),
        (((on_x,), (on_y,)), ((), ())),
        preferred_element_type=jnp.float32,
    )


def column_sum(x):
    return jnp.sum(x, axis=0, keepdims=True)


def count_links(ids_ref, first, slots, wide, links):
    points, columns = links.shape
    block, rows, groups = 256, 16, 4
    here = lax.broadcasted_iota(jnp.int32, (rows, columns), 0).astype(jnp.bfloat16)
    one = jnp.ones((rows, columns), jnp.bfloat16)
    zero = jnp.zeros((rows, columns), jnp.bfloat16)
    for start in range(0, points, block):
        for k in range(slots):
            local = ids_ref[first + k : first + k + 1, :] - float(start)
            wide[k] = jnp.broadcast_to(local, (rows, columns)).astype(jnp.bfloat16)

        def some(step, carry):
            base = step * (rows * groups)
            names = [here + (base + g * rows).astype(jnp.float32).astype(jnp.bfloat16) for g in range(groups)]
            totals = [zero] * groups
            for k in range(slots):
                ids = wide[k]
                totals = [
                    total + jnp.where(ids == name, one, zero) for total, name in zip(totals, names)
                ]
            for g in range(groups):
                at = pl.ds(pl.multiple_of(start + base + g * rows, rows), rows)
                links[at, :] = totals[g]
            return carry

        lax.fori_loop(0, block // (rows * groups), some, 0)


def links_kernel(firsts, slots, ids_ref, *refs):
    wide = refs[-1]
    for first, links in zip(firsts, refs[:-1]):
        count_links(ids_ref, first, slots, wide, links)


def part_links(part, firsts, slots, points):
    columns = part.shape[1]
    edges = len(firsts) * slots * points * columns
    return pl.pallas_call(
        functools.partial(links_kernel, firsts, slots),
        out_shape=[jax.ShapeDtypeStruct((points, columns), jnp.bfloat16)] * len(firsts),
        scratch_shapes=[pltpu.VMEM((slots, 16, columns), jnp.bfloat16)],
        compiler_params=params(8),
        cost_estimate=pl.CostEstimate(
            flops=100 * edges, bytes_accessed=2 * points * columns, transcendentals=0
        ),
        name="part_links",
    )(part)


def table_stats(x, weight, links, slots, a_ref, b_ref, in_ref, deg_ref, stat_ref):
    points, width = x.shape
    outs = weight.shape[1]
    upper, lower = weight[:width], weight[width:]
    joined = jnp.concatenate([upper - lower, lower], axis=1)
    middle = column_sum(x) / points
    level = jnp.dot(
        jnp.broadcast_to(middle, (8, width)), joined, precision=lax.Precision.HIGHEST
    )
    both = product(x - middle, joined, 1, 0) + level[0:1]
    a, b = both[:, :outs], both[:, outs:]
    mean_a = column_sum(a) / points
    a_off = a - mean_a
    terms = two_terms(a_off)
    seen = degree = 0.0
    for m, part in enumerate(links):
        columns = part.shape[1]
        some = terms[m * columns : (m + 1) * columns]
        seen = seen + jnp.dot(part[...], some, preferred_element_type=jnp.float32)
        degree = degree + jnp.sum(part[...].astype(jnp.float32), axis=1, keepdims=True)
    seen = halves_sum(seen)
    mean_b = column_sum(degree * b) / (points * slots)
    b_off = b - mean_b
    inward = seen + degree * b_off
    a_ref[...] = a
    b_ref[...] = b
    in_ref[...] = inward
    deg_ref[...] = jnp.broadcast_to(degree, deg_ref.shape)
    stat_ref[0:1, :] = mean_a + mean_b
    stat_ref[1:2, :] = slots * column_sum(a_off * a_off) + column_sum((seen + inward) * b_off)


def first_kernel(slots, width, count, *refs):
    parts, early, (weight_ref, x_ref, ids_ref, a_ref, b_ref, in_ref, deg_ref, stat_ref, *late, wide) = (
        refs[:count],
        refs[count : count + count // 2],
        refs[count + count // 2 :],
    )
    rows = parts[0].shape[1]
    fill = jnp.zeros((128 - parts[0].shape[0], rows), jnp.float32)
    for m, part in enumerate(parts):
        ids_ref[:, m * rows : (m + 1) * rows] = part[width:, :]
        x_ref[m * rows : (m + 1) * rows, :] = jnp.concatenate([part[...], fill], axis=0).T
    for part, links in zip(parts[len(early) :], late):
        count_links(part, width, slots, wide, links)
    table_stats(
        x_ref[:, :width], weight_ref[...], (*early, *late), slots, a_ref, b_ref, in_ref, deg_ref, stat_ref
    )


def first_tables(parts, early, weight, slots):
    count, columns = len(parts), parts[0].shape[1]
    points = count * columns
    width, outs = weight.shape[0] // 2, weight.shape[1]
    return pl.pallas_call(
        functools.partial(first_kernel, slots, width, count),
        out_shape=[
            f32(points, 128),
            f32(2 * slots, points),
            f32(points, outs),
            f32(points, outs),
            f32(points, outs),
            f32(points, 128),
            f32(2, outs),
        ],
        scratch_shapes=[pltpu.VMEM((points, columns), jnp.bfloat16)] * (count - len(early))
        + [pltpu.VMEM((slots, 16, columns), jnp.bfloat16)],
        compiler_params=params(24),
        name="first_tables",
    )(*parts, *early, weight)


def second_kernel(slots, x_ref, weight_ref, *refs):
    links, outs = refs[:-5], refs[-5:]
    table_stats(x_ref[...], weight_ref[...], links, slots, *outs)


def second_tables(x, weight, links, slots):
    points, outs = x.shape[0], weight.shape[1]
    return pl.pallas_call(
        functools.partial(second_kernel, slots),
        out_shape=[
            f32(points, outs),
            f32(points, outs),
            f32(points, outs),
            f32(points, 128),
            f32(2, outs),
        ],
        compiler_params=params(24),
        name="second_tables",
    )(x, weight, *links)


def edge_kernel(
    edges, layer, slots, first, tile, x_ref, a_ref, b_ref, stat_ref, small_ref,
    out_ref, weight_ref, inv_ref, slope_ref, moment_ref, ysum_ref, table, centre, held, bounded,
):
    points, width = a_ref.shape
    step = pl.program_id(0)
    block = 8

    @pl.when(step == 0)
    def _():
        gain = small_ref[2 * layer : 2 * layer + 1, 0:width]
        shift = small_ref[2 * layer + 1 : 2 * layer + 2, 0:width]
        scale = gain * lax.rsqrt(stat_ref[1:2, :] / edges + norm_eps) * -LOG2E
        middle = column_sum(b_ref[...]) / points
        there = (b_ref[...] - middle) * scale
        here = (a_ref[...] + (middle - stat_ref[0:1, :])) * scale - shift * LOG2E
        table[...] = two_terms(there)
        centre[...] = here
        reach = jnp.max(jnp.abs(here), axis=0, keepdims=True) + jnp.max(
            jnp.abs(there), axis=0, keepdims=True
        )
        bounded[0] = (jnp.max(reach) < 60.0).astype(jnp.int32)

    rows = pl.ds(pl.multiple_of(step * tile, tile), tile)
    columns = lax.broadcasted_iota(jnp.int32, (tile, points), 1).astype(jnp.float32)

    def gather(ids):
        pick = jnp.where(ids == columns, 1.0, 0.0).astype(jnp.bfloat16)
        return jnp.dot(pick, table[...], preferred_element_type=jnp.float32)

    def finish(at, top, totals):
        mass, slope, moment, total = totals
        out_ref[at, :] = top + jnp.log(mass)
        inv = 0.8 / mass
        inv_ref[at, :] = inv
        slope_ref[at, :] = slope * inv
        moment_ref[at, :] = moment * inv * (-1.0 / LOG2E)
        ysum_ref[at, :] = total * (-1.0 / LOG2E)

    @pl.when(bounded[0] == 1)
    def _():
        found = [gather(x_ref[rows, first + k : first + k + 1]) for k in range(slots)]
        for start in range(0, tile, block):
            at = slice(start, start + block)
            here = centre[pl.ds(pl.multiple_of(step * tile + start, block), block), :]
            totals = [jnp.zeros((block, width), jnp.float32)] * 4
            for k in range(slots):
                t = here + halves_sum(found[k][at])
                grown = 1.0 + jnp.exp2(t)
                fall = jnp.exp2((-0.2 * LOG2E) * jnp.log(grown) - t)
                share = grown * fall
                part = fall + 0.25 * share
                weight_ref[k, at, :] = part
                totals = [total + term for total, term in zip(totals, (share, part, part * t, t))]
            finish(at, 0.0, totals)

    @pl.when(bounded[0] == 0)
    def _():
        lanes = lax.broadcasted_iota(jnp.int32, (tile, x_ref.shape[1]), 1)

        def collect(k, carry):
            ids = jnp.sum(jnp.where(lanes == first + k, x_ref[rows, :], 0.0), axis=1, keepdims=True)
            held[k] = centre[rows, :] + halves_sum(gather(ids))
            return carry

        lax.fori_loop(0, slots, collect, 0)

        def rise(t):
            grown = 1.0 + jnp.exp2(jnp.minimum(t, 64.0))
            return jnp.maximum((0.8 * LOG2E) * jnp.log(grown), 0.8 * t) - t, grown

        def some(b, carry):
            at = pl.ds(pl.multiple_of(b * block, block), block)
            low = held[0, at, :]
            for k in range(1, slots):
                low = jnp.minimum(low, held[k, at, :])
            peak, _ = rise(low)
            totals = [jnp.zeros((block, width), jnp.float32)] * 4
            for k in range(slots):
                t = held[k, at, :]
                level, grown = rise(t)
                share = jnp.exp2(level - peak)
                part = share * (1.0 / grown + 0.25)
                weight_ref[k, at, :] = part
                totals = [total + term for total, term in zip(totals, (share, part, part * t, t))]
            finish(at, peak * (1.0 / LOG2E), totals)
            return carry

        lax.fori_loop(0, tile // block, some, 0)


def edge_forward(edges, layer, slots, first, tile, x, a, b, stat, small):
    points, width = a.shape
    some = pl.BlockSpec((tile, width), lambda step: (step, 0))
    return pl.pallas_call(
        functools.partial(edge_kernel, edges, layer, slots, first, tile),
        grid=(points // tile,),
        in_specs=[whole(v.shape) for v in (x, a, b, stat, small)],
        out_specs=[some, pl.BlockSpec((slots, tile, width), lambda step: (0, step, 0))] + [some] * 4,
        out_shape=[f32(points, width), in_hbm(slots, points, width)] + [f32(points, width)] * 4,
        scratch_shapes=[
            pltpu.VMEM((points, 2 * width), jnp.bfloat16),
            pltpu.VMEM((points, width), jnp.float32),
            pltpu.VMEM((slots, tile, width), jnp.float32),
            pltpu.SMEM((1,), jnp.int32),
        ],
        compiler_params=params(24),
        name="edges",
    )(x, a, b, stat, small)


def pool_kernel(me_ref, out_ref, inv_ref, slope_ref, moment_ref, gmax_ref, gmean_ref, *refs):
    count = (len(refs) - 2) // 2
    acts, parts = refs[:count], refs[count : 2 * count]
    scaled_ref, own_ref = refs[2 * count :]
    me = me_ref[0]
    points, width = out_ref.shape
    rows = points // count
    out = out_ref[...]
    top = jnp.max(out, axis=0, keepdims=True)
    pool = top + jnp.log(column_sum(jnp.exp(out - top)))
    mean = column_sum(out) / points
    to_max = gmax_ref[pl.ds(me, 1), :]
    to_mean = gmean_ref[pl.ds(me, 1), :] / points
    own_sum = moment_sum = jnp.zeros((1, width), jnp.float32)
    for m in range(count):
        here = slice(m * rows, (m + 1) * rows)
        part = out[here]
        parts[m][0:rows, :] = part
        parts[m][rows : rows + 1, :] = pool
        parts[m][rows + 1 : rows + 2, :] = mean
        parts[m][rows + 4 : rows + 8, :] = jnp.zeros((4, width), jnp.float32)
        grad = acts[m][...] + to_max * jnp.exp(part - pool) + to_mean
        own = grad * slope_ref[here, :]
        scaled_ref[here, :] = grad * inv_ref[here, :]
        own_ref[here, :] = own
        own_sum = own_sum + column_sum(own)
        moment_sum = moment_sum + column_sum(grad * moment_ref[here, :])
    for m in range(count):
        parts[m][rows + 2 : rows + 3, :] = own_sum
        parts[m][rows + 3 : rows + 4, :] = moment_sum


def pools(me, out, inv, slope, moment, grad_max, grad_mean, acts):
    points, width = out.shape
    count = len(acts)
    rows = points // count
    results = pl.pallas_call(
        pool_kernel,
        in_specs=[SMEM] + [pl.BlockSpec(memory_space=pltpu.VMEM)] * (6 + count),
        out_shape=[f32(rows + 8, width)] * count + [f32(points, width)] * 2,
        compiler_params=params(16),
        name="pools",
    )(me, out, inv, slope, moment, grad_max, grad_mean, *acts)
    return results[:count], results[count], results[count + 1]


def scatter_kernel(first, group, ids_ref, grad_ref, weight_ref, sum_ref):
    step = pl.program_id(0)
    points = grad_ref.shape[0]
    rows = lax.broadcasted_iota(jnp.int32, (points, points), 0).astype(jnp.float32)
    picks, terms = [], []
    for g in range(group):
        ids = ids_ref[pl.ds(first + step * group + g, 1), :]
        picks.append(jnp.where(ids == rows, 1.0, 0.0).astype(jnp.bfloat16))
        terms.append(two_terms(grad_ref[...] * weight_ref[g]))
    found = halves_sum(
        jnp.dot(
            jnp.concatenate(picks, axis=1),
            jnp.concatenate(terms, axis=0),
            preferred_element_type=jnp.float32,
        )
    )

    @pl.when(step == 0)
    def _():
        sum_ref[...] = found

    @pl.when(step > 0)
    def _():
        sum_ref[...] += found


def scatter(ids, first, grad, weight, start, stop, group):
    points, width = grad.shape
    edges = (stop - start) * points
    return pl.pallas_call(
        functools.partial(scatter_kernel, first + start, group),
        grid=((stop - start) // group,),
        in_specs=[
            whole(ids.shape),
            whole(grad.shape),
            pl.BlockSpec((group, points, width), lambda step: (start // group + step, 0, 0)),
        ],
        out_specs=whole((points, width)),
        out_shape=f32(points, width),
        compiler_params=params(28),
        cost_estimate=pl.CostEstimate(
            flops=4 * edges * points * width, bytes_accessed=4 * edges * width, transcendentals=0
        ),
        name="scatter",
    )(ids, grad, from_hbm(weight))


def point_grads(edges, slots, own, inward_grads, ysum, inward, degree, local, stat, sums, gain, shift):
    spread = lax.rsqrt(stat[1:2, :] / edges + norm_eps)
    scale = gain * spread
    own_all = sums[0:1, :]
    gain_all = (sums[1:2, :] - shift * own_all) / gain
    shift_part = own_all / edges
    gain_part = gain_all / edges
    leave = scale * (own - slots * shift_part - gain_part * ((ysum - slots * shift) / gain))
    normed = spread * (inward + degree * (local[0:1, :] - stat[0:1, :]))
    reach = scale * (inward_grads - degree * shift_part - gain_part * normed)
    return leave, reach, gain_all


def turned(weight):
    width = weight.shape[0] // 2
    return jnp.concatenate([weight[:width] - weight[width:], weight[width:]], axis=1)


def weight_grad(x, leave, reach):
    grads = jnp.concatenate([leave, reach - leave], axis=1)
    middle = column_sum(x) / x.shape[0]
    level = lax.dot_general(
        jnp.broadcast_to(middle, (8, x.shape[1])) * 0.125,
        jnp.broadcast_to(column_sum(grads), (8, grads.shape[1])),
        (((0,), (0,)), ((), ())),
        precision=lax.Precision.HIGHEST,
        preferred_element_type=jnp.float32,
    )
    return product(x - middle, grads, 0, 0) + level


def total_of(refs):
    total = refs[0][...]
    for ref in refs[1:]:
        total = total + ref[...]
    return total


def middle_kernel(
    edges, slots, count, me_ref, own_ref, ysum_ref, in_ref, deg_ref, local_ref, stat_ref, sums_ref,
    small_ref, x_ref, weight_ref, inv_ref, slope_ref, moment_ref, *refs,
):
    wgrad = refs[-1]
    scaled_ref, next_ref, gain_out_ref = refs[-4:-1]
    reached, parts = refs[: -4 - count], refs[-4 - count : -4]
    leave, reach, gain_all = point_grads(
        edges, slots, own_ref[...], total_of(reached), ysum_ref[...], in_ref[...], deg_ref[:, 0:1],
        local_ref[...], stat_ref[...], sums_ref[...], small_ref[2:3, :], small_ref[3:4, :],
    )
    gain_out_ref[...] = gain_all
    width, outs = x_ref.shape[1], leave.shape[1]
    both = weight_grad(x_ref[...], leave, reach)
    wgrad[0:width, :] = both[:, :outs]
    wgrad[width:, :] = both[:, outs:]
    grad = product(jnp.concatenate([leave, reach], axis=1), turned(weight_ref[...]), 1, 1)
    own = grad * slope_ref[...]
    scaled_ref[...] = grad * inv_ref[...]
    next_ref[...] = own
    own_sum = column_sum(own)
    moment_sum = column_sum(grad * moment_ref[...])
    me = me_ref[0]
    piece = 2 * width // count
    for mask, part in enumerate(parts):
        start = pl.multiple_of((me ^ mask) * piece, piece)
        part[0:piece, :] = wgrad[pl.ds(start, piece), :]
        part[piece:, :] = jnp.zeros((8, outs), jnp.float32)
        part[piece : piece + 1, 0:width] = own_sum
        part[piece + 1 : piece + 2, 0:width] = moment_sum


def middle(
    edges, slots, count, me, own, ysum, inward, degree, local, stat, sums, small, x, weight,
    inv, slope, moment, reached,
):
    points, width = x.shape
    outs = weight.shape[1]
    operands = (own, ysum, inward, degree, local, stat, sums, small, x, weight, inv, slope, moment)
    results = pl.pallas_call(
        functools.partial(middle_kernel, edges, slots, count),
        in_specs=[SMEM] + [pl.BlockSpec(memory_space=pltpu.VMEM)] * (len(operands) + len(reached)),
        out_shape=[f32(2 * width // count + 8, outs)] * count
        + [f32(points, width), f32(points, width), f32(1, outs)],
        scratch_shapes=[pltpu.VMEM((2 * width, outs), jnp.float32)],
        compiler_params=params(32),
        name="middle",
    )(me, *operands, *reached)
    return results[:count], *results[count:]


def last_kernel(
    edges, slots, count, own_ref, ysum_ref, in_ref, deg_ref, local_ref, stat_ref, joined_ref,
    small_ref, x_ref, weight_ref, *refs,
):
    reached, (gain_out_ref, wgrad_ref), parts = (
        refs[: -2 - count],
        refs[-2 - count : -count],
        refs[-count:],
    )
    width, outs = weight_ref.shape[0] // 2, weight_ref.shape[1]
    piece = joined_ref.shape[0] - 8
    leave, reach, gain_all = point_grads(
        edges, slots, own_ref[...], total_of(reached), ysum_ref[...], in_ref[...], deg_ref[:, 0:1],
        local_ref[...], stat_ref[...], joined_ref[piece : piece + 2, 0:outs],
        small_ref[0:1, 0:outs], small_ref[1:2, 0:outs],
    )
    gain_out_ref[...] = gain_all
    wgrad_ref[...] = weight_grad(x_ref[:, 0:width], leave, reach)
    grad = product(turned(weight_ref[...]), jnp.concatenate([leave, reach], axis=1), 1, 1)
    rows = grad.shape[1] // count
    for m, part in enumerate(parts):
        part[0:width, :] = grad[:, m * rows : (m + 1) * rows]
        part[width:, :] = joined_ref[0:piece, :]


def last(
    edges, slots, count, own, ysum, inward, degree, local, stat, joined, small, x, weight, reached
):
    points = x.shape[0]
    width, outs = weight.shape[0] // 2, weight.shape[1]
    lanes = points // count
    assert lanes == 2 * outs == joined.shape[1]
    results = pl.pallas_call(
        functools.partial(last_kernel, edges, slots, count),
        out_shape=[f32(1, outs), f32(width, 2 * outs)] + [f32(width + joined.shape[0] - 8, lanes)] * count,
        compiler_params=params(32),
        name="last",
    )(own, ysum, inward, degree, local, stat, joined, small, x, weight, *reached)
    return results[0], results[1], results[2:]


def body(
    features,
    neighbours_one,
    neighbours_two,
    weight_one,
    gain_one,
    shift_one,
    weight_two,
    gain_two,
    shift_two,
    grad_act,
    grad_max,
    grad_mean,
):
    clouds, rows, width = features.shape
    slots = neighbours_one.shape[1]
    count = lax.axis_size("pts")
    assert clouds == count
    points = rows * count
    local_edges = points * slots
    edges = float(local_edges * lax.axis_size(BOTH))
    me = lax.axis_index("pts").astype(jnp.int32).reshape(1)
    def to_owner(parts):
        return [parts[0]] + [exchange(part, "pts", m) for m, part in enumerate(parts) if m]

    with jax.named_scope("bring_clouds"):
        parts, small, (weight_one, weight_two) = pack(
            me, features, neighbours_one, neighbours_two,
            (gain_one, shift_one, gain_two, shift_two), (weight_one, weight_two),
        )
        parts = to_owner(parts)
        firsts = (width, width + slots)
        early = [part_links(part, firsts, slots, points) for part in parts[: count // 2]]
    with jax.named_scope("bring_cotangents"):
        acts = to_owner(split(me, grad_act))

    with jax.named_scope("layer_one"):
        x, ids, a_one, b_one, in_one, deg_one, local_one = first_tables(
            parts, [links[0] for links in early], weight_one, slots
        )
        late = [part_links(part, firsts[1:], slots, points) for part in parts[count // 2 :]]
        links = [links[-1] for links in early + late]
        stat_one = join_stats(local_one, local_edges)
        hidden, share_one, inv_one, slope_one, moment_one, ysum_one = edge_forward(
            edges, 0, slots, width, 128, x, a_one, b_one, stat_one, small
        )
    with jax.named_scope("layer_two"):
        a_two, b_two, in_two, deg_two, local_two = second_tables(hidden, weight_two, links, slots)
        stat_two = join_stats(local_two, local_edges)
        out, share_two, inv_two, slope_two, moment_two, ysum_two = edge_forward(
            edges, 1, slots, width + slots, 128, x, a_two, b_two, stat_two, small
        )
    with jax.named_scope("pools"):
        out_parts, scaled_two, own_two = pools(
            me, out, inv_two, slope_two, moment_two, grad_max, grad_mean, acts
        )
        out_parts = to_owner(out_parts)
        output, pool_max, pool_mean = unpack_output(me, out_parts)

    cut = 4 * (3 * slots // 20)
    with jax.named_scope("layer_two_back"):
        sums_two, reached = sum_beside(
            lambda received: pair_sum([part[rows + 2 : rows + 4] for part in received]),
            out_parts,
            [
                lambda ready: scatter(ids, slots, scaled_two, share_two, 0, cut, 4),
                lambda ready: scatter(ids, slots, after(scaled_two, ready), share_two, cut, slots, 4),
            ],
        )
        wgrad_parts, scaled_one, own_one, gain_grad_two = middle(
            edges, slots, count, me, own_two, ysum_two, in_two, deg_two, local_two, stat_two, sums_two,
            small, hidden, weight_two, inv_one, slope_one, moment_one, reached,
        )
    with jax.named_scope("layer_one_back"):
        joined, reached = sum_beside(
            lambda received: pair_sum(list(received)),
            to_owner(wgrad_parts),
            [
                lambda ready: scatter(ids, 0, scaled_one, share_one, 0, cut, 4),
                lambda ready: scatter(ids, 0, after(scaled_one, ready), share_one, cut, slots, 4),
            ],
        )
        gain_grad_one, wgrad_one, grad_parts = last(
            edges, slots, count, own_one, ysum_one, in_one, deg_one, local_one, stat_one, joined,
            small, x, weight_one, reached,
        )
        wgrad_one = pair_sum(to_owner([wgrad_one] * count))
        wgrad_one, *grad_parts = lax.optimization_barrier((wgrad_one, *grad_parts))
        grad_parts = to_owner(grad_parts)
        wgrad_one = sum_stages(wgrad_one, list(stages())[1:])
        wgrad_one = jnp.concatenate(jnp.split(wgrad_one, 2, axis=1), axis=0)
        grad_features, wgrad_two = unpack_grad(me, grad_parts, width)
    return (
        output,
        pool_max,
        pool_mean,
        jnp.swapaxes(grad_features, 1, 2),
        wgrad_one,
        gain_grad_one.reshape(-1),
        joined[-8, : weight_one.shape[1]],
        wgrad_two,
        gain_grad_two.reshape(-1),
        sums_two[0],
    )


def solution(mesh):
    placed = (
        P("clouds", "pts", None),
        P("clouds", None, "pts"),
        P("clouds", None, "pts"),
        P(),
        P(),
        P(),
        P(),
        P(),
        P(),
        P("clouds", "pts", None),
        P("clouds", None),
        P("clouds", None),
    )
    return jax.shard_map(
        body,
        mesh=mesh,
        in_specs=placed,
        out_specs=(
            P("clouds", "pts", None),
            P("clouds", None),
            P("clouds", None),
            P("clouds", "pts", None),
            P(),
            P(),
            P(),
            P(),
            P(),
            P(),
        ),
        check_vma=False,
    )
```

```python
import functools

import jax
import jax.numpy as jnp
from jax import lax
from jax.experimental import pallas as pl
from jax.experimental.pallas import tpu as pltpu
from jax.sharding import PartitionSpec as P

norm_eps = 1e-05
LOG2E = 1.4426950408889634
BOTH = ("clouds", "pts")
MIB = 2**20
SMALL = jnp.float8_e4m3fn


def f32(*shape):
    return jax.ShapeDtypeStruct(shape, jnp.float32)


def in_hbm(*shape):
    return pltpu.HBM(shape, jnp.float32)


def from_hbm(x):
    return pltpu.with_memory_space_constraint(x, pltpu.HBM)


def params(mib):
    return pltpu.CompilerParams(vmem_limit_bytes=mib * MIB)


SMEM = pl.BlockSpec(memory_space=pltpu.SMEM)
VMEM = pl.BlockSpec(memory_space=pltpu.VMEM)


def exchange(x, axes, mask):
    size = lax.axis_size(axes)
    return lax.ppermute(x, axes, [(i, i ^ mask) for i in range(size)])


def bit_groups(size):
    bits = [1 << i for i in range(size.bit_length() - 1)]
    groups = [bits[:1]] if bits else []
    rest = bits[1:]
    while rest:
        groups.append(rest[:2])
        rest = rest[2:]
    return groups


def stages():
    yield "pts", list(range(1, lax.axis_size("pts")))
    for bits in bit_groups(lax.axis_size("clouds")):
        masks = [0]
        for bit in bits:
            masks = masks + [mask | bit for mask in masks]
        yield "clouds", masks[1:]


def swap(x, axes, masks):
    return [x] + [exchange(x, axes, mask) for mask in masks]


def pair_sum(values):
    while len(values) > 1:
        values = [values[i] + values[i + 1] for i in range(0, len(values), 2)]
    return values[0]


def sum_stages(x, cloud_stages):
    for axis, masks in cloud_stages:
        x = pair_sum(swap(x, axis, masks))
    return x


def after(value, *others):
    return lax.optimization_barrier((value, *others))[0]


def sum_beside(message, received, work):
    (axis, masks), *rest = list(stages())[:0:-1]
    first = work[0](None)
    total = message(lax.optimization_barrier((*received, first))[:-1])
    moving = swap(total, axis, masks)
    second = work[1](total)
    total = pair_sum(list(lax.optimization_barrier((*moving, second))[:-1]))
    return sum_stages(total, rest), [first, second]


def join_stats(stat, count):
    for axis, masks in stages():
        parts = swap(stat, axis, masks)
        mean = pair_sum([part[0:1] for part in parts]) / len(parts)
        away = pair_sum([(part[0:1] - mean) ** 2 for part in parts])
        stat = jnp.concatenate([mean, pair_sum([part[1:2] for part in parts]) + count * away], axis=0)
        count = count * len(parts)
    return stat


def pack_kernel(slots, me_ref, *refs):
    sources, outs, fetched, sems = refs[:9], refs[9:-10], refs[-10:-1], refs[-1]
    parts, small_ref, weights = outs[:-3], outs[-3], outs[-2:]
    copies = [
        pltpu.make_async_copy(source, target, sems.at[i])
        for i, (source, target) in enumerate(zip(sources, fetched))
    ]
    for copy in copies:
        copy.start()
    for copy in copies:
        copy.wait()
    feat_ref, one_ref, two_ref = fetched[:3]
    me = me_ref[0]
    width, rows = feat_ref.shape[1], feat_ref.shape[2]
    for mask, out in enumerate(parts):
        cloud = me ^ mask
        out[0:width, :] = feat_ref[cloud]
        for k in range(slots):
            for at, ids in ((width, one_ref), (width + slots, two_ref)):
                row = ids[k, pl.ds(cloud, 1), :] ^ (cloud * rows)
                out[at + k : at + k + 1, :] = row.astype(jnp.float32)
    small_ref[...] = jnp.zeros_like(small_ref)
    for i, vector in enumerate(fetched[3:7]):
        small_ref[i : i + 1, 0 : vector.shape[1]] = vector[...]
    for kept, weight in zip(weights, fetched[7:9]):
        kept[...] = weight[...]


def pack(me, features, neighbours_one, neighbours_two, vectors, weights):
    clouds, rows, width = features.shape
    slots = neighbours_one.shape[1]
    operands = (
        jnp.swapaxes(features, 1, 2),
        jnp.swapaxes(neighbours_one, 0, 1),
        jnp.swapaxes(neighbours_two, 0, 1),
        *(v.reshape(1, -1) for v in vectors),
        *weights,
    )
    results = pl.pallas_call(
        functools.partial(pack_kernel, slots),
        in_specs=[SMEM] + [pl.BlockSpec(memory_space=pltpu.HBM)] * len(operands),
        out_shape=[f32(width + 2 * slots, rows)] * clouds
        + [f32(8, max(v.shape[0] for v in vectors))]
        + [f32(*w.shape) for w in weights],
        scratch_shapes=[pltpu.VMEM(v.shape, v.dtype) for v in operands]
        + [pltpu.SemaphoreType.DMA((len(operands),))],
        compiler_params=params(8),
        name="pack",
    )(me, *(from_hbm(v) for v in operands))
    return results[:clouds], results[clouds], results[clouds + 1 :]


def split_kernel(me_ref, x_ref, *outs):
    me = me_ref[0]
    for mask, out in enumerate(outs):
        out[...] = x_ref[me ^ mask]


def split(me, x):
    clouds, rows, width = x.shape
    return pl.pallas_call(
        split_kernel,
        in_specs=[SMEM, VMEM],
        out_shape=[f32(rows, width)] * clouds,
        compiler_params=params(16),
        name="split",
    )(me, from_hbm(x))


def unpack_output_kernel(rows, me_ref, *refs):
    parts, (act_ref, max_ref, mean_ref) = refs[:-3], refs[-3:]
    me = me_ref[0]
    for mask, part in enumerate(parts):
        cloud = me ^ mask
        act_ref[cloud] = part[0:rows]
        max_ref[pl.ds(cloud, 1), :] = part[rows : rows + 1]
        mean_ref[pl.ds(cloud, 1), :] = part[rows + 1 : rows + 2]


def unpack_output(me, parts):
    clouds, width = len(parts), parts[0].shape[1]
    rows = parts[0].shape[0] - 8
    return pl.pallas_call(
        functools.partial(unpack_output_kernel, rows),
        in_specs=[SMEM] + [VMEM] * clouds,
        out_shape=[f32(clouds, rows, width), f32(clouds, width), f32(clouds, width)],
        compiler_params=params(16),
        name="unpack_output",
    )(me, *parts)


def unpack_grad_kernel(me_ref, *refs):
    parts, (grad_ref, wgrad_ref) = refs[:-2], refs[-2:]
    me = me_ref[0]
    width = grad_ref.shape[1]
    piece = wgrad_ref.shape[0] // len(parts)
    for mask, part in enumerate(parts):
        other = me ^ mask
        grad_ref[other] = part[0:width]
        wgrad_ref[pl.ds(pl.multiple_of(other * piece, piece), piece), :] = part[width:]


def unpack_grad(me, parts, width):
    rows, lanes = parts[0].shape
    count = len(parts)
    return pl.pallas_call(
        unpack_grad_kernel,
        in_specs=[SMEM] + [VMEM] * count,
        out_shape=[f32(count, width, lanes), f32(count * (rows - width), lanes)],
        compiler_params=params(16),
        name="unpack_grad",
    )(me, *parts)


def two_terms(x):
    high = x.astype(jnp.bfloat16)
    low = (x - high.astype(jnp.float32)).astype(jnp.bfloat16)
    return jnp.concatenate([high, low], axis=1)


def halves_sum(x):
    half = x.shape[1] // 2
    return x[:, :half] + x[:, half:]


def product(x, y, on_x, on_y):
    x_high, y_high = x.astype(jnp.bfloat16), y.astype(jnp.bfloat16)
    x_low = (x - x_high.astype(jnp.float32)).astype(jnp.bfloat16)
    y_low = (y - y_high.astype(jnp.float32)).astype(jnp.bfloat16)
    return lax.dot_general(
        jnp.concatenate([x_high, x_low, x_high], axis=on_x),
        jnp.concatenate([y_high, y_high, y_low], axis=on_y),
        (((on_x,), (on_y,)), ((), ())),
        preferred_element_type=jnp.float32,
    )


def column_sum(x):
    return jnp.sum(x, axis=0, keepdims=True)


def count_links(ids_ref, first, slots, wide, links):
    points, columns = links.shape
    block, rows, groups = 256, 16, 4
    here = lax.broadcasted_iota(jnp.int32, (rows, columns), 0).astype(jnp.bfloat16)
    one = jnp.ones((rows, columns), jnp.bfloat16)
    zero = jnp.zeros((rows, columns), jnp.bfloat16)
    for start in range(0, points, block):
        for k in range(slots):
            local = ids_ref[first + k : first + k + 1, :] - float(start)
            wide[k] = jnp.broadcast_to(local, (rows, columns)).astype(jnp.bfloat16)

        def some(step, carry):
            base = step * (rows * groups)
            names = [here + (base + g * rows).astype(jnp.float32).astype(jnp.bfloat16) for g in range(groups)]
            totals = [zero] * groups
            for k in range(slots):
                ids = wide[k]
                totals = [
                    total + jnp.where(ids == name, one, zero) for total, name in zip(totals, names)
                ]
            for g in range(groups):
                at = pl.ds(pl.multiple_of(start + base + g * rows, rows), rows)
                links[at, :] = totals[g]
            return carry

        lax.fori_loop(0, block // (rows * groups), some, 0)


def links_kernel(firsts, slots, ids_ref, *refs):
    wide = refs[-1]
    for first, links in zip(firsts, refs[:-1]):
        count_links(ids_ref, first, slots, wide, links)


def part_links(part, firsts, slots, points):
    columns = part.shape[1]
    edges = len(firsts) * slots * points * columns
    return pl.pallas_call(
        functools.partial(links_kernel, firsts, slots),
        out_shape=[jax.ShapeDtypeStruct((points, columns), jnp.bfloat16)] * len(firsts),
        scratch_shapes=[pltpu.VMEM((slots, 16, columns), jnp.bfloat16)],
        compiler_params=params(8),
        cost_estimate=pl.CostEstimate(
            flops=100 * edges, bytes_accessed=2 * points * columns, transcendentals=0
        ),
        name="part_links",
    )(part)


def table_stats(x, weight, links, slots, a_ref, b_ref, in_ref, deg_ref, stat_ref):
    points, width = x.shape
    outs = weight.shape[1]
    upper, lower = weight[:width], weight[width:]
    joined = jnp.concatenate([upper - lower, lower], axis=1)
    middle = column_sum(x) / points
    level = jnp.dot(
        jnp.broadcast_to(middle, (8, width)), joined, precision=lax.Precision.HIGHEST
    )
    both = product(x - middle, joined, 1, 0) + level[0:1]
    a, b = both[:, :outs], both[:, outs:]
    mean_a = column_sum(a) / points
    a_off = a - mean_a
    terms = two_terms(a_off)
    seen = degree = 0.0
    for m, part in enumerate(links):
        columns = part.shape[1]
        some = terms[m * columns : (m + 1) * columns]
        seen = seen + jnp.dot(part[...], some, preferred_element_type=jnp.float32)
        degree = degree + jnp.sum(part[...].astype(jnp.float32), axis=1, keepdims=True)
    seen = halves_sum(seen)
    mean_b = column_sum(degree * b) / (points * slots)
    b_off = b - mean_b
    inward = seen + degree * b_off
    a_ref[...] = a
    b_ref[...] = b
    in_ref[...] = inward
    deg_ref[...] = jnp.broadcast_to(degree, deg_ref.shape)
    stat_ref[0:1, :] = mean_a + mean_b
    stat_ref[1:2, :] = slots * column_sum(a_off * a_off) + column_sum((seen + inward) * b_off)


def first_kernel(slots, width, count, *refs):
    parts, early, (weight_ref, x_ref, ids_ref, a_ref, b_ref, in_ref, deg_ref, stat_ref, *late, wide) = (
        refs[:count],
        refs[count : count + count // 2],
        refs[count + count // 2 :],
    )
    rows = parts[0].shape[1]
    fill = jnp.zeros((128 - parts[0].shape[0], rows), jnp.float32)
    for m, part in enumerate(parts):
        ids_ref[:, m * rows : (m + 1) * rows] = part[width:, :]
        x_ref[m * rows : (m + 1) * rows, :] = jnp.concatenate([part[...], fill], axis=0).T
    for part, links in zip(parts[len(early) :], late):
        count_links(part, width, slots, wide, links)
    table_stats(
        x_ref[:, :width], weight_ref[...], (*early, *late), slots, a_ref, b_ref, in_ref, deg_ref, stat_ref
    )


def first_tables(parts, early, weight, slots):
    count, columns = len(parts), parts[0].shape[1]
    points = count * columns
    width, outs = weight.shape[0] // 2, weight.shape[1]
    return pl.pallas_call(
        functools.partial(first_kernel, slots, width, count),
        out_shape=[
            f32(points, 128),
            f32(2 * slots, points),
            f32(points, outs),
            f32(points, outs),
            f32(points, outs),
            f32(points, 128),
            f32(2, outs),
        ],
        scratch_shapes=[pltpu.VMEM((points, columns), jnp.bfloat16)] * (count - len(early))
        + [pltpu.VMEM((slots, 16, columns), jnp.bfloat16)],
        compiler_params=params(24),
        name="first_tables",
    )(*parts, *early, weight)


def second_kernel(slots, x_ref, weight_ref, *refs):
    links, outs = refs[:-5], refs[-5:]
    table_stats(x_ref[...], weight_ref[...], links, slots, *outs)


def second_tables(x, weight, links, slots):
    points, outs = x.shape[0], weight.shape[1]
    return pl.pallas_call(
        functools.partial(second_kernel, slots),
        out_shape=[
            f32(points, outs),
            f32(points, outs),
            f32(points, outs),
            f32(points, 128),
            f32(2, outs),
        ],
        compiler_params=params(24),
        name="second_tables",
    )(x, weight, *links)


def edge_kernel(
    edges, layer, slots, first, tile, x_ref, a_ref, b_ref, stat_ref, small_ref,
    out_ref, weight_ref, inv_ref, slope_ref, moment_ref, ysum_ref, table, centre, held, bounded,
):
    points, width = a_ref.shape
    step = pl.program_id(0)
    block = 8

    @pl.when(step == 0)
    def _():
        gain = small_ref[2 * layer : 2 * layer + 1, 0:width]
        shift = small_ref[2 * layer + 1 : 2 * layer + 2, 0:width]
        scale = gain * lax.rsqrt(stat_ref[1:2, :] / edges + norm_eps) * -LOG2E
        middle = column_sum(b_ref[...]) / points
        there = (b_ref[...] - middle) * scale
        here = (a_ref[...] + (middle - stat_ref[0:1, :])) * scale - shift * LOG2E
        table[...] = two_terms(there)
        centre[...] = here
        reach = jnp.max(jnp.abs(here), axis=0, keepdims=True) + jnp.max(
            jnp.abs(there), axis=0, keepdims=True
        )
        bounded[0] = (jnp.max(reach) < 60.0).astype(jnp.int32)

    rows = pl.ds(pl.multiple_of(step * tile, tile), tile)
    columns = lax.broadcasted_iota(jnp.int32, (tile, points), 1).astype(jnp.float32)

    def gather(ids):
        pick = jnp.where(ids == columns, 1.0, 0.0).astype(jnp.bfloat16)
        return jnp.dot(pick, table[...], preferred_element_type=jnp.float32)

    def finish(at, top, totals):
        mass, slope, moment, total = totals
        out_ref[at, :] = top + jnp.log(mass)
        inv = 0.8 / mass
        inv_ref[at, :] = inv
        slope_ref[at, :] = slope * inv
        moment_ref[at, :] = moment * inv * (-1.0 / LOG2E)
        ysum_ref[at, :] = total * (-1.0 / LOG2E)

    @pl.when(bounded[0] == 1)
    def _():
        found = [gather(x_ref[rows, first + k : first + k + 1]) for k in range(slots)]
        for start in range(0, tile, block):
            at = slice(start, start + block)
            here = centre[pl.ds(pl.multiple_of(step * tile + start, block), block), :]
            totals = [jnp.zeros((block, width), jnp.float32)] * 4
            for k in range(slots):
                t = here + halves_sum(found[k][at])
                grown = 1.0 + jnp.exp2(t)
                fall = jnp.exp2((-0.2 * LOG2E) * jnp.log(grown) - t)
                share = grown * fall
                part = fall + 0.25 * share
                weight_ref[k, at, :] = part
                totals = [total + term for total, term in zip(totals, (share, part, part * t, t))]
            finish(at, 0.0, totals)

    @pl.when(bounded[0] == 0)
    def _():
        lanes = lax.broadcasted_iota(jnp.int32, (tile, x_ref.shape[1]), 1)

        def collect(k, carry):
            ids = jnp.sum(jnp.where(lanes == first + k, x_ref[rows, :], 0.0), axis=1, keepdims=True)
            held[k] = centre[rows, :] + halves_sum(gather(ids))
            return carry

        lax.fori_loop(0, slots, collect, 0)

        def rise(t):
            grown = 1.0 + jnp.exp2(jnp.minimum(t, 64.0))
            return jnp.maximum((0.8 * LOG2E) * jnp.log(grown), 0.8 * t) - t, grown

        def some(b, carry):
            at = pl.ds(pl.multiple_of(b * block, block), block)
            low = held[0, at, :]
            for k in range(1, slots):
                low = jnp.minimum(low, held[k, at, :])
            peak, _ = rise(low)
            totals = [jnp.zeros((block, width), jnp.float32)] * 4
            for k in range(slots):
                t = held[k, at, :]
                level, grown = rise(t)
                share = jnp.exp2(level - peak)
                part = share * (1.0 / grown + 0.25)
                weight_ref[k, at, :] = part
                totals = [total + term for total, term in zip(totals, (share, part, part * t, t))]
            finish(at, peak * (1.0 / LOG2E), totals)
            return carry

        lax.fori_loop(0, tile // block, some, 0)


def edge_forward(edges, layer, slots, first, tile, x, a, b, stat, small):
    points, width = a.shape
    some = pl.BlockSpec((tile, width), lambda step: (step, 0))
    return pl.pallas_call(
        functools.partial(edge_kernel, edges, layer, slots, first, tile),
        grid=(points // tile,),
        in_specs=[VMEM] * 5,
        out_specs=[some, pl.BlockSpec((slots, tile, width), lambda step: (0, step, 0))] + [some] * 4,
        out_shape=[f32(points, width), in_hbm(slots, points, width)] + [f32(points, width)] * 4,
        scratch_shapes=[
            pltpu.VMEM((points, 2 * width), jnp.bfloat16),
            pltpu.VMEM((points, width), jnp.float32),
            pltpu.VMEM((slots, tile, width), jnp.float32),
            pltpu.SMEM((1,), jnp.int32),
        ],
        compiler_params=params(24),
        name="edges",
    )(x, a, b, stat, small)


def pool_kernel(me_ref, out_ref, inv_ref, slope_ref, moment_ref, gmax_ref, gmean_ref, *refs):
    count = (len(refs) - 3) // 2
    acts, parts = refs[:count], refs[count : 2 * count]
    scaled_ref, own_ref, largest_ref = refs[2 * count :]
    me = me_ref[0]
    points, width = out_ref.shape
    rows = points // count
    out = out_ref[...]
    top = jnp.max(out, axis=0, keepdims=True)
    pool = top + jnp.log(column_sum(jnp.exp(out - top)))
    mean = column_sum(out) / points
    to_max = gmax_ref[pl.ds(me, 1), :]
    to_mean = gmean_ref[pl.ds(me, 1), :] / points
    own_sum = moment_sum = largest = jnp.zeros((1, width), jnp.float32)
    for m in range(count):
        here = slice(m * rows, (m + 1) * rows)
        part = out[here]
        parts[m][0:rows, :] = part
        parts[m][rows : rows + 1, :] = pool
        parts[m][rows + 1 : rows + 2, :] = mean
        parts[m][rows + 4 : rows + 8, :] = jnp.zeros((4, width), jnp.float32)
        grad = acts[m][...] + to_max * jnp.exp(part - pool) + to_mean
        own = grad * slope_ref[here, :]
        scaled_ref[here, :] = grad * inv_ref[here, :]
        own_ref[here, :] = own
        own_sum = own_sum + column_sum(own)
        moment_sum = moment_sum + column_sum(grad * moment_ref[here, :])
        largest = jnp.maximum(largest, jnp.max(jnp.abs(grad), axis=0, keepdims=True))
    largest_ref[...] = largest
    for m in range(count):
        parts[m][rows + 2 : rows + 3, :] = own_sum
        parts[m][rows + 3 : rows + 4, :] = moment_sum


def pools(me, out, inv, slope, moment, grad_max, grad_mean, acts):
    points, width = out.shape
    count = len(acts)
    rows = points // count
    results = pl.pallas_call(
        pool_kernel,
        in_specs=[SMEM] + [VMEM] * (6 + count),
        out_shape=[f32(rows + 8, width)] * count + [f32(points, width)] * 2 + [f32(1, width)],
        compiler_params=params(16),
        name="pools",
    )(me, out, inv, slope, moment, grad_max, grad_mean, *acts)
    return results[:count], *results[count:]


def scatter_kernel(first, group, small_rest, ids_ref, grad_ref, largest_ref, weight_ref, sum_ref):
    step = pl.program_id(0)
    points, width = grad_ref.shape
    rows = lax.broadcasted_iota(jnp.int32, (points, points), 0).astype(jnp.float32)
    scale = 2.0**16 / jnp.maximum(largest_ref[...], 1e-30)
    picks, small_picks, terms, rests = [], [], [], []
    for g in range(group):
        here = ids_ref[pl.ds(first + step * group + g, 1), :] == rows
        value = grad_ref[...] * weight_ref[g]
        picks.append(jnp.where(here, 1.0, 0.0).astype(jnp.bfloat16))
        if small_rest:
            high = value.astype(jnp.bfloat16)
            terms.append(high)
            small_picks.append(jnp.where(here, SMALL(1), SMALL(0)))
            rests.append(((value - high.astype(jnp.float32)) * scale).astype(SMALL))
        else:
            terms.append(two_terms(value))

    def found(picks, terms):
        return jnp.dot(
            jnp.concatenate(picks, axis=1),
            jnp.concatenate(terms, axis=0),
            preferred_element_type=jnp.float32,
        )

    if small_rest:
        total = found(picks, terms) + found(small_picks, rests) * (1.0 / scale)
    else:
        total = halves_sum(found(picks, terms))

    @pl.when(step == 0)
    def _():
        sum_ref[...] = total

    @pl.when(step > 0)
    def _():
        sum_ref[...] += total


def scatter(ids, first, grad, largest, weight, start, stop, group):
    points, width = grad.shape
    edges = (stop - start) * points
    return pl.pallas_call(
        functools.partial(scatter_kernel, first + start, group, width >= 256),
        grid=((stop - start) // group,),
        in_specs=[
            VMEM,
            VMEM,
            VMEM,
            pl.BlockSpec((group, points, width), lambda step: (start // group + step, 0, 0)),
        ],
        out_specs=VMEM,
        out_shape=f32(points, width),
        compiler_params=params(36),
        cost_estimate=pl.CostEstimate(
            flops=4 * edges * points * width, bytes_accessed=4 * edges * width, transcendentals=0
        ),
        name="scatter",
    )(ids, grad, largest, from_hbm(weight))


def point_grads(edges, slots, own, inward_grads, ysum, inward, degree, local, stat, sums, gain, shift):
    inward_grads = inward_grads + (column_sum(own) - column_sum(inward_grads)) / own.shape[0]
    spread = lax.rsqrt(stat[1:2, :] / edges + norm_eps)
    scale = gain * spread
    own_all = sums[0:1, :]
    gain_all = (sums[1:2, :] - shift * own_all) / gain
    shift_part = own_all / edges
    gain_part = gain_all / edges
    leave = scale * (own - slots * shift_part - gain_part * ((ysum - slots * shift) / gain))
    normed = spread * (inward + degree * (local[0:1, :] - stat[0:1, :]))
    reach = scale * (inward_grads - degree * shift_part - gain_part * normed)
    return leave, reach, gain_all


def turned(weight):
    width = weight.shape[0] // 2
    return jnp.concatenate([weight[:width] - weight[width:], weight[width:]], axis=1)


def weight_grad(x, leave, reach):
    middle = column_sum(x) / x.shape[0]
    level = lax.dot_general(
        jnp.broadcast_to(middle, (8, x.shape[1])) * 0.125,
        jnp.broadcast_to(column_sum(leave), (8, leave.shape[1])),
        (((0,), (0,)), ((), ())),
        precision=lax.Precision.HIGHEST,
        preferred_element_type=jnp.float32,
    )
    level = jnp.concatenate([level, jnp.zeros_like(level)], axis=1)
    return product(x - middle, jnp.concatenate([leave, reach - leave], axis=1), 0, 0) + level


def total_of(refs):
    total = refs[0][...]
    for ref in refs[1:]:
        total = total + ref[...]
    return total


def middle_kernel(
    edges, slots, count, me_ref, own_ref, ysum_ref, in_ref, deg_ref, local_ref, stat_ref, sums_ref,
    small_ref, x_ref, weight_ref, inv_ref, slope_ref, moment_ref, *refs,
):
    wgrad = refs[-1]
    scaled_ref, next_ref, gain_out_ref = refs[-4:-1]
    reached, parts = refs[: -4 - count], refs[-4 - count : -4]
    leave, reach, gain_all = point_grads(
        edges, slots, own_ref[...], total_of(reached), ysum_ref[...], in_ref[...], deg_ref[:, 0:1],
        local_ref[...], stat_ref[...], sums_ref[...], small_ref[2:3, :], small_ref[3:4, :],
    )
    gain_out_ref[...] = gain_all
    width, outs = x_ref.shape[1], leave.shape[1]
    both = weight_grad(x_ref[...], leave, reach)
    wgrad[0:width, :] = both[:, :outs]
    wgrad[width:, :] = both[:, outs:]
    grad = product(jnp.concatenate([leave, reach], axis=1), turned(weight_ref[...]), 1, 1)
    own = grad * slope_ref[...]
    scaled_ref[...] = grad * inv_ref[...]
    next_ref[...] = own
    own_sum = column_sum(own)
    moment_sum = column_sum(grad * moment_ref[...])
    me = me_ref[0]
    piece = 2 * width // count
    for mask, part in enumerate(parts):
        start = pl.multiple_of((me ^ mask) * piece, piece)
        part[0:piece, :] = wgrad[pl.ds(start, piece), :]
        part[piece:, :] = jnp.zeros((8, outs), jnp.float32)
        part[piece : piece + 1, 0:width] = own_sum
        part[piece + 1 : piece + 2, 0:width] = moment_sum


def middle(
    edges, slots, count, me, own, ysum, inward, degree, local, stat, sums, small, x, weight,
    inv, slope, moment, reached,
):
    points, width = x.shape
    outs = weight.shape[1]
    operands = (own, ysum, inward, degree, local, stat, sums, small, x, weight, inv, slope, moment)
    results = pl.pallas_call(
        functools.partial(middle_kernel, edges, slots, count),
        in_specs=[SMEM] + [VMEM] * (len(operands) + len(reached)),
        out_shape=[f32(2 * width // count + 8, outs)] * count
        + [f32(points, width), f32(points, width), f32(1, outs)],
        scratch_shapes=[pltpu.VMEM((2 * width, outs), jnp.float32)],
        compiler_params=params(32),
        name="middle",
    )(me, *operands, *reached)
    return results[:count], *results[count:]


def last_kernel(
    edges, slots, count, own_ref, ysum_ref, in_ref, deg_ref, local_ref, stat_ref, joined_ref,
    small_ref, x_ref, weight_ref, *refs,
):
    reached, (gain_out_ref, wgrad_ref), parts = (
        refs[: -2 - count],
        refs[-2 - count : -count],
        refs[-count:],
    )
    width, outs = weight_ref.shape[0] // 2, weight_ref.shape[1]
    piece = joined_ref.shape[0] - 8
    leave, reach, gain_all = point_grads(
        edges, slots, own_ref[...], total_of(reached), ysum_ref[...], in_ref[...], deg_ref[:, 0:1],
        local_ref[...], stat_ref[...], joined_ref[piece : piece + 2, 0:outs],
        small_ref[0:1, 0:outs], small_ref[1:2, 0:outs],
    )
    gain_out_ref[...] = gain_all
    wgrad_ref[...] = weight_grad(x_ref[:, 0:width], leave, reach)
    grad = product(turned(weight_ref[...]), jnp.concatenate([leave, reach], axis=1), 1, 1)
    rows = grad.shape[1] // count
    for m, part in enumerate(parts):
        part[0:width, :] = grad[:, m * rows : (m + 1) * rows]
        part[width:, :] = joined_ref[0:piece, :]


def last(
    edges, slots, count, own, ysum, inward, degree, local, stat, joined, small, x, weight, reached
):
    points = x.shape[0]
    width, outs = weight.shape[0] // 2, weight.shape[1]
    lanes = points // count
    assert lanes == 2 * outs == joined.shape[1]
    results = pl.pallas_call(
        functools.partial(last_kernel, edges, slots, count),
        out_shape=[f32(1, outs), f32(width, 2 * outs)] + [f32(width + joined.shape[0] - 8, lanes)] * count,
        compiler_params=params(32),
        name="last",
    )(own, ysum, inward, degree, local, stat, joined, small, x, weight, *reached)
    return results[0], results[1], results[2:]


def body(
    features,
    neighbours_one,
    neighbours_two,
    weight_one,
    gain_one,
    shift_one,
    weight_two,
    gain_two,
    shift_two,
    grad_act,
    grad_max,
    grad_mean,
):
    clouds, rows, width = features.shape
    slots = neighbours_one.shape[1]
    count = lax.axis_size("pts")
    assert clouds == count
    points = rows * count
    local_edges = points * slots
    edges = float(local_edges * lax.axis_size(BOTH))
    me = lax.axis_index("pts").astype(jnp.int32).reshape(1)
    def to_owner(parts):
        return [parts[0]] + [exchange(part, "pts", m) for m, part in enumerate(parts) if m]

    with jax.named_scope("bring_clouds"):
        parts, small, (weight_one, weight_two) = pack(
            me, features, neighbours_one, neighbours_two,
            (gain_one, shift_one, gain_two, shift_two), (weight_one, weight_two),
        )
        parts = to_owner(parts)
        firsts = (width, width + slots)
        early = [part_links(part, firsts, slots, points) for part in parts[: count // 2]]
    with jax.named_scope("bring_cotangents"):
        acts = to_owner(split(me, grad_act))

    with jax.named_scope("layer_one"):
        x, ids, a_one, b_one, in_one, deg_one, local_one = first_tables(
            parts, [links[0] for links in early], weight_one, slots
        )
        late = [part_links(part, firsts[1:], slots, points) for part in parts[count // 2 :]]
        links = [links[-1] for links in early + late]
        stat_one = join_stats(local_one, local_edges)
        hidden, share_one, inv_one, slope_one, moment_one, ysum_one = edge_forward(
            edges, 0, slots, width, 128, x, a_one, b_one, stat_one, small
        )
    with jax.named_scope("layer_two"):
        a_two, b_two, in_two, deg_two, local_two = second_tables(hidden, weight_two, links, slots)
        stat_two = join_stats(local_two, local_edges)
        out, share_two, inv_two, slope_two, moment_two, ysum_two = edge_forward(
            edges, 1, slots, width + slots, 128, x, a_two, b_two, stat_two, small
        )
    with jax.named_scope("pools"):
        out_parts, scaled_two, own_two, largest_two = pools(
            me, out, inv_two, slope_two, moment_two, grad_max, grad_mean, acts
        )
        out_parts = to_owner(out_parts)
        output, pool_max, pool_mean = unpack_output(me, out_parts)

    cut = 4 * (3 * slots // 20)
    with jax.named_scope("layer_two_back"):
        sums_two, reached = sum_beside(
            lambda received: pair_sum([part[rows + 2 : rows + 4] for part in received]),
            out_parts,
            [
                lambda ready: scatter(ids, slots, scaled_two, largest_two, share_two, 0, cut, 4),
                lambda ready: scatter(ids, slots, after(scaled_two, ready), largest_two, share_two, cut, slots, 4),
            ],
        )
        wgrad_parts, scaled_one, own_one, gain_grad_two = middle(
            edges, slots, count, me, own_two, ysum_two, in_two, deg_two, local_two, stat_two, sums_two,
            small, hidden, weight_two, inv_one, slope_one, moment_one, reached,
        )
    with jax.named_scope("layer_one_back"):
        joined, reached = sum_beside(
            lambda received: pair_sum(list(received)),
            to_owner(wgrad_parts),
            [
                lambda ready: scatter(ids, 0, scaled_one, scaled_one[:1], share_one, 0, cut, 4),
                lambda ready: scatter(ids, 0, after(scaled_one, ready), scaled_one[:1], share_one, cut, slots, 4),
            ],
        )
        gain_grad_one, wgrad_one, grad_parts = last(
            edges, slots, count, own_one, ysum_one, in_one, deg_one, local_one, stat_one, joined,
            small, x, weight_one, reached,
        )
        wgrad_one = pair_sum(to_owner([wgrad_one] * count))
        wgrad_one, *grad_parts = lax.optimization_barrier((wgrad_one, *grad_parts))
        grad_parts = to_owner(grad_parts)
        wgrad_one = sum_stages(wgrad_one, list(stages())[1:])
        wgrad_one = jnp.concatenate(jnp.split(wgrad_one, 2, axis=1), axis=0)
        grad_features, wgrad_two = unpack_grad(me, grad_parts, width)
    return (
        output,
        pool_max,
        pool_mean,
        jnp.swapaxes(grad_features, 1, 2),
        wgrad_one,
        gain_grad_one.reshape(-1),
        joined[-8, : weight_one.shape[1]],
        wgrad_two,
        gain_grad_two.reshape(-1),
        sums_two[0],
    )


def solution(mesh):
    placed = (
        P("clouds", "pts", None),
        P("clouds", None, "pts"),
        P("clouds", None, "pts"),
        P(),
        P(),
        P(),
        P(),
        P(),
        P(),
        P("clouds", "pts", None),
        P("clouds", None),
        P("clouds", None),
    )
    return jax.shard_map(
        body,
        mesh=mesh,
        in_specs=placed,
        out_specs=(
            P("clouds", "pts", None),
            P("clouds", None),
            P("clouds", None),
            P("clouds", "pts", None),
            P(),
            P(),
            P(),
            P(),
            P(),
            P(),
        ),
        check_vma=False,
    )
```

```python
import functools

import jax
import jax.numpy as jnp
from jax import lax
from jax.experimental import pallas as pl
from jax.experimental.pallas import tpu as pltpu
from jax.sharding import PartitionSpec as P

norm_eps = 1e-05
LOG2E = 1.4426950408889634
BOTH = ("clouds", "pts")
MIB = 2**20
SMALL = jnp.float8_e4m3fn


def f32(*shape):
    return jax.ShapeDtypeStruct(shape, jnp.float32)


def in_hbm(*shape):
    return pltpu.HBM(shape, jnp.float32)


def from_hbm(x):
    return pltpu.with_memory_space_constraint(x, pltpu.HBM)


def params(mib):
    return pltpu.CompilerParams(vmem_limit_bytes=mib * MIB)


SMEM = pl.BlockSpec(memory_space=pltpu.SMEM)
VMEM = pl.BlockSpec(memory_space=pltpu.VMEM)


def exchange(x, axes, mask):
    size = lax.axis_size(axes)
    return lax.ppermute(x, axes, [(i, i ^ mask) for i in range(size)])


def bit_groups(size):
    bits = [1 << i for i in range(size.bit_length() - 1)]
    groups = [bits[:1]] if bits else []
    rest = bits[1:]
    while rest:
        groups.append(rest[:2])
        rest = rest[2:]
    return groups


def stages():
    yield "pts", list(range(1, lax.axis_size("pts")))
    for bits in bit_groups(lax.axis_size("clouds")):
        masks = [0]
        for bit in bits:
            masks = masks + [mask | bit for mask in masks]
        yield "clouds", masks[1:]


def swap(x, axes, masks):
    return [x] + [exchange(x, axes, mask) for mask in masks]


def pair_sum(values):
    while len(values) > 1:
        values = [values[i] + values[i + 1] for i in range(0, len(values), 2)]
    return values[0]


def sum_stages(x, cloud_stages):
    for axis, masks in cloud_stages:
        x = pair_sum(swap(x, axis, masks))
    return x


def after(value, *others):
    return lax.optimization_barrier((value, *others))[0]


def sum_beside(message, received, work):
    cloud_stages = list(stages())[:0:-1]
    done = [work[0](None)]
    total = message(lax.optimization_barrier((*received, done[0]))[:-1])
    for piece, (axis, masks) in zip(work[1:], cloud_stages):
        moving = swap(total, axis, masks)
        done.append(piece(total))
        total = pair_sum(list(lax.optimization_barrier((*moving, done[-1]))[:-1]))
    return sum_stages(total, cloud_stages[len(work) - 1 :]), done


def join_stats(stat, count):
    for axis, masks in stages():
        parts = swap(stat, axis, masks)
        mean = pair_sum([part[0:1] for part in parts]) / len(parts)
        away = pair_sum([(part[0:1] - mean) ** 2 for part in parts])
        stat = jnp.concatenate([mean, pair_sum([part[1:2] for part in parts]) + count * away], axis=0)
        count = count * len(parts)
    return stat


def pack_kernel(slots, me_ref, *refs):
    sources, outs, fetched, sems = refs[:9], refs[9:-10], refs[-10:-1], refs[-1]
    parts, small_ref, weights = outs[:-3], outs[-3], outs[-2:]
    copies = [
        pltpu.make_async_copy(source, target, sems.at[i])
        for i, (source, target) in enumerate(zip(sources, fetched))
    ]
    for copy in copies:
        copy.start()
    for copy in copies:
        copy.wait()
    feat_ref, one_ref, two_ref = fetched[:3]
    me = me_ref[0]
    width, rows = feat_ref.shape[1], feat_ref.shape[2]
    for mask, out in enumerate(parts):
        cloud = me ^ mask
        out[0:width, :] = feat_ref[cloud]
        for k in range(slots):
            for at, ids in ((width, one_ref), (width + slots, two_ref)):
                row = ids[k, pl.ds(cloud, 1), :] ^ (cloud * rows)
                out[at + k : at + k + 1, :] = row.astype(jnp.float32)
    small_ref[...] = jnp.zeros_like(small_ref)
    for i, vector in enumerate(fetched[3:7]):
        small_ref[i : i + 1, 0 : vector.shape[1]] = vector[...]
    for kept, weight in zip(weights, fetched[7:9]):
        kept[...] = weight[...]


def pack(me, features, neighbours_one, neighbours_two, vectors, weights):
    clouds, rows, width = features.shape
    slots = neighbours_one.shape[1]
    operands = (
        jnp.swapaxes(features, 1, 2),
        jnp.swapaxes(neighbours_one, 0, 1),
        jnp.swapaxes(neighbours_two, 0, 1),
        *(v.reshape(1, -1) for v in vectors),
        *weights,
    )
    results = pl.pallas_call(
        functools.partial(pack_kernel, slots),
        in_specs=[SMEM] + [pl.BlockSpec(memory_space=pltpu.HBM)] * len(operands),
        out_shape=[f32(width + 2 * slots, rows)] * clouds
        + [f32(8, max(v.shape[0] for v in vectors))]
        + [f32(*w.shape) for w in weights],
        scratch_shapes=[pltpu.VMEM(v.shape, v.dtype) for v in operands]
        + [pltpu.SemaphoreType.DMA((len(operands),))],
        compiler_params=params(8),
        name="pack",
    )(me, *(from_hbm(v) for v in operands))
    return results[:clouds], results[clouds], results[clouds + 1 :]


def split_kernel(me_ref, x_ref, *outs):
    me = me_ref[0]
    for mask, out in enumerate(outs):
        out[...] = x_ref[me ^ mask]


def split(me, x):
    clouds, rows, width = x.shape
    return pl.pallas_call(
        split_kernel,
        in_specs=[SMEM, VMEM],
        out_shape=[f32(rows, width)] * clouds,
        compiler_params=params(16),
        name="split",
    )(me, from_hbm(x))


def unpack_output_kernel(rows, me_ref, *refs):
    parts, (act_ref, max_ref, mean_ref) = refs[:-3], refs[-3:]
    me = me_ref[0]
    for mask, part in enumerate(parts):
        cloud = me ^ mask
        act_ref[cloud] = part[0:rows]
        max_ref[pl.ds(cloud, 1), :] = part[rows : rows + 1]
        mean_ref[pl.ds(cloud, 1), :] = part[rows + 1 : rows + 2]


def unpack_output(me, parts):
    clouds, width = len(parts), parts[0].shape[1]
    rows = parts[0].shape[0] - 8
    return pl.pallas_call(
        functools.partial(unpack_output_kernel, rows),
        in_specs=[SMEM] + [VMEM] * clouds,
        out_shape=[f32(clouds, rows, width), f32(clouds, width), f32(clouds, width)],
        compiler_params=params(16),
        name="unpack_output",
    )(me, *parts)


def unpack_grad_kernel(me_ref, *refs):
    parts, (grad_ref, wgrad_ref) = refs[:-2], refs[-2:]
    me = me_ref[0]
    width = grad_ref.shape[1]
    piece = wgrad_ref.shape[0] // len(parts)
    for mask, part in enumerate(parts):
        other = me ^ mask
        grad_ref[other] = part[0:width]
        wgrad_ref[pl.ds(pl.multiple_of(other * piece, piece), piece), :] = part[width:]


def unpack_grad(me, parts, width):
    rows, lanes = parts[0].shape
    count = len(parts)
    return pl.pallas_call(
        unpack_grad_kernel,
        in_specs=[SMEM] + [VMEM] * count,
        out_shape=[f32(count, width, lanes), f32(count * (rows - width), lanes)],
        compiler_params=params(16),
        name="unpack_grad",
    )(me, *parts)


def two_terms(x):
    high = x.astype(jnp.bfloat16)
    low = (x - high.astype(jnp.float32)).astype(jnp.bfloat16)
    return jnp.concatenate([high, low], axis=1)


def halves_sum(x):
    half = x.shape[1] // 2
    return x[:, :half] + x[:, half:]


def terms_of(x):
    high = x.astype(jnp.bfloat16)
    return high, (x - high.astype(jnp.float32)).astype(jnp.bfloat16)


def term_product(x_terms, y_terms, on_x, on_y):
    (x_high, x_low), (y_high, y_low) = x_terms, y_terms
    return lax.dot_general(
        jnp.concatenate([x_high, x_low, x_high], axis=on_x),
        jnp.concatenate([y_high, y_high, y_low], axis=on_y),
        (((on_x,), (on_y,)), ((), ())),
        preferred_element_type=jnp.float32,
    )


def product(x, y, on_x, on_y):
    return term_product(terms_of(x), terms_of(y), on_x, on_y)


def column_sum(x):
    return jnp.sum(x, axis=0, keepdims=True)


def count_links(ids_ref, first, slots, wide, links):
    points, columns = links.shape
    block, rows, groups = 256, 16, 4
    here = lax.broadcasted_iota(jnp.int32, (rows, columns), 0).astype(jnp.bfloat16)
    one = jnp.ones((rows, columns), jnp.bfloat16)
    zero = jnp.zeros((rows, columns), jnp.bfloat16)
    for start in range(0, points, block):
        for k in range(slots):
            local = ids_ref[first + k : first + k + 1, :] - float(start)
            wide[k] = jnp.broadcast_to(local, (rows, columns)).astype(jnp.bfloat16)

        def some(step, carry):
            base = step * (rows * groups)
            names = [here + (base + g * rows).astype(jnp.float32).astype(jnp.bfloat16) for g in range(groups)]
            totals = [zero] * groups
            for k in range(slots):
                ids = wide[k]
                totals = [
                    total + jnp.where(ids == name, one, zero) for total, name in zip(totals, names)
                ]
            for g in range(groups):
                at = pl.ds(pl.multiple_of(start + base + g * rows, rows), rows)
                links[at, :] = totals[g]
            return carry

        lax.fori_loop(0, block // (rows * groups), some, 0)


def links_kernel(firsts, slots, ids_ref, *refs):
    wide = refs[-1]
    for first, links in zip(firsts, refs[:-1]):
        count_links(ids_ref, first, slots, wide, links)


def part_links(part, firsts, slots, points):
    columns = part.shape[1]
    edges = len(firsts) * slots * points * columns
    return pl.pallas_call(
        functools.partial(links_kernel, firsts, slots),
        out_shape=[jax.ShapeDtypeStruct((points, columns), jnp.bfloat16)] * len(firsts),
        scratch_shapes=[pltpu.VMEM((slots, 16, columns), jnp.bfloat16)],
        compiler_params=params(8),
        cost_estimate=pl.CostEstimate(
            flops=100 * edges, bytes_accessed=2 * points * columns, transcendentals=0
        ),
        name="part_links",
    )(part)


def table_stats(x, weight, links, slots, a_ref, b_ref, in_ref, deg_ref, stat_ref):
    points, width = x.shape
    outs = weight.shape[1]
    upper, lower = weight[:width], weight[width:]
    joined = jnp.concatenate([upper - lower, lower], axis=1)
    middle = column_sum(x) / points
    level = jnp.dot(
        jnp.broadcast_to(middle, (8, width)), joined, precision=lax.Precision.HIGHEST
    )
    both = product(x - middle, joined, 1, 0) + level[0:1]
    a, b = both[:, :outs], both[:, outs:]
    mean_a = column_sum(a) / points
    a_off = a - mean_a
    terms = two_terms(a_off)
    seen = degree = 0.0
    for m, part in enumerate(links):
        columns = part.shape[1]
        some = terms[m * columns : (m + 1) * columns]
        seen = seen + jnp.dot(part[...], some, preferred_element_type=jnp.float32)
        degree = degree + jnp.sum(part[...].astype(jnp.float32), axis=1, keepdims=True)
    seen = halves_sum(seen)
    mean_b = column_sum(degree * b) / (points * slots)
    b_off = b - mean_b
    inward = seen + degree * b_off
    a_ref[...] = a
    b_ref[...] = b
    in_ref[...] = inward
    deg_ref[...] = jnp.broadcast_to(degree, deg_ref.shape)
    stat_ref[0:1, :] = mean_a + mean_b
    stat_ref[1:2, :] = slots * column_sum(a_off * a_off) + column_sum((seen + inward) * b_off)


def first_kernel(slots, width, count, *refs):
    parts, early, (weight_ref, x_ref, ids_ref, a_ref, b_ref, in_ref, deg_ref, stat_ref, *late, wide) = (
        refs[:count],
        refs[count : count + count // 2],
        refs[count + count // 2 :],
    )
    rows = parts[0].shape[1]
    fill = jnp.zeros((128 - parts[0].shape[0], rows), jnp.float32)
    for m, part in enumerate(parts):
        ids_ref[:, m * rows : (m + 1) * rows] = part[width:, :]
        x_ref[m * rows : (m + 1) * rows, :] = jnp.concatenate([part[...], fill], axis=0).T
    for part, links in zip(parts[len(early) :], late):
        count_links(part, width, slots, wide, links)
    table_stats(
        x_ref[:, :width], weight_ref[...], (*early, *late), slots, a_ref, b_ref, in_ref, deg_ref, stat_ref
    )


def first_tables(parts, early, weight, slots):
    count, columns = len(parts), parts[0].shape[1]
    points = count * columns
    width, outs = weight.shape[0] // 2, weight.shape[1]
    return pl.pallas_call(
        functools.partial(first_kernel, slots, width, count),
        out_shape=[
            f32(points, 128),
            f32(2 * slots, points),
            f32(points, outs),
            f32(points, outs),
            f32(points, outs),
            f32(points, 128),
            f32(2, outs),
        ],
        scratch_shapes=[pltpu.VMEM((points, columns), jnp.bfloat16)] * (count - len(early))
        + [pltpu.VMEM((slots, 16, columns), jnp.bfloat16)],
        compiler_params=params(24),
        name="first_tables",
    )(*parts, *early, weight)


def second_kernel(slots, x_ref, weight_ref, *refs):
    links, outs = refs[:-5], refs[-5:]
    table_stats(x_ref[...], weight_ref[...], links, slots, *outs)


def second_tables(x, weight, links, slots):
    points, outs = x.shape[0], weight.shape[1]
    return pl.pallas_call(
        functools.partial(second_kernel, slots),
        out_shape=[
            f32(points, outs),
            f32(points, outs),
            f32(points, outs),
            f32(points, 128),
            f32(2, outs),
        ],
        compiler_params=params(24),
        name="second_tables",
    )(x, weight, *links)


def edge_kernel(
    edges, layer, slots, first, tile, x_ref, a_ref, b_ref, stat_ref, small_ref,
    out_ref, weight_ref, inv_ref, slope_ref, moment_ref, ysum_ref, table, centre, held, bounded,
):
    points, width = a_ref.shape
    step = pl.program_id(0)
    block = 8

    @pl.when(step == 0)
    def _():
        gain = small_ref[2 * layer : 2 * layer + 1, 0:width]
        shift = small_ref[2 * layer + 1 : 2 * layer + 2, 0:width]
        scale = gain * lax.rsqrt(stat_ref[1:2, :] / edges + norm_eps) * -LOG2E
        middle = column_sum(b_ref[...]) / points
        there = (b_ref[...] - middle) * scale
        here = (a_ref[...] + (middle - stat_ref[0:1, :])) * scale - shift * LOG2E
        table[...] = two_terms(there)
        centre[...] = here
        reach = jnp.max(jnp.abs(here), axis=0, keepdims=True) + jnp.max(
            jnp.abs(there), axis=0, keepdims=True
        )
        bounded[0] = (jnp.max(reach) < 60.0).astype(jnp.int32)

    rows = pl.ds(pl.multiple_of(step * tile, tile), tile)
    columns = lax.broadcasted_iota(jnp.int32, (tile, points), 1).astype(jnp.float32)

    def gather(ids):
        pick = jnp.where(ids == columns, 1.0, 0.0).astype(jnp.bfloat16)
        return jnp.dot(pick, table[...], preferred_element_type=jnp.float32)

    def finish(at, top, totals):
        mass, slope, moment, total = totals
        out_ref[at, :] = top + jnp.log(mass)
        inv = 0.8 / mass
        inv_ref[at, :] = inv
        slope_ref[at, :] = slope * inv
        moment_ref[at, :] = moment * inv * (-1.0 / LOG2E)
        ysum_ref[at, :] = total * (-1.0 / LOG2E)

    @pl.when(bounded[0] == 1)
    def _():
        found = [gather(x_ref[rows, first + k : first + k + 1]) for k in range(slots)]
        for start in range(0, tile, block):
            at = slice(start, start + block)
            here = centre[pl.ds(pl.multiple_of(step * tile + start, block), block), :]
            totals = [jnp.zeros((block, width), jnp.float32)] * 4
            for k in range(slots):
                t = here + halves_sum(found[k][at])
                grown = 1.0 + jnp.exp2(t)
                fall = jnp.exp2((-0.2 * LOG2E) * jnp.log(grown) - t)
                share = grown * fall
                part = fall + 0.25 * share
                weight_ref[k, at, :] = part
                totals = [total + term for total, term in zip(totals, (share, part, part * t, t))]
            finish(at, 0.0, totals)

    @pl.when(bounded[0] == 0)
    def _():
        lanes = lax.broadcasted_iota(jnp.int32, (tile, x_ref.shape[1]), 1)

        def collect(k, carry):
            ids = jnp.sum(jnp.where(lanes == first + k, x_ref[rows, :], 0.0), axis=1, keepdims=True)
            held[k] = centre[rows, :] + halves_sum(gather(ids))
            return carry

        lax.fori_loop(0, slots, collect, 0)

        def rise(t):
            grown = 1.0 + jnp.exp2(jnp.minimum(t, 64.0))
            return jnp.maximum((0.8 * LOG2E) * jnp.log(grown), 0.8 * t) - t, grown

        def some(b, carry):
            at = pl.ds(pl.multiple_of(b * block, block), block)
            low = held[0, at, :]
            for k in range(1, slots):
                low = jnp.minimum(low, held[k, at, :])
            peak, _ = rise(low)
            totals = [jnp.zeros((block, width), jnp.float32)] * 4
            for k in range(slots):
                t = held[k, at, :]
                level, grown = rise(t)
                share = jnp.exp2(level - peak)
                part = share * (1.0 / grown + 0.25)
                weight_ref[k, at, :] = part
                totals = [total + term for total, term in zip(totals, (share, part, part * t, t))]
            finish(at, peak * (1.0 / LOG2E), totals)
            return carry

        lax.fori_loop(0, tile // block, some, 0)


def edge_forward(edges, layer, slots, first, tile, x, a, b, stat, small):
    points, width = a.shape
    some = pl.BlockSpec((tile, width), lambda step: (step, 0))
    return pl.pallas_call(
        functools.partial(edge_kernel, edges, layer, slots, first, tile),
        grid=(points // tile,),
        in_specs=[VMEM] * 5,
        out_specs=[some, pl.BlockSpec((slots, tile, width), lambda step: (0, step, 0))] + [some] * 4,
        out_shape=[f32(points, width), in_hbm(slots, points, width)] + [f32(points, width)] * 4,
        scratch_shapes=[
            pltpu.VMEM((points, 2 * width), jnp.bfloat16),
            pltpu.VMEM((points, width), jnp.float32),
            pltpu.VMEM((slots, tile, width), jnp.float32),
            pltpu.SMEM((1,), jnp.int32),
        ],
        compiler_params=params(24),
        name="edges",
    )(x, a, b, stat, small)


def pool_kernel(me_ref, out_ref, inv_ref, slope_ref, moment_ref, gmax_ref, gmean_ref, *refs):
    count = (len(refs) - 3) // 2
    acts, parts = refs[:count], refs[count : 2 * count]
    scaled_ref, own_ref, largest_ref = refs[2 * count :]
    me = me_ref[0]
    points, width = out_ref.shape
    rows = points // count
    out = out_ref[...]
    top = jnp.max(out, axis=0, keepdims=True)
    pool = top + jnp.log(column_sum(jnp.exp(out - top)))
    mean = column_sum(out) / points
    to_max = gmax_ref[pl.ds(me, 1), :]
    to_mean = gmean_ref[pl.ds(me, 1), :] / points
    own_sum = moment_sum = largest = jnp.zeros((1, width), jnp.float32)
    for m in range(count):
        here = slice(m * rows, (m + 1) * rows)
        part = out[here]
        parts[m][0:rows, :] = part
        parts[m][rows : rows + 1, :] = pool
        parts[m][rows + 1 : rows + 2, :] = mean
        parts[m][rows + 4 : rows + 8, :] = jnp.zeros((4, width), jnp.float32)
        grad = acts[m][...] + to_max * jnp.exp(part - pool) + to_mean
        own = grad * slope_ref[here, :]
        scaled_ref[here, :] = grad * inv_ref[here, :]
        own_ref[here, :] = own
        own_sum = own_sum + column_sum(own)
        moment_sum = moment_sum + column_sum(grad * moment_ref[here, :])
        largest = jnp.maximum(largest, jnp.max(jnp.abs(grad), axis=0, keepdims=True))
    largest_ref[...] = largest
    for m in range(count):
        parts[m][rows + 2 : rows + 3, :] = own_sum
        parts[m][rows + 3 : rows + 4, :] = moment_sum


def pools(me, out, inv, slope, moment, grad_max, grad_mean, acts):
    points, width = out.shape
    count = len(acts)
    rows = points // count
    results = pl.pallas_call(
        pool_kernel,
        in_specs=[SMEM] + [VMEM] * (6 + count),
        out_shape=[f32(rows + 8, width)] * count + [f32(points, width)] * 2 + [f32(1, width)],
        compiler_params=params(16),
        name="pools",
    )(me, out, inv, slope, moment, grad_max, grad_mean, *acts)
    return results[:count], *results[count:]


def scatter_kernel(first, group, small_rest, ids_ref, grad_ref, largest_ref, weight_ref, sum_ref):
    step = pl.program_id(0)
    points, width = grad_ref.shape
    rows = lax.broadcasted_iota(jnp.int32, (points, points), 0).astype(jnp.float32)
    scale = 2.0**16 / jnp.maximum(largest_ref[...], 1e-30)
    picks, small_picks, terms, rests = [], [], [], []
    for g in range(group):
        here = ids_ref[pl.ds(first + step * group + g, 1), :] == rows
        value = grad_ref[...] * weight_ref[g]
        picks.append(jnp.where(here, 1.0, 0.0).astype(jnp.bfloat16))
        if small_rest:
            high = value.astype(jnp.bfloat16)
            terms.append(high)
            small_picks.append(jnp.where(here, SMALL(1), SMALL(0)))
            rests.append(((value - high.astype(jnp.float32)) * scale).astype(SMALL))
        else:
            terms.append(two_terms(value))

    def found(picks, terms):
        return jnp.dot(
            jnp.concatenate(picks, axis=1),
            jnp.concatenate(terms, axis=0),
            preferred_element_type=jnp.float32,
        )

    if small_rest:
        total = found(picks, terms) + found(small_picks, rests) * (1.0 / scale)
    else:
        total = halves_sum(found(picks, terms))

    @pl.when(step == 0)
    def _():
        sum_ref[...] = total

    @pl.when(step > 0)
    def _():
        sum_ref[...] += total


def scatter(ids, first, grad, largest, weight, start, stop, group):
    points, width = grad.shape
    edges = (stop - start) * points
    return pl.pallas_call(
        functools.partial(scatter_kernel, first + start, group, width >= 256),
        grid=((stop - start) // group,),
        in_specs=[
            VMEM,
            VMEM,
            VMEM,
            pl.BlockSpec((group, points, width), lambda step: (start // group + step, 0, 0)),
        ],
        out_specs=VMEM,
        out_shape=f32(points, width),
        compiler_params=params(36),
        cost_estimate=pl.CostEstimate(
            flops=4 * edges * points * width, bytes_accessed=4 * edges * width, transcendentals=0
        ),
        name="scatter",
    )(ids, grad, largest, from_hbm(weight))


def point_grads(edges, slots, own, inward_grads, ysum, inward, degree, local, stat, sums, gain, shift):
    inward_grads = inward_grads + (column_sum(own) - column_sum(inward_grads)) / own.shape[0]
    spread = lax.rsqrt(stat[1:2, :] / edges + norm_eps)
    scale = gain * spread
    own_all = sums[0:1, :]
    gain_all = (sums[1:2, :] - shift * own_all) / gain
    shift_part = own_all / edges
    gain_part = gain_all / edges
    leave = scale * (own - slots * shift_part - gain_part * ((ysum - slots * shift) / gain))
    normed = spread * (inward + degree * (local[0:1, :] - stat[0:1, :]))
    reach = scale * (inward_grads - degree * shift_part - gain_part * normed)
    return leave, reach, gain_all


def turned(weight):
    width = weight.shape[0] // 2
    return jnp.concatenate([weight[:width] - weight[width:], weight[width:]], axis=1)


def weight_grad(x, leave, pair_terms):
    middle = column_sum(x) / x.shape[0]
    level = lax.dot_general(
        jnp.broadcast_to(middle, (8, x.shape[1])) * 0.125,
        jnp.broadcast_to(column_sum(leave), (8, leave.shape[1])),
        (((0,), (0,)), ((), ())),
        precision=lax.Precision.HIGHEST,
        preferred_element_type=jnp.float32,
    )
    both = term_product(terms_of(x - middle), pair_terms, 0, 0)
    outs = leave.shape[1]
    return both[:, :outs] + level, both[:, outs:] - both[:, :outs]


def total_of(refs):
    total = refs[0][...]
    for ref in refs[1:]:
        total = total + ref[...]
    return total


def middle_kernel(
    edges, slots, count, me_ref, own_ref, ysum_ref, in_ref, deg_ref, local_ref, stat_ref, sums_ref,
    small_ref, x_ref, weight_ref, inv_ref, slope_ref, moment_ref, *refs,
):
    wgrad = refs[-1]
    scaled_ref, next_ref, gain_out_ref = refs[-4:-1]
    reached, parts = refs[: -4 - count], refs[-4 - count : -4]
    leave, reach, gain_all = point_grads(
        edges, slots, own_ref[...], total_of(reached), ysum_ref[...], in_ref[...], deg_ref[:, 0:1],
        local_ref[...], stat_ref[...], sums_ref[...], small_ref[2:3, :], small_ref[3:4, :],
    )
    gain_out_ref[...] = gain_all
    width, outs = x_ref.shape[1], leave.shape[1]
    pair_terms = terms_of(jnp.concatenate([leave, reach], axis=1))
    wgrad[0:width, :], wgrad[width:, :] = weight_grad(x_ref[...], leave, pair_terms)
    grad = term_product(pair_terms, terms_of(turned(weight_ref[...])), 1, 1)
    own = grad * slope_ref[...]
    scaled_ref[...] = grad * inv_ref[...]
    next_ref[...] = own
    own_sum = column_sum(own)
    moment_sum = column_sum(grad * moment_ref[...])
    me = me_ref[0]
    piece = 2 * width // count
    for mask, part in enumerate(parts):
        start = pl.multiple_of((me ^ mask) * piece, piece)
        part[0:piece, :] = wgrad[pl.ds(start, piece), :]
        part[piece:, :] = jnp.zeros((8, outs), jnp.float32)
        part[piece : piece + 1, 0:width] = own_sum
        part[piece + 1 : piece + 2, 0:width] = moment_sum


def middle(
    edges, slots, count, me, own, ysum, inward, degree, local, stat, sums, small, x, weight,
    inv, slope, moment, reached,
):
    points, width = x.shape
    outs = weight.shape[1]
    operands = (own, ysum, inward, degree, local, stat, sums, small, x, weight, inv, slope, moment)
    results = pl.pallas_call(
        functools.partial(middle_kernel, edges, slots, count),
        in_specs=[SMEM] + [VMEM] * (len(operands) + len(reached)),
        out_shape=[f32(2 * width // count + 8, outs)] * count
        + [f32(points, width), f32(points, width), f32(1, outs)],
        scratch_shapes=[pltpu.VMEM((2 * width, outs), jnp.float32)],
        compiler_params=params(32),
        name="middle",
    )(me, *operands, *reached)
    return results[:count], *results[count:]


def last_kernel(
    edges, slots, count, own_ref, ysum_ref, in_ref, deg_ref, local_ref, stat_ref, joined_ref,
    small_ref, x_ref, weight_ref, *refs,
):
    reached, (gain_out_ref, wgrad_ref), parts = (
        refs[: -2 - count],
        refs[-2 - count : -count],
        refs[-count:],
    )
    width, outs = weight_ref.shape[0] // 2, weight_ref.shape[1]
    piece = joined_ref.shape[0] - 8
    leave, reach, gain_all = point_grads(
        edges, slots, own_ref[...], total_of(reached), ysum_ref[...], in_ref[...], deg_ref[:, 0:1],
        local_ref[...], stat_ref[...], joined_ref[piece : piece + 2, 0:outs],
        small_ref[0:1, 0:outs], small_ref[1:2, 0:outs],
    )
    gain_out_ref[...] = gain_all
    pair_terms = terms_of(jnp.concatenate([leave, reach], axis=1))
    wgrad_ref[:, :outs], wgrad_ref[:, outs:] = weight_grad(x_ref[:, 0:width], leave, pair_terms)
    grad = term_product(terms_of(turned(weight_ref[...])), pair_terms, 1, 1)
    rows = grad.shape[1] // count
    for m, part in enumerate(parts):
        part[0:width, :] = grad[:, m * rows : (m + 1) * rows]
        part[width:, :] = joined_ref[0:piece, :]


def last(
    edges, slots, count, own, ysum, inward, degree, local, stat, joined, small, x, weight, reached
):
    points = x.shape[0]
    width, outs = weight.shape[0] // 2, weight.shape[1]
    lanes = points // count
    assert lanes == 2 * outs == joined.shape[1]
    results = pl.pallas_call(
        functools.partial(last_kernel, edges, slots, count),
        out_shape=[f32(1, outs), f32(width, 2 * outs)] + [f32(width + joined.shape[0] - 8, lanes)] * count,
        compiler_params=params(32),
        name="last",
    )(own, ysum, inward, degree, local, stat, joined, small, x, weight, *reached)
    return results[0], results[1], results[2:]


def body(
    features,
    neighbours_one,
    neighbours_two,
    weight_one,
    gain_one,
    shift_one,
    weight_two,
    gain_two,
    shift_two,
    grad_act,
    grad_max,
    grad_mean,
):
    clouds, rows, width = features.shape
    slots = neighbours_one.shape[1]
    count = lax.axis_size("pts")
    assert clouds == count
    points = rows * count
    local_edges = points * slots
    edges = float(local_edges * lax.axis_size(BOTH))
    me = lax.axis_index("pts").astype(jnp.int32).reshape(1)
    def to_owner(parts):
        return [parts[0]] + [exchange(part, "pts", m) for m, part in enumerate(parts) if m]

    with jax.named_scope("bring_clouds"):
        parts, small, (weight_one, weight_two) = pack(
            me, features, neighbours_one, neighbours_two,
            (gain_one, shift_one, gain_two, shift_two), (weight_one, weight_two),
        )
        parts = to_owner(parts)
        firsts = (width, width + slots)
        early = [part_links(part, firsts, slots, points) for part in parts[: count // 2]]
    with jax.named_scope("bring_cotangents"):
        acts = to_owner(split(me, grad_act))

    with jax.named_scope("layer_one"):
        x, ids, a_one, b_one, in_one, deg_one, local_one = first_tables(
            parts, [links[0] for links in early], weight_one, slots
        )
        late = [part_links(part, firsts[1:], slots, points) for part in parts[count // 2 :]]
        links = [links[-1] for links in early + late]
        stat_one = join_stats(local_one, local_edges)
        hidden, share_one, inv_one, slope_one, moment_one, ysum_one = edge_forward(
            edges, 0, slots, width, 128, x, a_one, b_one, stat_one, small
        )
    with jax.named_scope("layer_two"):
        a_two, b_two, in_two, deg_two, local_two = second_tables(hidden, weight_two, links, slots)
        stat_two = join_stats(local_two, local_edges)
        out, share_two, inv_two, slope_two, moment_two, ysum_two = edge_forward(
            edges, 1, slots, width + slots, 128, x, a_two, b_two, stat_two, small
        )
    with jax.named_scope("pools"):
        out_parts, scaled_two, own_two, largest_two = pools(
            me, out, inv_two, slope_two, moment_two, grad_max, grad_mean, acts
        )
        out_parts = to_owner(out_parts)
        output, pool_max, pool_mean = unpack_output(me, out_parts)

    def pieces(first, scaled, largest, share, *cuts):
        def piece(start, stop):
            return lambda ready: scatter(
                ids, first, scaled if ready is None else after(scaled, ready), largest, share, start, stop, 4
            )

        return [piece(*cut) for cut in zip((0, *cuts), (*cuts, slots))]

    with jax.named_scope("layer_two_back"):
        sums_two, reached = sum_beside(
            lambda received: pair_sum([part[rows + 2 : rows + 4] for part in received]),
            out_parts,
            pieces(slots, scaled_two, largest_two, share_two, slots - 8),
        )
        wgrad_parts, scaled_one, own_one, gain_grad_two = middle(
            edges, slots, count, me, own_two, ysum_two, in_two, deg_two, local_two, stat_two, sums_two,
            small, hidden, weight_two, inv_one, slope_one, moment_one, reached,
        )
    with jax.named_scope("layer_one_back"):
        joined, reached = sum_beside(
            lambda received: pair_sum(list(received)),
            to_owner(wgrad_parts),
            pieces(0, scaled_one, scaled_one[:1], share_one, slots - 12, slots - 4),
        )
        gain_grad_one, wgrad_one, grad_parts = last(
            edges, slots, count, own_one, ysum_one, in_one, deg_one, local_one, stat_one, joined,
            small, x, weight_one, reached,
        )
        wgrad_one = pair_sum(to_owner([wgrad_one] * count))
        wgrad_one, *grad_parts = lax.optimization_barrier((wgrad_one, *grad_parts))
        grad_parts = to_owner(grad_parts)
        wgrad_one = sum_stages(wgrad_one, list(stages())[1:])
        wgrad_one = jnp.concatenate(jnp.split(wgrad_one, 2, axis=1), axis=0)
        grad_features, wgrad_two = unpack_grad(me, grad_parts, width)
    return (
        output,
        pool_max,
        pool_mean,
        jnp.swapaxes(grad_features, 1, 2),
        wgrad_one,
        gain_grad_one.reshape(-1),
        joined[-8, : weight_one.shape[1]],
        wgrad_two,
        gain_grad_two.reshape(-1),
        sums_two[0],
    )


def solution(mesh):
    placed = (
        P("clouds", "pts", None),
        P("clouds", None, "pts"),
        P("clouds", None, "pts"),
        P(),
        P(),
        P(),
        P(),
        P(),
        P(),
        P("clouds", "pts", None),
        P("clouds", None),
        P("clouds", None),
    )
    return jax.shard_map(
        body,
        mesh=mesh,
        in_specs=placed,
        out_specs=(
            P("clouds", "pts", None),
            P("clouds", None),
            P("clouds", None),
            P("clouds", "pts", None),
            P(),
            P(),
            P(),
            P(),
            P(),
            P(),
        ),
        check_vma=False,
    )
```

```python
import functools

import jax
import jax.numpy as jnp
from jax import lax
from jax.experimental import pallas as pl
from jax.experimental.pallas import tpu as pltpu
from jax.sharding import PartitionSpec as P

norm_eps = 1e-05
LOG2E = 1.4426950408889634
BOTH = ("clouds", "pts")
MIB = 2**20
SMALL = jnp.float8_e4m3fn


def f32(*shape):
    return jax.ShapeDtypeStruct(shape, jnp.float32)


def in_hbm(*shape):
    return pltpu.HBM(shape, jnp.float32)


def in_vmem(*shape):
    return pltpu.VMEM(shape, jnp.float32)


def from_hbm(x):
    return pltpu.with_memory_space_constraint(x, pltpu.HBM)


def params(mib):
    return pltpu.CompilerParams(vmem_limit_bytes=mib * MIB)


SMEM = pl.BlockSpec(memory_space=pltpu.SMEM)
VMEM = pl.BlockSpec(memory_space=pltpu.VMEM)


def exchange(x, axes, mask):
    size = lax.axis_size(axes)
    return lax.ppermute(x, axes, [(i, i ^ mask) for i in range(size)])


def bit_groups(size):
    bits = [1 << i for i in range(size.bit_length() - 1)]
    groups = [bits[:1]] if bits else []
    rest = bits[1:]
    while rest:
        groups.append(rest[:2])
        rest = rest[2:]
    return groups


def stages():
    yield "pts", list(range(1, lax.axis_size("pts")))
    for bits in bit_groups(lax.axis_size("clouds")):
        masks = [0]
        for bit in bits:
            masks = masks + [mask | bit for mask in masks]
        yield "clouds", masks[1:]


def swap(x, axes, masks):
    return [x] + [exchange(x, axes, mask) for mask in masks]


def pair_sum(values):
    while len(values) > 1:
        values = [values[i] + values[i + 1] for i in range(0, len(values), 2)]
    return values[0]


def sum_stages(x, cloud_stages):
    for axis, masks in cloud_stages:
        x = pair_sum(swap(x, axis, masks))
    return x


def after(value, *others):
    return lax.optimization_barrier((value, *others))[0]


def sum_beside(message, received, work):
    cloud_stages = list(stages())[:0:-1]
    done = [work[0](None)]
    total = message(lax.optimization_barrier((*received, done[0]))[:-1])
    for piece, (axis, masks) in zip(work[1:], cloud_stages):
        moving = swap(total, axis, masks)
        done.append(piece(total))
        total = pair_sum(list(lax.optimization_barrier((*moving, done[-1]))[:-1]))
    return sum_stages(total, cloud_stages[len(work) - 1 :]), done


def join_stats(stat, count):
    for axis, masks in stages():
        parts = swap(stat, axis, masks)
        mean = pair_sum([part[0:1] for part in parts]) / len(parts)
        away = pair_sum([(part[0:1] - mean) ** 2 for part in parts])
        stat = jnp.concatenate([mean, pair_sum([part[1:2] for part in parts]) + count * away], axis=0)
        count = count * len(parts)
    return stat


def pack_kernel(slots, me_ref, *refs):
    sources, outs, fetched, sems = refs[:9], refs[9:-10], refs[-10:-1], refs[-1]
    parts, small_ref, weights = outs[:-3], outs[-3], outs[-2:]
    copies = [
        pltpu.make_async_copy(source, target, sems.at[i])
        for i, (source, target) in enumerate(zip(sources, fetched))
    ]
    for copy in copies:
        copy.start()
    for copy in copies:
        copy.wait()
    feat_ref, one_ref, two_ref = fetched[:3]
    me = me_ref[0]
    width, rows = feat_ref.shape[1], feat_ref.shape[2]
    for mask, out in enumerate(parts):
        cloud = me ^ mask
        out[0:width, :] = feat_ref[cloud]
        for k in range(slots):
            for at, ids in ((width, one_ref), (width + slots, two_ref)):
                row = ids[k, pl.ds(cloud, 1), :] ^ (cloud * rows)
                out[at + k : at + k + 1, :] = row.astype(jnp.float32)
    small_ref[...] = jnp.zeros_like(small_ref)
    for i, vector in enumerate(fetched[3:7]):
        small_ref[i : i + 1, 0 : vector.shape[1]] = vector[...]
    for kept, weight in zip(weights, fetched[7:9]):
        kept[...] = weight[...]


def pack(me, features, neighbours_one, neighbours_two, vectors, weights):
    clouds, rows, width = features.shape
    slots = neighbours_one.shape[1]
    operands = (
        jnp.swapaxes(features, 1, 2),
        jnp.swapaxes(neighbours_one, 0, 1),
        jnp.swapaxes(neighbours_two, 0, 1),
        *(v.reshape(1, -1) for v in vectors),
        *weights,
    )
    results = pl.pallas_call(
        functools.partial(pack_kernel, slots),
        in_specs=[SMEM] + [pl.BlockSpec(memory_space=pltpu.HBM)] * len(operands),
        out_shape=[f32(width + 2 * slots, rows)] * clouds
        + [f32(8, max(v.shape[0] for v in vectors))]
        + [f32(*w.shape) for w in weights],
        scratch_shapes=[pltpu.VMEM(v.shape, v.dtype) for v in operands]
        + [pltpu.SemaphoreType.DMA((len(operands),))],
        compiler_params=params(8),
        name="pack",
    )(me, *(from_hbm(v) for v in operands))
    return results[:clouds], results[clouds], results[clouds + 1 :]


def split_kernel(me_ref, x_ref, *outs):
    me = me_ref[0]
    for mask, out in enumerate(outs):
        out[...] = x_ref[me ^ mask]


def split(me, x):
    clouds, rows, width = x.shape
    return pl.pallas_call(
        split_kernel,
        in_specs=[SMEM, VMEM],
        out_shape=[f32(rows, width)] * clouds,
        compiler_params=params(16),
        name="split",
    )(me, from_hbm(x))


def unpack_output_kernel(rows, me_ref, *refs):
    parts, (act_ref, max_ref, mean_ref) = refs[:-3], refs[-3:]
    me = me_ref[0]
    for mask, part in enumerate(parts):
        cloud = me ^ mask
        act_ref[cloud] = part[0:rows]
        max_ref[pl.ds(cloud, 1), :] = part[rows : rows + 1]
        mean_ref[pl.ds(cloud, 1), :] = part[rows + 1 : rows + 2]


def unpack_output(me, parts):
    clouds, width = len(parts), parts[0].shape[1]
    rows = parts[0].shape[0] - 8
    return pl.pallas_call(
        functools.partial(unpack_output_kernel, rows),
        in_specs=[SMEM] + [VMEM] * clouds,
        out_shape=[f32(clouds, rows, width), f32(clouds, width), f32(clouds, width)],
        compiler_params=params(16),
        name="unpack_output",
    )(me, *parts)


def unpack_grad_kernel(me_ref, *refs):
    parts, (grad_ref, wgrad_ref) = refs[:-2], refs[-2:]
    me = me_ref[0]
    width = grad_ref.shape[1]
    piece = wgrad_ref.shape[0] // len(parts)
    for mask, part in enumerate(parts):
        other = me ^ mask
        grad_ref[other] = part[0:width]
        wgrad_ref[pl.ds(pl.multiple_of(other * piece, piece), piece), :] = part[width:]


def unpack_grad(me, parts, width):
    rows, lanes = parts[0].shape
    count = len(parts)
    return pl.pallas_call(
        unpack_grad_kernel,
        in_specs=[SMEM] + [VMEM] * count,
        out_shape=[f32(count, width, lanes), f32(count * (rows - width), lanes)],
        compiler_params=params(16),
        name="unpack_grad",
    )(me, *parts)


def two_terms(x):
    high = x.astype(jnp.bfloat16)
    low = (x - high.astype(jnp.float32)).astype(jnp.bfloat16)
    return jnp.concatenate([high, low], axis=1)


def halves_sum(x):
    half = x.shape[1] // 2
    return x[:, :half] + x[:, half:]


def terms_of(x):
    high = x.astype(jnp.bfloat16)
    return high, (x - high.astype(jnp.float32)).astype(jnp.bfloat16)


def term_product(x_terms, y_terms, on_x, on_y):
    (x_high, x_low), (y_high, y_low) = x_terms, y_terms
    return lax.dot_general(
        jnp.concatenate([x_high, x_low, x_high], axis=on_x),
        jnp.concatenate([y_high, y_high, y_low], axis=on_y),
        (((on_x,), (on_y,)), ((), ())),
        preferred_element_type=jnp.float32,
    )


def product(x, y, on_x, on_y):
    return term_product(terms_of(x), terms_of(y), on_x, on_y)


def column_sum(x):
    return jnp.sum(x, axis=0, keepdims=True)


def count_links(ids_ref, first, slots, wide, links):
    points, columns = links.shape
    block, rows, groups = 256, 16, 4
    here = lax.broadcasted_iota(jnp.int32, (rows, columns), 0).astype(jnp.bfloat16)
    one = jnp.ones((rows, columns), jnp.bfloat16)
    zero = jnp.zeros((rows, columns), jnp.bfloat16)
    for start in range(0, points, block):
        for k in range(slots):
            local = ids_ref[first + k : first + k + 1, :] - float(start)
            wide[k] = jnp.broadcast_to(local, (rows, columns)).astype(jnp.bfloat16)

        def some(step, carry):
            base = step * (rows * groups)
            names = [here + (base + g * rows).astype(jnp.float32).astype(jnp.bfloat16) for g in range(groups)]
            totals = [zero] * groups
            for k in range(slots):
                ids = wide[k]
                totals = [
                    total + jnp.where(ids == name, one, zero) for total, name in zip(totals, names)
                ]
            for g in range(groups):
                at = pl.ds(pl.multiple_of(start + base + g * rows, rows), rows)
                links[at, :] = totals[g]
            return carry

        lax.fori_loop(0, block // (rows * groups), some, 0)


def links_kernel(firsts, slots, ids_ref, *refs):
    wide = refs[-1]
    for first, links in zip(firsts, refs[:-1]):
        count_links(ids_ref, first, slots, wide, links)


def part_links(part, firsts, slots, points):
    columns = part.shape[1]
    edges = len(firsts) * slots * points * columns
    return pl.pallas_call(
        functools.partial(links_kernel, firsts, slots),
        out_shape=[jax.ShapeDtypeStruct((points, columns), jnp.bfloat16)] * len(firsts),
        scratch_shapes=[pltpu.VMEM((slots, 16, columns), jnp.bfloat16)],
        compiler_params=params(8),
        cost_estimate=pl.CostEstimate(
            flops=100 * edges, bytes_accessed=2 * points * columns, transcendentals=0
        ),
        name="part_links",
    )(part)


def table_stats(x, weight, links, slots, a_ref, b_ref, in_ref, deg_ref, stat_ref):
    points, width = x.shape
    outs = weight.shape[1]
    upper, lower = weight[:width], weight[width:]
    joined = jnp.concatenate([upper - lower, lower], axis=1)
    middle = column_sum(x) / points
    level = jnp.dot(
        jnp.broadcast_to(middle, (8, width)), joined, precision=lax.Precision.HIGHEST
    )
    both = product(x - middle, joined, 1, 0) + level[0:1]
    a, b = both[:, :outs], both[:, outs:]
    mean_a = column_sum(a) / points
    a_off = a - mean_a
    terms = two_terms(a_off)
    seen = degree = 0.0
    for m, part in enumerate(links):
        columns = part.shape[1]
        some = terms[m * columns : (m + 1) * columns]
        seen = seen + jnp.dot(part[...], some, preferred_element_type=jnp.float32)
        degree = degree + jnp.sum(part[...].astype(jnp.float32), axis=1, keepdims=True)
    seen = halves_sum(seen)
    mean_b = column_sum(degree * b) / (points * slots)
    b_off = b - mean_b
    inward = seen + degree * b_off
    a_ref[...] = a
    b_ref[...] = b
    in_ref[...] = inward
    deg_ref[...] = jnp.broadcast_to(degree, deg_ref.shape)
    stat_ref[0:1, :] = mean_a + mean_b
    stat_ref[1:2, :] = slots * column_sum(a_off * a_off) + column_sum((seen + inward) * b_off)


def first_kernel(slots, width, count, *refs):
    parts, early, (weight_ref, x_ref, ids_ref, a_ref, b_ref, in_ref, deg_ref, stat_ref, *late, wide) = (
        refs[:count],
        refs[count : count + count // 2],
        refs[count + count // 2 :],
    )
    rows = parts[0].shape[1]
    fill = jnp.zeros((128 - parts[0].shape[0], rows), jnp.float32)
    for m, part in enumerate(parts):
        ids_ref[:, m * rows : (m + 1) * rows] = part[width:, :]
        x_ref[m * rows : (m + 1) * rows, :] = jnp.concatenate([part[...], fill], axis=0).T
    for part, links in zip(parts[len(early) :], late):
        count_links(part, width, slots, wide, links)
    table_stats(
        x_ref[:, :width], weight_ref[...], (*early, *late), slots, a_ref, b_ref, in_ref, deg_ref, stat_ref
    )


def first_tables(parts, early, weight, slots):
    count, columns = len(parts), parts[0].shape[1]
    points = count * columns
    width, outs = weight.shape[0] // 2, weight.shape[1]
    return pl.pallas_call(
        functools.partial(first_kernel, slots, width, count),
        out_shape=[
            f32(points, 128),
            f32(2 * slots, points),
            f32(points, outs),
            f32(points, outs),
            f32(points, outs),
            f32(points, 128),
            f32(2, outs),
        ],
        scratch_shapes=[pltpu.VMEM((points, columns), jnp.bfloat16)] * (count - len(early))
        + [pltpu.VMEM((slots, 16, columns), jnp.bfloat16)],
        compiler_params=params(24),
        name="first_tables",
    )(*parts, *early, weight)


def second_kernel(slots, x_ref, weight_ref, *refs):
    links, outs = refs[:-5], refs[-5:]
    table_stats(x_ref[...], weight_ref[...], links, slots, *outs)


def second_tables(x, weight, links, slots):
    points, outs = x.shape[0], weight.shape[1]
    return pl.pallas_call(
        functools.partial(second_kernel, slots),
        out_shape=[
            f32(points, outs),
            f32(points, outs),
            f32(points, outs),
            f32(points, 128),
            f32(2, outs),
        ],
        compiler_params=params(24),
        name="second_tables",
    )(x, weight, *links)


def edge_kernel(
    edges, layer, slots, first, tile, away, x_ref, a_ref, b_ref, stat_ref, small_ref, *refs
):
    out_ref, inv_ref, slope_ref, moment_ref, ysum_ref = refs[:5]
    share_refs, (table, centre, held, bounded) = refs[5:-4], refs[-4:]
    points, width = a_ref.shape
    step = pl.program_id(0)
    block = 8

    @pl.when(step == 0)
    def _():
        gain = small_ref[2 * layer : 2 * layer + 1, 0:width]
        shift = small_ref[2 * layer + 1 : 2 * layer + 2, 0:width]
        scale = gain * lax.rsqrt(stat_ref[1:2, :] / edges + norm_eps) * -LOG2E
        middle = column_sum(b_ref[...]) / points
        there = (b_ref[...] - middle) * scale
        here = (a_ref[...] + (middle - stat_ref[0:1, :])) * scale - shift * LOG2E
        table[...] = two_terms(there)
        centre[...] = here
        reach = jnp.max(jnp.abs(here), axis=0, keepdims=True) + jnp.max(
            jnp.abs(there), axis=0, keepdims=True
        )
        bounded[0] = (jnp.max(reach) < 60.0).astype(jnp.int32)

    rows = pl.ds(pl.multiple_of(step * tile, tile), tile)

    def keep(k, start, value):
        if k < away:
            share_refs[0][k, pl.ds(start, block), :] = value
        else:
            at = pl.ds(pl.multiple_of(step * tile + start, block), block)
            share_refs[-1][k - away, at, :] = value

    columns = lax.broadcasted_iota(jnp.int32, (tile, points), 1).astype(jnp.float32)

    def gather(ids):
        pick = jnp.where(ids == columns, 1.0, 0.0).astype(jnp.bfloat16)
        return jnp.dot(pick, table[...], preferred_element_type=jnp.float32)

    def finish(at, top, totals):
        mass, slope, moment, total = totals
        out_ref[at, :] = top + jnp.log(mass)
        inv = 0.8 / mass
        inv_ref[at, :] = inv
        slope_ref[at, :] = slope * inv
        moment_ref[at, :] = moment * inv * (-1.0 / LOG2E)
        ysum_ref[at, :] = total * (-1.0 / LOG2E)

    @pl.when(bounded[0] == 1)
    def _():
        found = [gather(x_ref[rows, first + k : first + k + 1]) for k in range(slots)]
        for start in range(0, tile, block):
            at = slice(start, start + block)
            here = centre[pl.ds(pl.multiple_of(step * tile + start, block), block), :]
            totals = [jnp.zeros((block, width), jnp.float32)] * 4
            for k in range(slots):
                t = here + halves_sum(found[k][at])
                grown = 1.0 + jnp.exp2(t)
                fall = jnp.exp2((-0.2 * LOG2E) * jnp.log(grown) - t)
                share = grown * fall
                part = fall + 0.25 * share
                keep(k, start, part)
                totals = [total + term for total, term in zip(totals, (share, part, part * t, t))]
            finish(at, 0.0, totals)

    @pl.when(bounded[0] == 0)
    def _():
        lanes = lax.broadcasted_iota(jnp.int32, (tile, x_ref.shape[1]), 1)

        def collect(k, carry):
            ids = jnp.sum(jnp.where(lanes == first + k, x_ref[rows, :], 0.0), axis=1, keepdims=True)
            held[k] = centre[rows, :] + halves_sum(gather(ids))
            return carry

        lax.fori_loop(0, slots, collect, 0)

        def rise(t):
            grown = 1.0 + jnp.exp2(jnp.minimum(t, 64.0))
            return jnp.maximum((0.8 * LOG2E) * jnp.log(grown), 0.8 * t) - t, grown

        def some(b, carry):
            at = pl.ds(pl.multiple_of(b * block, block), block)
            low = held[0, at, :]
            for k in range(1, slots):
                low = jnp.minimum(low, held[k, at, :])
            peak, _ = rise(low)
            totals = [jnp.zeros((block, width), jnp.float32)] * 4
            for k in range(slots):
                t = held[k, at, :]
                level, grown = rise(t)
                share = jnp.exp2(level - peak)
                part = share * (1.0 / grown + 0.25)
                keep(k, pl.multiple_of(b * block, block), part)
                totals = [total + term for total, term in zip(totals, (share, part, part * t, t))]
            finish(at, peak * (1.0 / LOG2E), totals)
            return carry

        lax.fori_loop(0, tile // block, some, 0)


def edge_forward(edges, layer, slots, first, tile, away, x, a, b, stat, small):
    points, width = a.shape
    some = pl.BlockSpec((tile, width), lambda step: (step, 0))
    specs, shapes = [some] * 5, [f32(points, width)] * 5
    if away:
        specs.append(pl.BlockSpec((away, tile, width), lambda step: (0, step, 0)))
        shapes.append(in_hbm(away, points, width))
    if away < slots:
        specs.append(VMEM)
        shapes.append(in_vmem(slots - away, points, width))
    results = pl.pallas_call(
        functools.partial(edge_kernel, edges, layer, slots, first, tile, away),
        grid=(points // tile,),
        in_specs=[VMEM] * 5,
        out_specs=specs,
        out_shape=shapes,
        scratch_shapes=[
            pltpu.VMEM((points, 2 * width), jnp.bfloat16),
            pltpu.VMEM((points, width), jnp.float32),
            pltpu.VMEM((slots, tile, width), jnp.float32),
            pltpu.SMEM((1,), jnp.int32),
        ],
        compiler_params=params(20),
        name="edges",
    )(x, a, b, stat, small)
    return *results[:5], results[5:]


def pool_kernel(me_ref, out_ref, inv_ref, slope_ref, moment_ref, gmax_ref, gmean_ref, *refs):
    count = (len(refs) - 3) // 2
    acts, parts = refs[:count], refs[count : 2 * count]
    scaled_ref, own_ref, largest_ref = refs[2 * count :]
    me = me_ref[0]
    points, width = out_ref.shape
    rows = points // count
    out = out_ref[...]
    top = jnp.max(out, axis=0, keepdims=True)
    pool = top + jnp.log(column_sum(jnp.exp(out - top)))
    mean = column_sum(out) / points
    to_max = gmax_ref[pl.ds(me, 1), :]
    to_mean = gmean_ref[pl.ds(me, 1), :] / points
    own_sum = moment_sum = largest = jnp.zeros((1, width), jnp.float32)
    for m in range(count):
        here = slice(m * rows, (m + 1) * rows)
        part = out[here]
        parts[m][0:rows, :] = part
        parts[m][rows : rows + 1, :] = pool
        parts[m][rows + 1 : rows + 2, :] = mean
        parts[m][rows + 4 : rows + 8, :] = jnp.zeros((4, width), jnp.float32)
        grad = acts[m][...] + to_max * jnp.exp(part - pool) + to_mean
        own = grad * slope_ref[here, :]
        scaled_ref[here, :] = grad * inv_ref[here, :]
        own_ref[here, :] = own
        own_sum = own_sum + column_sum(own)
        moment_sum = moment_sum + column_sum(grad * moment_ref[here, :])
        largest = jnp.maximum(largest, jnp.max(jnp.abs(grad), axis=0, keepdims=True))
    largest_ref[...] = largest
    for m in range(count):
        parts[m][rows + 2 : rows + 3, :] = own_sum
        parts[m][rows + 3 : rows + 4, :] = moment_sum


def pools(me, out, inv, slope, moment, grad_max, grad_mean, acts):
    points, width = out.shape
    count = len(acts)
    rows = points // count
    results = pl.pallas_call(
        pool_kernel,
        in_specs=[SMEM] + [VMEM] * (6 + count),
        out_shape=[f32(rows + 8, width)] * count + [f32(points, width)] * 2 + [f32(1, width)],
        compiler_params=params(8),
        name="pools",
    )(me, out, inv, slope, moment, grad_max, grad_mean, *acts)
    return results[:count], *results[count:]


def scatter_kernel(first, start, group, resident, small_rest, ids_ref, grad_ref, largest_ref, weight_ref, sum_ref):
    step = pl.program_id(0)
    points, width = grad_ref.shape
    rows = lax.broadcasted_iota(jnp.int32, (points, points), 0).astype(jnp.float32)
    scale = 2.0**16 / jnp.maximum(largest_ref[...], 1e-30)
    picks, small_picks, terms, rests = [], [], [], []
    for g in range(group):
        here = ids_ref[pl.ds(first + step * group + g, 1), :] == rows
        value = grad_ref[...] * weight_ref[start + step * group + g if resident else g]
        picks.append(jnp.where(here, 1.0, 0.0).astype(jnp.bfloat16))
        if small_rest:
            high = value.astype(jnp.bfloat16)
            terms.append(high)
            small_picks.append(jnp.where(here, SMALL(1), SMALL(0)))
            rests.append(((value - high.astype(jnp.float32)) * scale).astype(SMALL))
        else:
            terms.append(two_terms(value))

    def found(picks, terms):
        return jnp.dot(
            jnp.concatenate(picks, axis=1),
            jnp.concatenate(terms, axis=0),
            preferred_element_type=jnp.float32,
        )

    if small_rest:
        total = found(picks, terms) + found(small_picks, rests) * (1.0 / scale)
    else:
        total = halves_sum(found(picks, terms))

    @pl.when(step == 0)
    def _():
        sum_ref[...] = total

    @pl.when(step > 0)
    def _():
        sum_ref[...] += total


def scatter(ids, first, resident, grad, largest, weight, start, stop, group):
    points, width = grad.shape
    edges = (stop - start) * points
    return pl.pallas_call(
        functools.partial(scatter_kernel, first, start, group, resident, width >= 256),
        grid=((stop - start) // group,),
        in_specs=[
            VMEM,
            VMEM,
            VMEM,
            VMEM
            if resident
            else pl.BlockSpec((group, points, width), lambda step: (start // group + step, 0, 0)),
        ],
        out_specs=VMEM,
        out_shape=f32(points, width),
        compiler_params=params(24),
        cost_estimate=pl.CostEstimate(
            flops=4 * edges * points * width, bytes_accessed=4 * edges * width, transcendentals=0
        ),
        name="scatter",
    )(ids, grad, largest, weight if resident else from_hbm(weight))


def point_grads(edges, slots, own, inward_grads, ysum, inward, degree, local, stat, sums, gain, shift):
    inward_grads = inward_grads + (column_sum(own) - column_sum(inward_grads)) / own.shape[0]
    spread = lax.rsqrt(stat[1:2, :] / edges + norm_eps)
    scale = gain * spread
    own_all = sums[0:1, :]
    gain_all = (sums[1:2, :] - shift * own_all) / gain
    shift_part = own_all / edges
    gain_part = gain_all / edges
    leave = scale * (own - slots * shift_part - gain_part * ((ysum - slots * shift) / gain))
    normed = spread * (inward + degree * (local[0:1, :] - stat[0:1, :]))
    reach = scale * (inward_grads - degree * shift_part - gain_part * normed)
    return leave, reach, gain_all


def turned(weight):
    width = weight.shape[0] // 2
    return jnp.concatenate([weight[:width] - weight[width:], weight[width:]], axis=1)


def weight_grad(x, leave, pair_terms):
    middle = column_sum(x) / x.shape[0]
    level = lax.dot_general(
        jnp.broadcast_to(middle, (8, x.shape[1])) * 0.125,
        jnp.broadcast_to(column_sum(leave), (8, leave.shape[1])),
        (((0,), (0,)), ((), ())),
        precision=lax.Precision.HIGHEST,
        preferred_element_type=jnp.float32,
    )
    both = term_product(terms_of(x - middle), pair_terms, 0, 0)
    outs = leave.shape[1]
    return both[:, :outs] + level, both[:, outs:] - both[:, :outs]


def total_of(refs):
    total = refs[0][...]
    for ref in refs[1:]:
        total = total + ref[...]
    return total


def middle_kernel(
    edges, slots, count, me_ref, own_ref, ysum_ref, in_ref, deg_ref, local_ref, stat_ref, sums_ref,
    small_ref, x_ref, weight_ref, inv_ref, slope_ref, moment_ref, *refs,
):
    wgrad = refs[-1]
    scaled_ref, next_ref, gain_out_ref = refs[-4:-1]
    reached, parts = refs[: -4 - count], refs[-4 - count : -4]
    leave, reach, gain_all = point_grads(
        edges, slots, own_ref[...], total_of(reached), ysum_ref[...], in_ref[...], deg_ref[:, 0:1],
        local_ref[...], stat_ref[...], sums_ref[...], small_ref[2:3, :], small_ref[3:4, :],
    )
    gain_out_ref[...] = gain_all
    width, outs = x_ref.shape[1], leave.shape[1]
    pair_terms = terms_of(jnp.concatenate([leave, reach], axis=1))
    wgrad[0:width, :], wgrad[width:, :] = weight_grad(x_ref[...], leave, pair_terms)
    grad = term_product(pair_terms, terms_of(turned(weight_ref[...])), 1, 1)
    own = grad * slope_ref[...]
    scaled_ref[...] = grad * inv_ref[...]
    next_ref[...] = own
    own_sum = column_sum(own)
    moment_sum = column_sum(grad * moment_ref[...])
    me = me_ref[0]
    piece = 2 * width // count
    for mask, part in enumerate(parts):
        start = pl.multiple_of((me ^ mask) * piece, piece)
        part[0:piece, :] = wgrad[pl.ds(start, piece), :]
        part[piece:, :] = jnp.zeros((8, outs), jnp.float32)
        part[piece : piece + 1, 0:width] = own_sum
        part[piece + 1 : piece + 2, 0:width] = moment_sum


def middle(
    edges, slots, count, me, own, ysum, inward, degree, local, stat, sums, small, x, weight,
    inv, slope, moment, reached,
):
    points, width = x.shape
    outs = weight.shape[1]
    operands = (own, ysum, inward, degree, local, stat, sums, small, x, weight, inv, slope, moment)
    results = pl.pallas_call(
        functools.partial(middle_kernel, edges, slots, count),
        in_specs=[SMEM] + [VMEM] * (len(operands) + len(reached)),
        out_shape=[f32(2 * width // count + 8, outs)] * count
        + [f32(points, width), f32(points, width), f32(1, outs)],
        scratch_shapes=[pltpu.VMEM((2 * width, outs), jnp.float32)],
        compiler_params=params(24),
        name="middle",
    )(me, *operands, *reached)
    return results[:count], *results[count:]


def last_kernel(
    edges, slots, count, own_ref, ysum_ref, in_ref, deg_ref, local_ref, stat_ref, joined_ref,
    small_ref, x_ref, weight_ref, *refs,
):
    reached, (gain_out_ref, wgrad_ref), parts = (
        refs[: -2 - count],
        refs[-2 - count : -count],
        refs[-count:],
    )
    width, outs = weight_ref.shape[0] // 2, weight_ref.shape[1]
    piece = joined_ref.shape[0] - 8
    leave, reach, gain_all = point_grads(
        edges, slots, own_ref[...], total_of(reached), ysum_ref[...], in_ref[...], deg_ref[:, 0:1],
        local_ref[...], stat_ref[...], joined_ref[piece : piece + 2, 0:outs],
        small_ref[0:1, 0:outs], small_ref[1:2, 0:outs],
    )
    gain_out_ref[...] = gain_all
    pair_terms = terms_of(jnp.concatenate([leave, reach], axis=1))
    wgrad_ref[:, :outs], wgrad_ref[:, outs:] = weight_grad(x_ref[:, 0:width], leave, pair_terms)
    grad = term_product(terms_of(turned(weight_ref[...])), pair_terms, 1, 1)
    rows = grad.shape[1] // count
    for m, part in enumerate(parts):
        part[0:width, :] = grad[:, m * rows : (m + 1) * rows]
        part[width:, :] = joined_ref[0:piece, :]


def last(
    edges, slots, count, own, ysum, inward, degree, local, stat, joined, small, x, weight, reached
):
    points = x.shape[0]
    width, outs = weight.shape[0] // 2, weight.shape[1]
    lanes = points // count
    assert lanes == 2 * outs == joined.shape[1]
    results = pl.pallas_call(
        functools.partial(last_kernel, edges, slots, count),
        out_shape=[f32(1, outs), f32(width, 2 * outs)] + [f32(width + joined.shape[0] - 8, lanes)] * count,
        compiler_params=params(16),
        name="last",
    )(own, ysum, inward, degree, local, stat, joined, small, x, weight, *reached)
    return results[0], results[1], results[2:]


def body(
    features,
    neighbours_one,
    neighbours_two,
    weight_one,
    gain_one,
    shift_one,
    weight_two,
    gain_two,
    shift_two,
    grad_act,
    grad_max,
    grad_mean,
):
    clouds, rows, width = features.shape
    slots = neighbours_one.shape[1]
    count = lax.axis_size("pts")
    assert clouds == count
    points = rows * count
    local_edges = points * slots
    edges = float(local_edges * lax.axis_size(BOTH))
    me = lax.axis_index("pts").astype(jnp.int32).reshape(1)
    def to_owner(parts):
        return [parts[0]] + [exchange(part, "pts", m) for m, part in enumerate(parts) if m]

    with jax.named_scope("bring_clouds"):
        parts, small, (weight_one, weight_two) = pack(
            me, features, neighbours_one, neighbours_two,
            (gain_one, shift_one, gain_two, shift_two), (weight_one, weight_two),
        )
        parts = to_owner(parts)
        firsts = (width, width + slots)
        early = [part_links(part, firsts, slots, points) for part in parts[: count // 2]]
    with jax.named_scope("bring_cotangents"):
        acts = to_owner(split(me, grad_act))

    with jax.named_scope("layer_one"):
        x, ids, a_one, b_one, in_one, deg_one, local_one = first_tables(
            parts, [links[0] for links in early], weight_one, slots
        )
        late = [part_links(part, firsts[1:], slots, points) for part in parts[count // 2 :]]
        links = [links[-1] for links in early + late]
        stat_one = join_stats(local_one, local_edges)
        hidden, inv_one, slope_one, moment_one, ysum_one, share_one = edge_forward(
            edges, 0, slots, width, 128, 0, x, a_one, b_one, stat_one, small
        )
    with jax.named_scope("layer_two"):
        a_two, b_two, in_two, deg_two, local_two = second_tables(hidden, weight_two, links, slots)
        stat_two = join_stats(local_two, local_edges)
        out, inv_two, slope_two, moment_two, ysum_two, share_two = edge_forward(
            edges, 1, slots, width + slots, 128, slots - 8, x, a_two, b_two, stat_two, small
        )
    with jax.named_scope("pools"):
        out_parts, scaled_two, own_two, largest_two = pools(
            me, out, inv_two, slope_two, moment_two, grad_max, grad_mean, acts
        )
        out_parts = to_owner(out_parts)
        output, pool_max, pool_mean = unpack_output(me, out_parts)

    def pieces(first, away, scaled, largest, shares, *cuts):
        def piece(start, stop):
            near = start >= away
            offset = away if near else 0

            def run(ready):
                grad = scaled if ready is None else after(scaled, ready)
                return scatter(
                    ids, first + start, near, grad, largest, shares[-1 if near else 0],
                    start - offset, stop - offset, 4,
                )

            return run

        return [piece(*cut) for cut in zip((0, *cuts), (*cuts, slots))]

    with jax.named_scope("layer_two_back"):
        sums_two, reached = sum_beside(
            lambda received: pair_sum([part[rows + 2 : rows + 4] for part in received]),
            out_parts,
            pieces(slots, slots - 8, scaled_two, largest_two, share_two, slots - 8),
        )
        wgrad_parts, scaled_one, own_one, gain_grad_two = middle(
            edges, slots, count, me, own_two, ysum_two, in_two, deg_two, local_two, stat_two, sums_two,
            small, hidden, weight_two, inv_one, slope_one, moment_one, reached,
        )
    with jax.named_scope("layer_one_back"):
        joined, reached = sum_beside(
            lambda received: pair_sum(list(received)),
            to_owner(wgrad_parts),
            pieces(0, 0, scaled_one, scaled_one[:1], share_one, slots - 12, slots - 4),
        )
        gain_grad_one, wgrad_one, grad_parts = last(
            edges, slots, count, own_one, ysum_one, in_one, deg_one, local_one, stat_one, joined,
            small, x, weight_one, reached,
        )
        wgrad_one = pair_sum(to_owner([wgrad_one] * count))
        wgrad_one, *grad_parts = lax.optimization_barrier((wgrad_one, *grad_parts))
        grad_parts = to_owner(grad_parts)
        wgrad_one = sum_stages(wgrad_one, list(stages())[1:])
        wgrad_one = jnp.concatenate(jnp.split(wgrad_one, 2, axis=1), axis=0)
        grad_features, wgrad_two = unpack_grad(me, grad_parts, width)
    return (
        output,
        pool_max,
        pool_mean,
        jnp.swapaxes(grad_features, 1, 2),
        wgrad_one,
        gain_grad_one.reshape(-1),
        joined[-8, : weight_one.shape[1]],
        wgrad_two,
        gain_grad_two.reshape(-1),
        sums_two[0],
    )


def solution(mesh):
    placed = (
        P("clouds", "pts", None),
        P("clouds", None, "pts"),
        P("clouds", None, "pts"),
        P(),
        P(),
        P(),
        P(),
        P(),
        P(),
        P("clouds", "pts", None),
        P("clouds", None),
        P("clouds", None),
    )
    return jax.shard_map(
        body,
        mesh=mesh,
        in_specs=placed,
        out_specs=(
            P("clouds", "pts", None),
            P("clouds", None),
            P("clouds", None),
            P("clouds", "pts", None),
            P(),
            P(),
            P(),
            P(),
            P(),
            P(),
        ),
        check_vma=False,
    )
```

```python
import functools

import jax
import jax.numpy as jnp
from jax import lax
from jax.experimental import pallas as pl
from jax.experimental.pallas import tpu as pltpu
from jax.sharding import PartitionSpec as P

norm_eps = 1e-05
LOG2E = 1.4426950408889634
BOTH = ("clouds", "pts")
MIB = 2**20
SMALL = jnp.float8_e4m3fn


def f32(*shape):
    return jax.ShapeDtypeStruct(shape, jnp.float32)


def in_hbm(*shape):
    return pltpu.HBM(shape, jnp.float32)


def in_vmem(*shape):
    return pltpu.VMEM(shape, jnp.float32)


def from_hbm(x):
    return pltpu.with_memory_space_constraint(x, pltpu.HBM)


def params(mib):
    return pltpu.CompilerParams(vmem_limit_bytes=mib * MIB)


SMEM = pl.BlockSpec(memory_space=pltpu.SMEM)
VMEM = pl.BlockSpec(memory_space=pltpu.VMEM)


def exchange(x, axes, mask):
    size = lax.axis_size(axes)
    return lax.ppermute(x, axes, [(i, i ^ mask) for i in range(size)])


def bit_groups(size):
    bits = [1 << i for i in range(size.bit_length() - 1)]
    groups = [bits[:1]] if bits else []
    rest = bits[1:]
    while rest:
        groups.append(rest[:2])
        rest = rest[2:]
    return groups


def stages():
    yield "pts", list(range(1, lax.axis_size("pts")))
    for bits in bit_groups(lax.axis_size("clouds")):
        masks = [0]
        for bit in bits:
            masks = masks + [mask | bit for mask in masks]
        yield "clouds", masks[1:]


def swap(x, axes, masks):
    return [x] + [exchange(x, axes, mask) for mask in masks]


def pair_sum(values):
    while len(values) > 1:
        values = [values[i] + values[i + 1] for i in range(0, len(values), 2)]
    return values[0]


def sum_stages(x, cloud_stages):
    for axis, masks in cloud_stages:
        x = pair_sum(swap(x, axis, masks))
    return x


def after(value, *others):
    return lax.optimization_barrier((value, *others))[0]


def sum_beside(message, received, work):
    cloud_stages = list(stages())[:0:-1]
    done = [work[0](None)]
    total = message(lax.optimization_barrier((*received, done[0]))[:-1])
    for piece, (axis, masks) in zip(work[1:], cloud_stages):
        moving = swap(total, axis, masks)
        done.append(piece(total))
        total = pair_sum(list(lax.optimization_barrier((*moving, done[-1]))[:-1]))
    return sum_stages(total, cloud_stages[len(work) - 1 :]), done


def join_stats(stat, count):
    for axis, masks in stages():
        parts = swap(stat, axis, masks)
        mean = pair_sum([part[0:1] for part in parts]) / len(parts)
        away = pair_sum([(part[0:1] - mean) ** 2 for part in parts])
        stat = jnp.concatenate([mean, pair_sum([part[1:2] for part in parts]) + count * away], axis=0)
        count = count * len(parts)
    return stat


def pack_kernel(slots, me_ref, *refs):
    sources, outs, fetched, sems = refs[:9], refs[9:-10], refs[-10:-1], refs[-1]
    parts, small_ref, weights = outs[:-3], outs[-3], outs[-2:]
    copies = [
        pltpu.make_async_copy(source, target, sems.at[i])
        for i, (source, target) in enumerate(zip(sources, fetched))
    ]
    for copy in copies:
        copy.start()
    for copy in copies:
        copy.wait()
    feat_ref, one_ref, two_ref = fetched[:3]
    me = me_ref[0]
    width, rows = feat_ref.shape[1], feat_ref.shape[2]
    for mask, out in enumerate(parts):
        cloud = me ^ mask
        out[0:width, :] = feat_ref[cloud]
        for k in range(slots):
            for at, ids in ((width, one_ref), (width + slots, two_ref)):
                row = ids[k, pl.ds(cloud, 1), :] ^ (cloud * rows)
                out[at + k : at + k + 1, :] = row.astype(jnp.float32)
    small_ref[...] = jnp.zeros_like(small_ref)
    for i, vector in enumerate(fetched[3:7]):
        small_ref[i : i + 1, 0 : vector.shape[1]] = vector[...]
    for kept, weight in zip(weights, fetched[7:9]):
        kept[...] = weight[...]


def pack(me, features, neighbours_one, neighbours_two, vectors, weights):
    clouds, rows, width = features.shape
    slots = neighbours_one.shape[1]
    operands = (
        jnp.swapaxes(features, 1, 2),
        jnp.swapaxes(neighbours_one, 0, 1),
        jnp.swapaxes(neighbours_two, 0, 1),
        *(v.reshape(1, -1) for v in vectors),
        *weights,
    )
    results = pl.pallas_call(
        functools.partial(pack_kernel, slots),
        in_specs=[SMEM] + [pl.BlockSpec(memory_space=pltpu.HBM)] * len(operands),
        out_shape=[f32(width + 2 * slots, rows)] * clouds
        + [f32(8, max(v.shape[0] for v in vectors))]
        + [f32(*w.shape) for w in weights],
        scratch_shapes=[pltpu.VMEM(v.shape, v.dtype) for v in operands]
        + [pltpu.SemaphoreType.DMA((len(operands),))],
        compiler_params=params(8),
        name="pack",
    )(me, *(from_hbm(v) for v in operands))
    return results[:clouds], results[clouds], results[clouds + 1 :]


def split_kernel(me_ref, x_ref, *outs):
    me = me_ref[0]
    for mask, out in enumerate(outs):
        out[...] = x_ref[me ^ mask]


def split(me, x):
    clouds, rows, width = x.shape
    return pl.pallas_call(
        split_kernel,
        in_specs=[SMEM, VMEM],
        out_shape=[f32(rows, width)] * clouds,
        compiler_params=params(16),
        name="split",
    )(me, from_hbm(x))


def unpack_output_kernel(rows, me_ref, *refs):
    parts, (act_ref, max_ref, mean_ref) = refs[:-3], refs[-3:]
    me = me_ref[0]
    for mask, part in enumerate(parts):
        cloud = me ^ mask
        act_ref[cloud] = part[0:rows]
        max_ref[pl.ds(cloud, 1), :] = part[rows : rows + 1]
        mean_ref[pl.ds(cloud, 1), :] = part[rows + 1 : rows + 2]


def unpack_output(me, parts):
    clouds, width = len(parts), parts[0].shape[1]
    rows = parts[0].shape[0] - 8
    return pl.pallas_call(
        functools.partial(unpack_output_kernel, rows),
        in_specs=[SMEM] + [VMEM] * clouds,
        out_shape=[f32(clouds, rows, width), f32(clouds, width), f32(clouds, width)],
        compiler_params=params(16),
        name="unpack_output",
    )(me, *parts)


def unpack_grad_kernel(me_ref, *refs):
    parts, (grad_ref, wgrad_ref) = refs[:-2], refs[-2:]
    me = me_ref[0]
    width = grad_ref.shape[1]
    piece = wgrad_ref.shape[0] // len(parts)
    for mask, part in enumerate(parts):
        other = me ^ mask
        grad_ref[other] = part[0:width]
        wgrad_ref[pl.ds(pl.multiple_of(other * piece, piece), piece), :] = part[width:]


def unpack_grad(me, parts, width):
    rows, lanes = parts[0].shape
    count = len(parts)
    return pl.pallas_call(
        unpack_grad_kernel,
        in_specs=[SMEM] + [VMEM] * count,
        out_shape=[f32(count, width, lanes), f32(count * (rows - width), lanes)],
        compiler_params=params(16),
        name="unpack_grad",
    )(me, *parts)


def two_terms(x):
    high = x.astype(jnp.bfloat16)
    low = (x - high.astype(jnp.float32)).astype(jnp.bfloat16)
    return jnp.concatenate([high, low], axis=1)


def halves_sum(x):
    half = x.shape[1] // 2
    return x[:, :half] + x[:, half:]


def terms_of(x):
    high = x.astype(jnp.bfloat16)
    return high, (x - high.astype(jnp.float32)).astype(jnp.bfloat16)


def term_product(x_terms, y_terms, on_x, on_y):
    (x_high, x_low), (y_high, y_low) = x_terms, y_terms
    return lax.dot_general(
        jnp.concatenate([x_high, x_low, x_high], axis=on_x),
        jnp.concatenate([y_high, y_high, y_low], axis=on_y),
        (((on_x,), (on_y,)), ((), ())),
        preferred_element_type=jnp.float32,
    )


def product(x, y, on_x, on_y):
    return term_product(terms_of(x), terms_of(y), on_x, on_y)


def column_sum(x):
    return jnp.sum(x, axis=0, keepdims=True)


def count_links(ids_ref, first, slots, wide, links):
    points, columns = links.shape
    block, rows, groups = 256, 16, 4
    here = lax.broadcasted_iota(jnp.int32, (rows, columns), 0).astype(jnp.bfloat16)
    one = jnp.ones((rows, columns), jnp.bfloat16)
    zero = jnp.zeros((rows, columns), jnp.bfloat16)
    for start in range(0, points, block):
        for k in range(slots):
            local = ids_ref[first + k : first + k + 1, :] - float(start)
            wide[k] = jnp.broadcast_to(local, (rows, columns)).astype(jnp.bfloat16)

        def some(step, carry):
            base = step * (rows * groups)
            names = [here + (base + g * rows).astype(jnp.float32).astype(jnp.bfloat16) for g in range(groups)]
            totals = [zero] * groups
            for k in range(slots):
                ids = wide[k]
                totals = [
                    total + jnp.where(ids == name, one, zero) for total, name in zip(totals, names)
                ]
            for g in range(groups):
                at = pl.ds(pl.multiple_of(start + base + g * rows, rows), rows)
                links[at, :] = totals[g]
            return carry

        lax.fori_loop(0, block // (rows * groups), some, 0)


def links_kernel(firsts, slots, ids_ref, *refs):
    wide = refs[-1]
    for first, links in zip(firsts, refs[:-1]):
        count_links(ids_ref, first, slots, wide, links)


def part_links(part, firsts, slots, points):
    columns = part.shape[1]
    edges = len(firsts) * slots * points * columns
    return pl.pallas_call(
        functools.partial(links_kernel, firsts, slots),
        out_shape=[jax.ShapeDtypeStruct((points, columns), jnp.bfloat16)] * len(firsts),
        scratch_shapes=[pltpu.VMEM((slots, 16, columns), jnp.bfloat16)],
        compiler_params=params(8),
        cost_estimate=pl.CostEstimate(
            flops=100 * edges, bytes_accessed=2 * points * columns, transcendentals=0
        ),
        name="part_links",
    )(part)


def table_stats(x, weight, links, slots, a_ref, b_ref, in_ref, deg_ref, stat_ref):
    points, width = x.shape
    outs = weight.shape[1]
    upper, lower = weight[:width], weight[width:]
    joined = jnp.concatenate([upper - lower, lower], axis=1)
    middle = column_sum(x) / points
    level = jnp.dot(
        jnp.broadcast_to(middle, (8, width)), joined, precision=lax.Precision.HIGHEST
    )
    both = product(x - middle, joined, 1, 0) + level[0:1]
    a, b = both[:, :outs], both[:, outs:]
    mean_a = column_sum(a) / points
    a_off = a - mean_a
    terms = two_terms(a_off)
    seen = degree = 0.0
    for m, part in enumerate(links):
        columns = part.shape[1]
        some = terms[m * columns : (m + 1) * columns]
        seen = seen + jnp.dot(part[...], some, preferred_element_type=jnp.float32)
        degree = degree + jnp.sum(part[...].astype(jnp.float32), axis=1, keepdims=True)
    seen = halves_sum(seen)
    mean_b = column_sum(degree * b) / (points * slots)
    b_off = b - mean_b
    inward = seen + degree * b_off
    a_ref[...] = a
    b_ref[...] = b
    in_ref[...] = inward
    deg_ref[...] = jnp.broadcast_to(degree, deg_ref.shape)
    stat_ref[0:1, :] = mean_a + mean_b
    stat_ref[1:2, :] = slots * column_sum(a_off * a_off) + column_sum((seen + inward) * b_off)


def first_kernel(slots, width, count, *refs):
    parts, early, (weight_ref, x_ref, ids_ref, a_ref, b_ref, in_ref, deg_ref, stat_ref, *late, wide) = (
        refs[:count],
        refs[count : count + count // 2],
        refs[count + count // 2 :],
    )
    rows = parts[0].shape[1]
    fill = jnp.zeros((128 - parts[0].shape[0], rows), jnp.float32)
    for m, part in enumerate(parts):
        ids_ref[:, m * rows : (m + 1) * rows] = part[width:, :]
        x_ref[m * rows : (m + 1) * rows, :] = jnp.concatenate([part[...], fill], axis=0).T
    for part, links in zip(parts[len(early) :], late):
        count_links(part, width, slots, wide, links)
    table_stats(
        x_ref[:, :width], weight_ref[...], (*early, *late), slots, a_ref, b_ref, in_ref, deg_ref, stat_ref
    )


def first_tables(parts, early, weight, slots):
    count, columns = len(parts), parts[0].shape[1]
    points = count * columns
    width, outs = weight.shape[0] // 2, weight.shape[1]
    return pl.pallas_call(
        functools.partial(first_kernel, slots, width, count),
        out_shape=[
            f32(points, 128),
            f32(2 * slots, points),
            f32(points, outs),
            f32(points, outs),
            f32(points, outs),
            f32(points, 128),
            f32(2, outs),
        ],
        scratch_shapes=[pltpu.VMEM((points, columns), jnp.bfloat16)] * (count - len(early))
        + [pltpu.VMEM((slots, 16, columns), jnp.bfloat16)],
        compiler_params=params(24),
        name="first_tables",
    )(*parts, *early, weight)


def second_kernel(slots, x_ref, weight_ref, *refs):
    links, outs = refs[:-5], refs[-5:]
    table_stats(x_ref[...], weight_ref[...], links, slots, *outs)


def second_tables(x, weight, links, slots):
    points, outs = x.shape[0], weight.shape[1]
    return pl.pallas_call(
        functools.partial(second_kernel, slots),
        out_shape=[
            f32(points, outs),
            f32(points, outs),
            f32(points, outs),
            f32(points, 128),
            f32(2, outs),
        ],
        compiler_params=params(24),
        name="second_tables",
    )(x, weight, *links)


def edge_kernel(
    edges, layer, slots, first, tile, away, x_ref, a_ref, b_ref, stat_ref, small_ref, *refs
):
    out_ref, inv_ref, slope_ref, moment_ref, ysum_ref = refs[:5]
    share_refs, (table, centre, held, bounded) = refs[5:-4], refs[-4:]
    points, width = a_ref.shape
    step = pl.program_id(0)
    block = 8

    @pl.when(step == 0)
    def _():
        gain = small_ref[2 * layer : 2 * layer + 1, 0:width]
        shift = small_ref[2 * layer + 1 : 2 * layer + 2, 0:width]
        scale = gain * lax.rsqrt(stat_ref[1:2, :] / edges + norm_eps) * -LOG2E
        middle = column_sum(b_ref[...]) / points
        there = (b_ref[...] - middle) * scale
        here = (a_ref[...] + (middle - stat_ref[0:1, :])) * scale - shift * LOG2E
        table[...] = two_terms(there)
        centre[...] = here
        reach = jnp.max(jnp.abs(here), axis=0, keepdims=True) + jnp.max(
            jnp.abs(there), axis=0, keepdims=True
        )
        bounded[0] = (jnp.max(reach) < 60.0).astype(jnp.int32)

    rows = pl.ds(pl.multiple_of(step * tile, tile), tile)

    def keep(k, start, value):
        if k < away:
            share_refs[0][k, pl.ds(start, block), :] = value
        else:
            at = pl.ds(pl.multiple_of(step * tile + start, block), block)
            share_refs[-1][k - away, at, :] = value

    columns = lax.broadcasted_iota(jnp.int32, (tile, points), 1).astype(jnp.float32)

    def gather(ids):
        pick = jnp.where(ids == columns, 1.0, 0.0).astype(jnp.bfloat16)
        return jnp.dot(pick, table[...], preferred_element_type=jnp.float32)

    def finish(at, top, totals):
        mass, slope, moment, total = totals
        out_ref[at, :] = top + jnp.log(mass)
        inv = 0.8 / mass
        inv_ref[at, :] = inv
        slope_ref[at, :] = slope * inv
        moment_ref[at, :] = moment * inv * (-1.0 / LOG2E)
        ysum_ref[at, :] = total * (-1.0 / LOG2E)

    @pl.when(bounded[0] == 1)
    def _():
        found = [gather(x_ref[rows, first + k : first + k + 1]) for k in range(slots)]
        for start in range(0, tile, block):
            at = slice(start, start + block)
            here = centre[pl.ds(pl.multiple_of(step * tile + start, block), block), :]
            totals = [jnp.zeros((block, width), jnp.float32)] * 4
            for k in range(slots):
                t = here + halves_sum(found[k][at])
                grown = 1.0 + jnp.exp2(t)
                fall = jnp.exp2((-0.2 * LOG2E) * jnp.log(grown) - t)
                share = grown * fall
                part = fall + 0.25 * share
                keep(k, start, part)
                totals = [total + term for total, term in zip(totals, (share, part, part * t, t))]
            finish(at, 0.0, totals)

    @pl.when(bounded[0] == 0)
    def _():
        lanes = lax.broadcasted_iota(jnp.int32, (tile, x_ref.shape[1]), 1)

        def collect(k, carry):
            ids = jnp.sum(jnp.where(lanes == first + k, x_ref[rows, :], 0.0), axis=1, keepdims=True)
            held[k] = centre[rows, :] + halves_sum(gather(ids))
            return carry

        lax.fori_loop(0, slots, collect, 0)

        def rise(t):
            grown = 1.0 + jnp.exp2(jnp.minimum(t, 64.0))
            return jnp.maximum((0.8 * LOG2E) * jnp.log(grown), 0.8 * t) - t, grown

        def some(b, carry):
            at = pl.ds(pl.multiple_of(b * block, block), block)
            low = held[0, at, :]
            for k in range(1, slots):
                low = jnp.minimum(low, held[k, at, :])
            peak, _ = rise(low)
            totals = [jnp.zeros((block, width), jnp.float32)] * 4
            for k in range(slots):
                t = held[k, at, :]
                level, grown = rise(t)
                share = jnp.exp2(level - peak)
                part = share * (1.0 / grown + 0.25)
                keep(k, pl.multiple_of(b * block, block), part)
                totals = [total + term for total, term in zip(totals, (share, part, part * t, t))]
            finish(at, peak * (1.0 / LOG2E), totals)
            return carry

        lax.fori_loop(0, tile // block, some, 0)


def edge_forward(edges, layer, slots, first, tile, away, x, a, b, stat, small):
    points, width = a.shape
    some = pl.BlockSpec((tile, width), lambda step: (step, 0))
    specs, shapes = [some] * 5, [f32(points, width)] * 5
    if away:
        specs.append(pl.BlockSpec((away, tile, width), lambda step: (0, step, 0)))
        shapes.append(in_hbm(away, points, width))
    if away < slots:
        specs.append(VMEM)
        shapes.append(in_vmem(slots - away, points, width))
    results = pl.pallas_call(
        functools.partial(edge_kernel, edges, layer, slots, first, tile, away),
        grid=(points // tile,),
        in_specs=[VMEM] * 5,
        out_specs=specs,
        out_shape=shapes,
        scratch_shapes=[
            pltpu.VMEM((points, 2 * width), jnp.bfloat16),
            pltpu.VMEM((points, width), jnp.float32),
            pltpu.VMEM((slots, tile, width), jnp.float32),
            pltpu.SMEM((1,), jnp.int32),
        ],
        compiler_params=params(20),
        name="edges",
    )(x, a, b, stat, small)
    return *results[:5], results[5:]


def pool_kernel(me_ref, out_ref, inv_ref, slope_ref, moment_ref, gmax_ref, gmean_ref, *refs):
    count = (len(refs) - 3) // 2
    acts, parts = refs[:count], refs[count : 2 * count]
    scaled_ref, own_ref, largest_ref = refs[2 * count :]
    me = me_ref[0]
    points, width = out_ref.shape
    rows = points // count
    out = out_ref[...]
    top = jnp.max(out, axis=0, keepdims=True)
    pool = top + jnp.log(column_sum(jnp.exp(out - top)))
    mean = column_sum(out) / points
    to_max = gmax_ref[pl.ds(me, 1), :]
    to_mean = gmean_ref[pl.ds(me, 1), :] / points
    own_sum = moment_sum = largest = jnp.zeros((1, width), jnp.float32)
    for m in range(count):
        here = slice(m * rows, (m + 1) * rows)
        part = out[here]
        parts[m][0:rows, :] = part
        parts[m][rows : rows + 1, :] = pool
        parts[m][rows + 1 : rows + 2, :] = mean
        parts[m][rows + 4 : rows + 8, :] = jnp.zeros((4, width), jnp.float32)
        grad = acts[m][...] + to_max * jnp.exp(part - pool) + to_mean
        own = grad * slope_ref[here, :]
        scaled_ref[here, :] = grad * inv_ref[here, :]
        own_ref[here, :] = own
        own_sum = own_sum + column_sum(own)
        moment_sum = moment_sum + column_sum(grad * moment_ref[here, :])
        largest = jnp.maximum(largest, jnp.max(jnp.abs(grad), axis=0, keepdims=True))
    largest_ref[...] = largest
    for m in range(count):
        parts[m][rows + 2 : rows + 3, :] = own_sum
        parts[m][rows + 3 : rows + 4, :] = moment_sum


def pools(me, out, inv, slope, moment, grad_max, grad_mean, acts):
    points, width = out.shape
    count = len(acts)
    rows = points // count
    results = pl.pallas_call(
        pool_kernel,
        in_specs=[SMEM] + [VMEM] * (6 + count),
        out_shape=[f32(rows + 8, width)] * count + [f32(points, width)] * 2 + [f32(1, width)],
        compiler_params=params(8),
        name="pools",
    )(me, out, inv, slope, moment, grad_max, grad_mean, *acts)
    return results[:count], *results[count:]


def scatter_kernel(first, start, group, resident, small_rest, ids_ref, grad_ref, largest_ref, weight_ref, sum_ref):
    step = pl.program_id(0)
    points, width = grad_ref.shape
    rows = lax.broadcasted_iota(jnp.int32, (points, points), 0).astype(jnp.float32)
    scale = 2.0**16 / jnp.maximum(largest_ref[...], 1e-30)
    picks, small_picks, terms, rests = [], [], [], []
    for g in range(group):
        here = ids_ref[pl.ds(first + step * group + g, 1), :] == rows
        value = grad_ref[...] * weight_ref[start + step * group + g if resident else g]
        picks.append(jnp.where(here, 1.0, 0.0).astype(jnp.bfloat16))
        if small_rest:
            high = value.astype(jnp.bfloat16)
            terms.append(high)
            small_picks.append(jnp.where(here, SMALL(1), SMALL(0)))
            rests.append(((value - high.astype(jnp.float32)) * scale).astype(SMALL))
        else:
            terms.append(two_terms(value))

    def found(picks, terms):
        return jnp.dot(
            jnp.concatenate(picks, axis=1),
            jnp.concatenate(terms, axis=0),
            preferred_element_type=jnp.float32,
        )

    if small_rest:
        total = found(picks, terms) + found(small_picks, rests) * (1.0 / scale)
    else:
        total = halves_sum(found(picks, terms))

    @pl.when(step == 0)
    def _():
        sum_ref[...] = total

    @pl.when(step > 0)
    def _():
        sum_ref[...] += total


def scatter(ids, first, resident, grad, largest, weight, start, stop, group):
    points, width = grad.shape
    edges = (stop - start) * points
    return pl.pallas_call(
        functools.partial(scatter_kernel, first, start, group, resident, width >= 256),
        grid=((stop - start) // group,),
        in_specs=[
            VMEM,
            VMEM,
            VMEM,
            VMEM
            if resident
            else pl.BlockSpec((group, points, width), lambda step: (start // group + step, 0, 0)),
        ],
        out_specs=VMEM,
        out_shape=f32(points, width),
        compiler_params=params(20),
        cost_estimate=pl.CostEstimate(
            flops=4 * edges * points * width, bytes_accessed=4 * edges * width, transcendentals=0
        ),
        name="scatter",
    )(ids, grad, largest, weight if resident else from_hbm(weight))


def point_grads(edges, slots, own, inward_grads, ysum, inward, degree, local, stat, sums, gain, shift):
    inward_grads = inward_grads + (column_sum(own) - column_sum(inward_grads)) / own.shape[0]
    spread = lax.rsqrt(stat[1:2, :] / edges + norm_eps)
    scale = gain * spread
    own_all = sums[0:1, :]
    gain_all = (sums[1:2, :] - shift * own_all) / gain
    shift_part = own_all / edges
    gain_part = gain_all / edges
    leave = scale * (own - slots * shift_part - gain_part * ((ysum - slots * shift) / gain))
    normed = spread * (inward + degree * (local[0:1, :] - stat[0:1, :]))
    reach = scale * (inward_grads - degree * shift_part - gain_part * normed)
    return leave, reach, gain_all


def turned(weight):
    width = weight.shape[0] // 2
    return jnp.concatenate([weight[:width] - weight[width:], weight[width:]], axis=1)


def weight_grad(x, leave, pair_terms):
    middle = column_sum(x) / x.shape[0]
    level = lax.dot_general(
        jnp.broadcast_to(middle, (8, x.shape[1])) * 0.125,
        jnp.broadcast_to(column_sum(leave), (8, leave.shape[1])),
        (((0,), (0,)), ((), ())),
        precision=lax.Precision.HIGHEST,
        preferred_element_type=jnp.float32,
    )
    both = term_product(terms_of(x - middle), pair_terms, 0, 0)
    outs = leave.shape[1]
    return both[:, :outs] + level, both[:, outs:] - both[:, :outs]


def total_of(refs):
    total = refs[0][...]
    for ref in refs[1:]:
        total = total + ref[...]
    return total


def middle_kernel(
    edges, slots, count, me_ref, own_ref, ysum_ref, in_ref, deg_ref, local_ref, stat_ref, sums_ref,
    small_ref, x_ref, weight_ref, inv_ref, slope_ref, moment_ref, *refs,
):
    wgrad = refs[-1]
    scaled_ref, next_ref, gain_out_ref = refs[-4:-1]
    reached, parts = refs[: -4 - count], refs[-4 - count : -4]
    leave, reach, gain_all = point_grads(
        edges, slots, own_ref[...], total_of(reached), ysum_ref[...], in_ref[...], deg_ref[:, 0:1],
        local_ref[...], stat_ref[...], sums_ref[...], small_ref[2:3, :], small_ref[3:4, :],
    )
    gain_out_ref[...] = gain_all
    width, outs = x_ref.shape[1], leave.shape[1]
    pair_terms = terms_of(jnp.concatenate([leave, reach], axis=1))
    wgrad[0:width, :], wgrad[width:, :] = weight_grad(x_ref[...], leave, pair_terms)
    grad = term_product(pair_terms, terms_of(turned(weight_ref[...])), 1, 1)
    own = grad * slope_ref[...]
    scaled_ref[...] = grad * inv_ref[...]
    next_ref[...] = own
    own_sum = column_sum(own)
    moment_sum = column_sum(grad * moment_ref[...])
    me = me_ref[0]
    piece = 2 * width // count
    for mask, part in enumerate(parts):
        start = pl.multiple_of((me ^ mask) * piece, piece)
        part[0:piece, :] = wgrad[pl.ds(start, piece), :]
        part[piece:, :] = jnp.zeros((8, outs), jnp.float32)
        part[piece : piece + 1, 0:width] = own_sum
        part[piece + 1 : piece + 2, 0:width] = moment_sum


def middle(
    edges, slots, count, me, own, ysum, inward, degree, local, stat, sums, small, x, weight,
    inv, slope, moment, reached,
):
    points, width = x.shape
    outs = weight.shape[1]
    operands = (own, ysum, inward, degree, local, stat, sums, small, x, weight, inv, slope, moment)
    results = pl.pallas_call(
        functools.partial(middle_kernel, edges, slots, count),
        in_specs=[SMEM] + [VMEM] * (len(operands) + len(reached)),
        out_shape=[f32(2 * width // count + 8, outs)] * count
        + [f32(points, width), f32(points, width), f32(1, outs)],
        scratch_shapes=[pltpu.VMEM((2 * width, outs), jnp.float32)],
        compiler_params=params(24),
        name="middle",
    )(me, *operands, *reached)
    return results[:count], *results[count:]


def last_kernel(
    edges, slots, count, own_ref, ysum_ref, in_ref, deg_ref, local_ref, stat_ref, joined_ref,
    small_ref, x_ref, weight_ref, *refs,
):
    reached, (gain_out_ref, wgrad_ref), parts = (
        refs[: -2 - count],
        refs[-2 - count : -count],
        refs[-count:],
    )
    width, outs = weight_ref.shape[0] // 2, weight_ref.shape[1]
    piece = joined_ref.shape[0] - 8
    leave, reach, gain_all = point_grads(
        edges, slots, own_ref[...], total_of(reached), ysum_ref[...], in_ref[...], deg_ref[:, 0:1],
        local_ref[...], stat_ref[...], joined_ref[piece : piece + 2, 0:outs],
        small_ref[0:1, 0:outs], small_ref[1:2, 0:outs],
    )
    gain_out_ref[...] = gain_all
    pair_terms = terms_of(jnp.concatenate([leave, reach], axis=1))
    wgrad_ref[:, :outs], wgrad_ref[:, outs:] = weight_grad(x_ref[:, 0:width], leave, pair_terms)
    grad = term_product(terms_of(turned(weight_ref[...])), pair_terms, 1, 1)
    rows = grad.shape[1] // count
    for m, part in enumerate(parts):
        part[0:width, :] = grad[:, m * rows : (m + 1) * rows]
        part[width:, :] = joined_ref[0:piece, :]


def last(
    edges, slots, count, own, ysum, inward, degree, local, stat, joined, small, x, weight, reached
):
    points = x.shape[0]
    width, outs = weight.shape[0] // 2, weight.shape[1]
    lanes = points // count
    assert lanes == 2 * outs == joined.shape[1]
    results = pl.pallas_call(
        functools.partial(last_kernel, edges, slots, count),
        out_shape=[f32(1, outs), f32(width, 2 * outs)] + [f32(width + joined.shape[0] - 8, lanes)] * count,
        compiler_params=params(16),
        name="last",
    )(own, ysum, inward, degree, local, stat, joined, small, x, weight, *reached)
    return results[0], results[1], results[2:]


def body(
    features,
    neighbours_one,
    neighbours_two,
    weight_one,
    gain_one,
    shift_one,
    weight_two,
    gain_two,
    shift_two,
    grad_act,
    grad_max,
    grad_mean,
):
    clouds, rows, width = features.shape
    slots = neighbours_one.shape[1]
    count = lax.axis_size("pts")
    assert clouds == count
    points = rows * count
    local_edges = points * slots
    edges = float(local_edges * lax.axis_size(BOTH))
    me = lax.axis_index("pts").astype(jnp.int32).reshape(1)
    def to_owner(parts):
        return [parts[0]] + [exchange(part, "pts", m) for m, part in enumerate(parts) if m]

    with jax.named_scope("bring_clouds"):
        parts, small, (weight_one, weight_two) = pack(
            me, features, neighbours_one, neighbours_two,
            (gain_one, shift_one, gain_two, shift_two), (weight_one, weight_two),
        )
        parts = to_owner(parts)
        firsts = (width, width + slots)
        early = [part_links(part, firsts, slots, points) for part in parts[: count // 2]]
    with jax.named_scope("bring_cotangents"):
        acts = to_owner(split(me, grad_act))

    with jax.named_scope("layer_one"):
        x, ids, a_one, b_one, in_one, deg_one, local_one = first_tables(
            parts, [links[0] for links in early], weight_one, slots
        )
        late = [part_links(part, firsts[1:], slots, points) for part in parts[count // 2 :]]
        links = [links[-1] for links in early + late]
        stat_one = join_stats(local_one, local_edges)
        hidden, inv_one, slope_one, moment_one, ysum_one, share_one = edge_forward(
            edges, 0, slots, width, 128, 0, x, a_one, b_one, stat_one, small
        )
    with jax.named_scope("layer_two"):
        a_two, b_two, in_two, deg_two, local_two = second_tables(hidden, weight_two, links, slots)
        stat_two = join_stats(local_two, local_edges)
        out, inv_two, slope_two, moment_two, ysum_two, share_two = edge_forward(
            edges, 1, slots, width + slots, 128, slots - 8, x, a_two, b_two, stat_two, small
        )
    with jax.named_scope("pools"):
        out_parts, scaled_two, own_two, largest_two = pools(
            me, out, inv_two, slope_two, moment_two, grad_max, grad_mean, acts
        )
        out_parts = to_owner(out_parts)
        output, pool_max, pool_mean = unpack_output(me, out_parts)

    def pieces(first, away, scaled, largest, shares, *cuts):
        def piece(start, stop):
            near = start >= away
            offset = away if near else 0

            def run(ready):
                grad = scaled if ready is None else after(scaled, ready)
                return scatter(
                    ids, first + start, near, grad, largest, shares[-1 if near else 0],
                    start - offset, stop - offset, 4,
                )

            return run

        return [piece(*cut) for cut in zip((0, *cuts), (*cuts, slots))]

    with jax.named_scope("layer_two_back"):
        sums_two, reached = sum_beside(
            lambda received: pair_sum([part[rows + 2 : rows + 4] for part in received]),
            out_parts,
            pieces(slots, slots - 8, scaled_two, largest_two, share_two, slots - 8, slots - 4),
        )
        wgrad_parts, scaled_one, own_one, gain_grad_two = middle(
            edges, slots, count, me, own_two, ysum_two, in_two, deg_two, local_two, stat_two, sums_two,
            small, hidden, weight_two, inv_one, slope_one, moment_one, reached,
        )
    with jax.named_scope("layer_one_back"):
        joined, reached = sum_beside(
            lambda received: pair_sum(list(received)),
            to_owner(wgrad_parts),
            pieces(0, 0, scaled_one, scaled_one[:1], share_one, slots - 12, slots - 4),
        )
        gain_grad_one, wgrad_one, grad_parts = last(
            edges, slots, count, own_one, ysum_one, in_one, deg_one, local_one, stat_one, joined,
            small, x, weight_one, reached,
        )
        wgrad_one = pair_sum(to_owner([wgrad_one] * count))
        wgrad_one, *grad_parts = lax.optimization_barrier((wgrad_one, *grad_parts))
        grad_parts = to_owner(grad_parts)
        wgrad_one = sum_stages(wgrad_one, list(stages())[1:])
        wgrad_one = jnp.concatenate(jnp.split(wgrad_one, 2, axis=1), axis=0)
        grad_features, wgrad_two = unpack_grad(me, grad_parts, width)
    return (
        output,
        pool_max,
        pool_mean,
        jnp.swapaxes(grad_features, 1, 2),
        wgrad_one,
        gain_grad_one.reshape(-1),
        joined[-8, : weight_one.shape[1]],
        wgrad_two,
        gain_grad_two.reshape(-1),
        sums_two[0],
    )


def solution(mesh):
    placed = (
        P("clouds", "pts", None),
        P("clouds", None, "pts"),
        P("clouds", None, "pts"),
        P(),
        P(),
        P(),
        P(),
        P(),
        P(),
        P("clouds", "pts", None),
        P("clouds", None),
        P("clouds", None),
    )
    return jax.shard_map(
        body,
        mesh=mesh,
        in_specs=placed,
        out_specs=(
            P("clouds", "pts", None),
            P("clouds", None),
            P("clouds", None),
            P("clouds", "pts", None),
            P(),
            P(),
            P(),
            P(),
            P(),
            P(),
        ),
        check_vma=False,
    )
```
